128 devices in a mesh: slab: 32 (over y, x_lo, z), chan: 4 (over x_hi, core).
Axes of the slice: x: 4 (x_hi: 2, x_lo: 2; x = x_hi * 2 + x_lo), y: 4, z: 4, core: 2. Of those that a mesh axis runs over, the one named last changes fastest.
Arguments:
- features: bfloat16 [4, 128, 128, 512], P(None, 'slab', 'chan'), may hold values from -6 to 6
- neighbours: int32 [128, 27], P('slab'), may hold values from -1 to 7, as said below
- face_lists: int32 [32, 2, 2], P('slab'), may hold values from -1 to 3, as said below
- weight_first: bfloat16 [27, 128, 128], P(None, None, 'chan'), may hold values from -0.109375 to 0.109375
- bias_first: float32 [128], P('chan'), may hold values from -3 to 3
- weight_second: bfloat16 [27, 128, 128], P(None, None, 'chan'), may hold values from -0.109375 to 0.109375
- bias_second: float32 [128], P('chan'), may hold values from -3 to 3
- level_embed: float32 [4, 128], P(None, 'chan'), may hold values from -3 to 3
Outputs:
- denoised: bfloat16 [4, 128, 128, 512], P(None, 'slab', 'chan')
The draws below stay inside these ranges and needn't reach their ends.
Inputs may be any that keep to these rules, and one draw needn't show every extreme that they name: `neighbours`: slab s holds in its used slots, in some order, the active bricks of its two brick layers at positions of a 8 x 8 grid; each layer has at most 2 active bricks. Rows of unused slots are all -1; a used slot names itself at offset 13. Offsets with dz = -1 from the bottom layer name the slab below (never for slab 0), dz = +1 from the top layer the slab above (never for the last slab). `face_lists`: entry [s, 0, c] is the slot of the active bottom-layer brick at position c, entry [s, 1, c] that of the top-layer brick; -1 where the position has no active brick. The slots of a slab's used bricks each appear once.
All inputs are finite; a program needn't handle non-finite values.
Results may differ from the reference program's by a relative error of at most 0.02.
Values may be sent and summed in bfloat16 or wider, within the bound.
No kernel may reach another device: no remote copies, remote signals or barrier semaphores. Data moves between devices by JAX's collectives and lax.ppermute only.
A program may use at most 128 MiB of HBM per device.

```python
import jax
import jax.numpy as jnp
from jax import lax

C = 128
LEVELS = 4
EDGE = 8
GRID = 8
NB_DEV = 4
FACE = 2
SLABS = 32
BRICKS = 128
N_CHAN = 4


def layout(key):
    base = jax.random.fold_in(key, 31)
    k_spot, k_count, k_pick, k_rank = jax.random.split(base, 4)
    cells = GRID * GRID
    spots = jax.random.permutation(k_spot, cells)[:FACE].astype(jnp.int32)
    counts = jax.random.randint(k_count, (SLABS, 2), 1, FACE + 1).astype(jnp.int32)
    fullest = jax.random.randint(k_pick, (), 0, SLABS - 1)
    slab = jnp.arange(SLABS, dtype=jnp.int32)
    counts = jnp.where(((slab == fullest) | (slab == fullest + 1))[:, None], FACE, counts)
    counts = jnp.where((slab == (fullest + 2) % SLABS)[:, None], 1, counts)
    column = jnp.arange(FACE, dtype=jnp.int32)
    valid = column[None, None, :] < counts[:, :, None]
    entry = jnp.arange(NB_DEV, dtype=jnp.int32)
    ranks = jax.vmap(lambda k: jax.random.permutation(k, NB_DEV))(jax.random.split(k_rank, SLABS)).astype(jnp.int32)
    sort_key = jnp.where(valid.reshape(SLABS, NB_DEV), ranks, NB_DEV + entry[None, :])
    order = jnp.argsort(sort_key, axis=1, stable=True).astype(jnp.int32)
    slot_of = jnp.argsort(order, axis=1, stable=True).astype(jnp.int32)
    cell_ids = jnp.arange(cells, dtype=jnp.int32)
    match = spots[:, None] == cell_ids[None, :]
    holder = jnp.where(valid, slot_of.reshape(SLABS, 2, FACE) + 1, 0)
    slot_at = jnp.sum(holder[:, :, :, None] * match[None, None].astype(jnp.int32), axis=2) - 1
    col_of = jnp.sum(jnp.where(match, column[:, None] + 1, 0), axis=0) - 1
    prev_top = jnp.where(slab > 0, jnp.roll(counts[:, 1], 1), 0)
    next_bottom = jnp.where(slab < SLABS - 1, jnp.roll(counts[:, 0], -1), 0)
    row_pos = spots // GRID
    col_pos = spots % GRID
    tiers = jnp.arange(2, dtype=jnp.int32)
    results = []
    for dz in (-1, 0, 1):
        for dy in (-1, 0, 1):
            for dx in (-1, 0, 1):
                near_y = row_pos + dy
                near_x = col_pos + dx
                inside = (near_y >= 0) & (near_y < GRID) & (near_x >= 0) & (near_x < GRID)
                cell = jnp.clip(near_y, 0, GRID - 1) * GRID + jnp.clip(near_x, 0, GRID - 1)
                other = col_of[cell][None, None, :]
                level_z = tiers[:, None] + dz
                same = slot_at[:, jnp.clip(level_z, 0, 1), cell[None, :]]
                lower = jnp.where((other >= 0) & (other < prev_top[:, None, None]), NB_DEV + other, -1)
                upper = jnp.where((other >= 0) & (other < next_bottom[:, None, None]), NB_DEV + FACE + other, -1)
                value = jnp.where(level_z[None] < 0, lower, jnp.where(level_z[None] > 1, upper, same))
                value = jnp.where(inside[None, None, :], value, -1)
                results.append(value)
    table = jnp.stack(results, axis=-1)
    table = jnp.where(valid[..., None], table, -1).reshape(SLABS, NB_DEV, 27)
    table = jnp.take_along_axis(table, order[:, :, None], axis=1)
    lists = jnp.where(valid, slot_of.reshape(SLABS, 2, FACE), -1)
    return (table.reshape(SLABS * NB_DEV, 27).astype(jnp.int32), lists.astype(jnp.int32))


def draw_neighbours(key, part):
    return layout(key)[0]


def draw_face_lists(key, part):
    return layout(key)[1]


def block_scale(own_key, shape, cuts, least, top_value):
    factor_of, own = 1.0, jax.random.fold_in(own_key, 6)
    for position, shards_of in cuts:
        draws = jnp.exp(jax.random.uniform(jax.random.fold_in(own, position), (shards_of,), jnp.float32, least / len(cuts), top_value / len(cuts)))
        factor_of = factor_of * jnp.repeat(draws, shape[position] // shards_of).reshape([-1 if axis == position else 1 for axis in range(len(shape))])
    return factor_of


def noise(stream_key, dims, deviation, limit, shards=(), kind=jnp.bfloat16):
    values = jax.random.normal(stream_key, dims, jnp.float32) * deviation
    if len(shards) > 0:
        values = block_scale(stream_key, dims, shards, -0.22, 0.18) * values
    return jnp.clip(values, min=-limit, max=limit).astype(kind)


def setup_inputs(seed: int = 0) -> dict:
    arg_keys = jax.random.split(jax.random.key(seed), 9)
    features = noise(arg_keys[0], (LEVELS, BRICKS, C, EDGE * EDGE * EDGE), 1.0, 6.0, ((1, 32), (2, 4)))
    neighbours = draw_neighbours(jax.random.fold_in(arg_keys[8], 71), 0)
    face_lists = draw_face_lists(jax.random.fold_in(arg_keys[8], 71), 0)
    weight_first = noise(arg_keys[3], (27, C, C), (27 * C) ** -0.5, 0.109375, ((2, 4),))
    bias_first = noise(arg_keys[4], (C,), 0.5, 3.0, ((0, 4),), jnp.float32)
    weight_second = noise(arg_keys[5], (27, C, C), (27 * C) ** -0.5, 0.109375, ((2, 4),))
    bias_second = noise(arg_keys[6], (C,), 0.5, 3.0, ((0, 4),), jnp.float32)
    level_embed = noise(arg_keys[7], (LEVELS, C), 0.5, 3.0, ((1, 4),), jnp.float32)
    return dict(features=features, neighbours=neighbours, face_lists=face_lists, weight_first=weight_first, bias_first=bias_first, weight_second=weight_second, bias_second=bias_second, level_embed=level_embed)


def span(step):
    if step < 0:
        return 7, 8
    if step == 0:
        return 0, 8
    return 0, 1


def assemble(full_pool, low_pool, high_pool, full_index, low_index, high_index):
    layers = []
    for dz in (-1, 0, 1):
        rows = []
        for dy in (-1, 0, 1):
            pieces = []
            for dx in (-1, 0, 1):
                k = 9 * (dz + 1) + 3 * (dy + 1) + (dx + 1)
                y_lo, y_hi = span(dy)
                x_lo, x_hi = span(dx)
                if dz == 0:
                    source = full_pool[:, :, :, :, y_lo:y_hi, x_lo:x_hi]
                    index = full_index[:, k]
                elif dz < 0:
                    source = low_pool[:, :, :, None, y_lo:y_hi, x_lo:x_hi]
                    index = low_index[:, k]
                else:
                    source = high_pool[:, :, :, None, y_lo:y_hi, x_lo:x_hi]
                    index = high_index[:, k]
                pieces.append(jnp.take(source, index, axis=1))
            rows.append(jnp.concatenate(pieces, axis=5))
        layers.append(jnp.concatenate(rows, axis=4))
    return jnp.concatenate(layers, axis=3)


def global_table(neighbours, face_lists):
    table = neighbours.reshape(SLABS, NB_DEV, 27)
    slab = jnp.arange(SLABS, dtype=jnp.int32)[:, None, None]
    below = jnp.clip(slab - 1, 0, SLABS - 1)
    above = jnp.clip(slab + 1, 0, SLABS - 1)
    col_low = jnp.clip(table - NB_DEV, 0, FACE - 1)
    col_high = jnp.clip(table - NB_DEV - FACE, 0, FACE - 1)
    from_low = below * NB_DEV + face_lists[below, 1, col_low]
    from_high = above * NB_DEV + face_lists[above, 0, col_high]
    local = slab * NB_DEV + table
    glob = jnp.where(table < 0, BRICKS, jnp.where(table < NB_DEV, local, jnp.where(table < NB_DEV + FACE, from_low, from_high)))
    return glob.astype(jnp.int32)


def convolve(padded, weight):
    levels, count, group = padded.shape[0], padded.shape[1], padded.shape[2]
    acc = jnp.zeros((levels, count, weight.shape[1], 512), jnp.float32)
    for dz in (-1, 0, 1):
        for dy in (-1, 0, 1):
            for dx in (-1, 0, 1):
                k = 9 * (dz + 1) + 3 * (dy + 1) + (dx + 1)
                window = padded[:, :, :, 1 + dz:9 + dz, 1 + dy:9 + dy, 1 + dx:9 + dx].reshape(levels, count, group, 512)
                acc = acc + jnp.einsum('oc,lbcv->lbov', weight[k].astype(jnp.float32), window.astype(jnp.float32))
    return acc


def conv_layer(features, glob, mask, weight, bias, shift):
    pool = features.reshape(LEVELS, BRICKS, C, 8, 8, 8)
    pool = jnp.concatenate([pool, jnp.zeros((LEVELS, 1, C, 8, 8, 8), features.dtype)], axis=1)
    low = pool[:, :, :, 7]
    high = pool[:, :, :, 0]
    group = C // N_CHAN

    def one_slab(index):
        padded = assemble(pool, low, high, index, index, index)
        total = jnp.zeros((LEVELS, NB_DEV, C, 512), jnp.float32)
        for g in range(N_CHAN):
            part = convolve(padded[:, :, g * group:(g + 1) * group], weight[:, :, g * group:(g + 1) * group])
            rounded = lax.optimization_barrier(part.astype(jnp.bfloat16))
            total = total + rounded.astype(jnp.float32)
        return total

    totals = lax.map(one_slab, glob)
    totals = totals.transpose(1, 0, 2, 3, 4).reshape(LEVELS, BRICKS, C, 512)
    act = jax.nn.silu(totals + bias[None, None, :, None] + shift[:, None, :, None]) * mask[None, :, None, None]
    return act.astype(jnp.bfloat16)


def reference(features, neighbours, face_lists, weight_first, bias_first, weight_second, bias_second, level_embed):
    glob = global_table(neighbours, face_lists)
    mask = (neighbours[:, 13] >= 0).astype(jnp.float32)
    hidden = conv_layer(features, glob, mask, weight_first, bias_first, level_embed)
    no_shift = jnp.zeros((LEVELS, C), jnp.float32)
    return conv_layer(hidden, glob, mask, weight_second, bias_second, no_shift)
```

```python
import jax
import jax.numpy as jnp
from jax import lax
from jax.experimental import pallas as pl
from jax.experimental.pallas import tpu as pltpu
from jax.sharding import PartitionSpec as P

BF16, F32 = jnp.bfloat16, jnp.float32
NONE = 8
HBM = pl.BlockSpec(memory_space=pl.ANY)
VMEM = pl.BlockSpec(memory_space=pltpu.VMEM)
SMEM = pl.BlockSpec(memory_space=pltpu.SMEM)
SPAN = {-1: (7, 0, 1), 0: (0, 1, 8), 1: (0, 9, 1)}


def offset(dz, dy, dx):
    return 9 * (dz + 1) + 3 * (dy + 1) + (dx + 1)


def split_kernel(feat, lists, *refs):
    outs, sem = refs[:11], refs[11]
    pieces, up, down = outs[:3], outs[3:7], outs[7:11]
    me = lax.axis_index("chan")
    copies = []
    for m in range(4):
        level = me ^ m
        for c in range(2):
            top = jnp.maximum(lists[0, 1, c], 0)
            low = jnp.maximum(lists[0, 0, c], 0)
            copies.append((feat.at[level, top, :, pl.ds(384, 128)], up[m].at[c]))
            copies.append((feat.at[level, low, :, pl.ds(0, 128)], down[m].at[c]))
        if m:
            copies.append((feat.at[level], pieces[m - 1]))
    started = []
    for i, (source, target) in enumerate(copies):
        copy = pltpu.make_async_copy(source, target, sem.at[i])
        copy.start()
        started.append(copy)
    for copy in started:
        copy.wait()


def split(features, face_lists):
    piece = jax.ShapeDtypeStruct((4, 32, 512), BF16)
    side = jax.ShapeDtypeStruct((2, 32, 128), BF16)
    return pl.pallas_call(
        split_kernel,
        out_shape=[piece] * 3 + [side] * 8,
        in_specs=[HBM, SMEM],
        out_specs=[HBM] * 11,
        scratch_shapes=[pltpu.SemaphoreType.DMA((19,))],
        name="split_features",
    )(features, face_lists)


def weights_kernel(w1, w2, b1, b2, lev, out1, out2):
    me = lax.axis_index("chan")
    rows = lax.broadcasted_iota(jnp.int32, (32, 32), 0)
    eye = (rows == lax.broadcasted_iota(jnp.int32, (32, 32), 1)).astype(BF16)
    for w, out in ((w1, out1), (w2, out2)):
        for k in range(27):
            turned = lax.dot_general(eye, w[k], (((1,), (1,)), ((), ())), preferred_element_type=F32)
            out[pl.ds(32 * k, 32), :] = turned.astype(BF16)
    values = jnp.concatenate([b1[...], b2[...], lev[...], jnp.zeros((2, 32), F32)], axis=0)
    values = jnp.concatenate([values] * 4, axis=1)
    lane = lax.broadcasted_iota(jnp.int32, (8, 128), 1)
    values = jnp.where(lane // 32 == me, values, 0.0)
    high = values.astype(BF16).astype(F32)
    out1[pl.ds(864, 16), :] = jnp.concatenate([high, values - high], axis=0).astype(BF16)
    out1[pl.ds(880, 16), :] = jnp.zeros((16, 128), BF16)


def turn_weights(w1, w2, b1, b2, lev):
    return pl.pallas_call(
        weights_kernel,
        out_shape=[jax.ShapeDtypeStruct((896, 128), BF16), jax.ShapeDtypeStruct((864, 128), BF16)],
        in_specs=[VMEM] * 5,
        out_specs=[VMEM] * 2,
        compiler_params=pltpu.CompilerParams(vmem_limit_bytes=24 << 20),
        name="turn_weights",
    )(w1, w2, b1.reshape(1, 32), b2.reshape(1, 32), lev)


def silu(v):
    return v / (1.0 + jnp.exp(-v))


def gather_padded(slots, pad, lead, slot, planes):
    x = lax.broadcasted_iota(jnp.int32, (1, 8, 128), 1)
    for dz, z_from, z_to in planes:
        for dy in (-1, 0, 1):
            y_from, y_to, n = SPAN[dy]
            parts = ([], [], [])
            for w in range(2):
                mid, left, right = (
                    slots[slot(w, offset(dz, dy, dx)), z_from, y_from : y_from + n] for dx in (0, -1, 1)
                )
                parts[0].append(pltpu.roll(jnp.where(x == 7, left, mid), 1, 1))
                parts[1].append(mid)
                parts[2].append(pltpu.roll(jnp.where(x == 0, right, mid), 7, 1))
            for d in range(3):
                tile = jnp.concatenate(parts[d], axis=1).astype(BF16)
                pad[lead, z_to, y_to : y_to + n, :, 128 * d : 128 * d + 128] = tile


OWN_PLANES = [(-1, 7, 0)] + [(0, z, z + 1) for z in range(8)] + [(1, 0, 9)]


def conv_pair(pad, lead, w):
    zero = jnp.zeros((128, 128), BF16)
    total = None
    blocks = [(zin, dy) for zin in range(4) for dy in range(3)]
    for first in range(0, 12, 2):
        left, right = [], []
        for zin, dy in blocks[first : first + 2]:
            planes = [pad[lead, zin + 2 * j, dy : dy + 8].reshape(128, 384) for j in range(4)]
            left.append(jnp.concatenate(planes, axis=0))
            for dx in range(3):
                even = w[9 * zin + 3 * dy + dx] if zin < 3 else zero
                odd = w[9 * (zin - 1) + 3 * dy + dx] if zin > 0 else zero
                right.append(jnp.concatenate([even, odd], axis=1))
        part = jnp.dot(
            jnp.concatenate(left, axis=1), jnp.concatenate(right, axis=0), preferred_element_type=F32
        )
        total = part if total is None else total + part
    return total


def conv_face(pad, w):
    total = None
    blocks = [(dz, dy) for dz in range(3) for dy in range(3)]
    for group in (blocks[0:2], blocks[2:4], blocks[4:6], blocks[6:9]):
        left, right = [], []
        for dz, dy in group:
            sides = [pad[side, dz, dy : dy + 8].reshape(128, 384) for side in range(2)]
            left.append(jnp.concatenate(sides, axis=0))
            right += [w[9 * dz + 3 * dy + dx] for dx in range(3)]
        part = jnp.dot(
            jnp.concatenate(left, axis=1), jnp.concatenate(right, axis=0), preferred_element_type=F32
        )
        total = part if total is None else total + part
    return total


def conv_kernel(tab, fl, tab_b, fl_b, tab_a, fl_a, *refs):
    feat, side_b, side_a = refs[0:4], refs[4:8], refs[8:12]
    w1_in, w2_in = refs[12:16], refs[16:20]
    outs = refs[20:24]
    fs, hs, w1, w2, bias, slots, pad, pad_face, acc, shift, turned, sem = refs[24:]
    me = lax.axis_index("chan")

    f_copies, w1_copies, w2_copies = [], [], []
    for m in range(4):
        f_copies.append(pltpu.make_async_copy(feat[m], fs.at[m], sem.at[m]))
        f_copies.append(pltpu.make_async_copy(side_b[m], hs.at[0, m], sem.at[4 + m]))
        f_copies.append(pltpu.make_async_copy(side_a[m], hs.at[1, m], sem.at[8 + m]))
        g = pl.multiple_of((me ^ m) * 32, 32)
        w1_copies.append(
            pltpu.make_async_copy(
                w1_in[m].at[pl.ds(0, 27)], w1.at[:, pl.ds(32 * m, 32), :], sem.at[12 + m]
            )
        )
        w1_copies.append(
            pltpu.make_async_copy(w1_in[m].at[27, pl.ds(0, 16)], bias.at[m], sem.at[16 + m])
        )
        w2_copies.append(pltpu.make_async_copy(w2_in[m], w2.at[:, pl.ds(g, 32), :], sem.at[20 + m]))
    for copy in f_copies + w1_copies + w2_copies:
        copy.start()
    for copy in f_copies:
        copy.wait()

    slots[NONE] = jnp.zeros((8, 8, 8, 128), F32)
    for b in range(4):
        brick = jnp.concatenate([fs[m, b] for m in range(4)], axis=0)
        slots[b] = brick.T.astype(F32).reshape(8, 8, 8, 128)
    for side in range(2):
        for c in range(2):
            face = jnp.concatenate([hs[side, m, c] for m in range(4)], axis=0)
            first = 6 if side == 0 else 0
            slots[4 + 2 * side + c, first : first + 2] = face.T.astype(F32).reshape(2, 8, 8, 128)

    def own(pair):
        def slot(w, k):
            t = tab[2 * pair + w, k]
            return jnp.where(t < 0, NONE, t)

        return slot

    def below(c, k):
        t = tab_b[jnp.maximum(fl_b[0, 1, c], 0), k]
        if k < 18:
            found = jnp.where(t == fl_b[0, 1, 0], 4, jnp.where(t == fl_b[0, 1, 1], 5, NONE))
            return jnp.where(t < 0, NONE, found)
        u = fl[0, 0, jnp.clip(t - 6, 0, 1)]
        return jnp.where((t < 6) | (u < 0), NONE, u)

    def above(c, k):
        t = tab_a[jnp.maximum(fl_a[0, 0, c], 0), k]
        if k >= 9:
            found = jnp.where(t == fl_a[0, 0, 0], 6, jnp.where(t == fl_a[0, 0, 1], 7, NONE))
            return jnp.where(t < 0, NONE, found)
        u = fl[0, 1, jnp.clip(t - 4, 0, 1)]
        return jnp.where((t < 4) | (t > 5) | (u < 0), NONE, u)

    gather_padded(slots, pad_face, 0, below, [(0, 6, 0), (0, 7, 1), (1, 0, 2)])
    gather_padded(slots, pad_face, 1, above, [(-1, 7, 0), (0, 0, 1), (0, 1, 2)])
    for pair in range(2):
        gather_padded(slots, pad, pair, own(pair), OWN_PLANES)

    for copy in w1_copies:
        copy.wait()
    values = sum(bias[m].astype(F32) for m in range(4))
    shift[...] = values[0:8] + values[8:16]
    shift_second = shift[1:2, :]
    shift_first = shift[0:1, :] + shift[pl.ds(2 + me, 1), :]

    def finish(pair, moved):
        for j in range(4):
            for zo in range(2):
                tile = silu(acc[128 * j : 128 * j + 128, 128 * zo : 128 * zo + 128] + moved)
                tile = tile.reshape(8, 2, 8, 128)
                for w in range(2):
                    b = 2 * pair + w
                    slots[b, 2 * j + zo] = jnp.where(tab[b, 13] >= 0, tile[:, w], 0.0)

    for pair in range(2):
        acc[...] = conv_pair(pad, pair, w1)
        finish(pair, shift_first)
    faces = silu(conv_face(pad_face, w1) + shift_first).reshape(2, 8, 2, 8, 128)
    for c in range(2):
        slots[4 + c, 7] = faces[0, :, c]
        slots[6 + c, 0] = faces[1, :, c]

    for pair in range(2):
        gather_padded(slots, pad, pair, own(pair), OWN_PLANES)
    for copy in w2_copies:
        copy.wait()
    for pair in range(2):
        acc[...] = conv_pair(pad, pair, w2)
        finish(pair, shift_second)
    for b in range(4):
        brick = slots[b].reshape(512, 128).astype(BF16).T
        for g in range(4):
            turned[g, b] = brick[32 * g : 32 * g + 32]
    out_copies = [
        pltpu.make_async_copy(turned.at[me ^ m], outs[m], sem.at[24 + m]) for m in range(4)
    ]
    for copy in out_copies:
        copy.start()
    for copy in out_copies:
        copy.wait()


def convolve(tables, feat, side_b, side_a, w1, w2):
    piece = jax.ShapeDtypeStruct((4, 32, 512), BF16)
    return pl.pallas_call(
        conv_kernel,
        out_shape=[piece] * 4,
        in_specs=[SMEM] * 6 + [HBM] * 20,
        out_specs=[HBM] * 4,
        scratch_shapes=[
            pltpu.VMEM((4, 4, 32, 512), BF16),
            pltpu.VMEM((2, 4, 2, 32, 128), BF16),
            pltpu.VMEM((27, 128, 128), BF16),
            pltpu.VMEM((27, 128, 128), BF16),
            pltpu.VMEM((4, 16, 128), BF16),
            pltpu.VMEM((9, 8, 8, 8, 128), F32),
            pltpu.VMEM((2, 10, 10, 16, 384), BF16),
            pltpu.VMEM((2, 3, 10, 16, 384), BF16),
            pltpu.VMEM((512, 256), F32),
            pltpu.VMEM((8, 128), F32),
            pltpu.VMEM((4, 4, 32, 512), BF16),
            pltpu.SemaphoreType.DMA((28,)),
        ],
        compiler_params=pltpu.CompilerParams(vmem_limit_bytes=40 << 20),
        cost_estimate=pl.CostEstimate(flops=8 * 10**9, bytes_accessed=4 * 10**6, transcendentals=10**6),
        name="convolve",
    )(*tables, *feat, *side_b, *side_a, *w1, *w2)


def join_kernel(*refs):
    pieces, out, sem = refs[:4], refs[4], refs[5]
    me = lax.axis_index("chan")
    copies = [pltpu.make_async_copy(pieces[m], out.at[me ^ m], sem.at[m]) for m in range(4)]
    for copy in copies:
        copy.start()
    for copy in copies:
        copy.wait()


def join(pieces):
    return pl.pallas_call(
        join_kernel,
        out_shape=jax.ShapeDtypeStruct((4, 4, 32, 512), BF16),
        in_specs=[HBM] * 4,
        out_specs=HBM,
        scratch_shapes=[pltpu.SemaphoreType.DMA((4,))],
        name="join_levels",
    )(*pieces)


def swap(value, m):
    return lax.ppermute(value, "chan", [(i, i ^ m) for i in range(4)])


def to_slab(value, steps, m):
    slabs = lax.axis_size("slab")
    pairs = [
        (4 * s + g, 4 * (s + steps) + (g ^ m))
        for s in range(slabs)
        if 0 <= s + steps < slabs
        for g in range(4)
    ]
    return lax.ppermute(value, ("slab", "chan"), pairs)


def shards(features, neighbours, face_lists, w_first, b_first, w_second, b_second, level_embed):
    parts = split(features, face_lists)
    pieces, up, down = parts[:3], parts[3:7], parts[7:11]
    w1, w2 = turn_weights(w_first, w_second, b_first, b_second, level_embed)
    w1, w2 = w1.reshape(28, 32, 128), w2.reshape(27, 32, 128)

    side_b = [to_slab(up[m], 1, m) for m in range(4)]
    side_a = [to_slab(down[m], -1, m) for m in range(4)]
    tables = [neighbours, face_lists]
    tables += [to_slab(neighbours, 1, 0), to_slab(face_lists, 1, 0)]
    tables += [to_slab(neighbours, -1, 0), to_slab(face_lists, -1, 0)]

    me = lax.axis_index("chan")
    mine = lax.dynamic_index_in_dim(features, me, 0, keepdims=False)
    feat = [mine, swap(pieces[0], 1), swap(pieces[1], 2), swap(pieces[2], 3)]

    def all_shards(w):
        near, far = swap(w, 1), swap(w, 2)
        return [w, near, far, swap(far, 1)]

    outs = convolve(tables, feat, side_b, side_a, all_shards(w1), all_shards(w2))
    return join([outs[0]] + [swap(outs[m], m) for m in (1, 2, 3)])


def solution(mesh):
    placed = (
        P(None, "slab", "chan", None),
        P("slab", None),
        P("slab", None, None),
        P(None, None, "chan"),
        P("chan"),
        P(None, None, "chan"),
        P("chan"),
        P(None, "chan"),
    )
    return jax.shard_map(
        shards, mesh=mesh, in_specs=placed, out_specs=P(None, "slab", "chan", None), check_vma=False
    )
```

```python
import jax
import jax.numpy as jnp
from jax import lax
from jax.experimental import pallas as pl
from jax.experimental.pallas import tpu as pltpu
from jax.sharding import PartitionSpec as P

BF16, F32 = jnp.bfloat16, jnp.float32
NONE = 8
HBM = pl.BlockSpec(memory_space=pl.ANY)
VMEM = pl.BlockSpec(memory_space=pltpu.VMEM)
SMEM = pl.BlockSpec(memory_space=pltpu.SMEM)
SPAN = {-1: (7, 0, 1), 0: (0, 1, 8), 1: (0, 9, 1)}


def offset(dz, dy, dx):
    return 9 * (dz + 1) + 3 * (dy + 1) + (dx + 1)


def split_kernel(feat, near, lists_block, lists, *refs):
    pieces, sides = refs[:3], refs[3:5]
    me = lax.axis_index("chan")
    for m in range(1, 4):
        pieces[m - 1][...] = feat[me ^ m]
    for tier, lanes, out in ((1, 384, sides[0]), (0, 0, sides[1])):
        for c in range(2):
            b = jnp.maximum(lists[0, tier, c], 0)
            for level in range(4):
                out[pl.ds(64 * level + 32 * c, 32), :] = feat[level, b, :, lanes : lanes + 128]
        out[pl.ds(256, 16), :] = jnp.zeros((16, 128), BF16)
        out[pl.ds(256, 4), pl.ds(0, 27)] = near[...].astype(F32).astype(BF16)
        out[pl.ds(264, 2), pl.ds(0, 2)] = lists_block[0].astype(F32).astype(BF16)


def split(features, neighbours, face_lists):
    piece = jax.ShapeDtypeStruct((4, 32, 512), BF16)
    side = jax.ShapeDtypeStruct((272, 128), BF16)
    return pl.pallas_call(
        split_kernel,
        out_shape=[piece] * 3 + [side] * 2,
        in_specs=[VMEM, VMEM, VMEM, SMEM],
        out_specs=[VMEM] * 5,
        name="split_features",
    )(features, neighbours, face_lists, face_lists)


def sides_kernel(from_below, from_above, *refs):
    pieces, tables = refs[:4], refs[4]
    me = lax.axis_index("chan")
    for side, source in enumerate((from_below, from_above)):
        for m in range(4):
            rows = pl.ds(pl.multiple_of(64 * (me ^ m), 64), 64)
            pieces[m][pl.ds(64 * side, 64), :] = source[rows, :]
        tables[pl.ds(16 * side, 16), :] = source[pl.ds(256, 16), :].astype(F32).astype(jnp.int32)


def sort_sides(from_below, from_above):
    side = jax.ShapeDtypeStruct((128, 128), BF16)
    return pl.pallas_call(
        sides_kernel,
        out_shape=[side] * 4 + [jax.ShapeDtypeStruct((32, 128), jnp.int32)],
        in_specs=[VMEM] * 2,
        out_specs=[VMEM] * 5,
        name="sort_sides",
    )(from_below, from_above)


def weights_kernel(w1, w2, b1, b2, lev, both, cross):
    me = lax.axis_index("chan")
    odd = lax.axis_index("slab") % 2
    rows = lax.broadcasted_iota(jnp.int32, (32, 32), 0)
    eye = (rows == lax.broadcasted_iota(jnp.int32, (32, 32), 1)).astype(BF16)
    for i, w in enumerate((w1, w2)):
        for k in range(27):
            turned = lax.dot_general(eye, w[k], (((1,), (1,)), ((), ())), preferred_element_type=F32)
            both[i, k] = turned.astype(BF16)
    values = jnp.concatenate([b1[...], b2[...], lev[...], jnp.zeros((2, 32), F32)], axis=0)
    values = jnp.concatenate([values] * 4, axis=1)
    lane = lax.broadcasted_iota(jnp.int32, (8, 128), 1)
    values = jnp.where(lane // 32 == me, values, 0.0)
    high = values.astype(BF16).astype(F32)
    both[0, 27] = jnp.concatenate([high, values - high, jnp.zeros((16, 128), F32)], axis=0).astype(BF16)
    both[1, 27] = jnp.zeros((32, 128), BF16)
    cross[...] = both[odd]


def turn_weights(w1, w2, b1, b2, lev):
    shard = (28, 32, 128)
    return pl.pallas_call(
        weights_kernel,
        out_shape=[jax.ShapeDtypeStruct((2, *shard), BF16), jax.ShapeDtypeStruct(shard, BF16)],
        in_specs=[VMEM] * 5,
        out_specs=[VMEM] * 2,
        compiler_params=pltpu.CompilerParams(vmem_limit_bytes=24 << 20),
        name="turn_weights",
    )(w1, w2, b1.reshape(1, 32), b2.reshape(1, 32), lev)


def silu(v):
    return v / (1.0 + jnp.exp(-v))


def gather_padded(slots, pad, lead, slot, planes):
    x = lax.broadcasted_iota(jnp.int32, (1, 8, 128), 1)
    for dz, z_from, z_to in planes:
        for dy in (-1, 0, 1):
            y_from, y_to, n = SPAN[dy]
            parts = ([], [], [])
            for w in range(2):
                mid, left, right = (
                    slots[slot(w, offset(dz, dy, dx)), z_from, y_from : y_from + n] for dx in (0, -1, 1)
                )
                parts[0].append(pltpu.roll(jnp.where(x == 7, left, mid), 1, 1))
                parts[1].append(mid)
                parts[2].append(pltpu.roll(jnp.where(x == 0, right, mid), 7, 1))
            for d in range(3):
                tile = jnp.concatenate(parts[d], axis=1).astype(BF16)
                pad[lead, z_to, y_to : y_to + n, :, 128 * d : 128 * d + 128] = tile


OWN_PLANES = [(-1, 7, 0)] + [(0, z, z + 1) for z in range(8)] + [(1, 0, 9)]


def conv_pair(pad, lead, w):
    zero = jnp.zeros((128, 128), BF16)
    total = None
    blocks = [(zin, dy) for zin in range(4) for dy in range(3)]
    for first in range(0, 12, 2):
        left, right = [], []
        for zin, dy in blocks[first : first + 2]:
            planes = [pad[lead, zin + 2 * j, dy : dy + 8].reshape(128, 384) for j in range(4)]
            left.append(jnp.concatenate(planes, axis=0))
            for dx in range(3):
                even = w[9 * zin + 3 * dy + dx] if zin < 3 else zero
                odd = w[9 * (zin - 1) + 3 * dy + dx] if zin > 0 else zero
                right.append(jnp.concatenate([even, odd], axis=1))
        part = jnp.dot(
            jnp.concatenate(left, axis=1), jnp.concatenate(right, axis=0), preferred_element_type=F32
        )
        total = part if total is None else total + part
    return total


def conv_face(pad, w):
    total = None
    blocks = [(dz, dy) for dz in range(3) for dy in range(3)]
    for group in (blocks[0:2], blocks[2:4], blocks[4:6], blocks[6:9]):
        left, right = [], []
        for dz, dy in group:
            sides = [pad[side, dz, dy : dy + 8].reshape(128, 384) for side in range(2)]
            left.append(jnp.concatenate(sides, axis=0))
            right += [w[9 * dz + 3 * dy + dx] for dx in range(3)]
        part = jnp.dot(
            jnp.concatenate(left, axis=1), jnp.concatenate(right, axis=0), preferred_element_type=F32
        )
        total = part if total is None else total + part
    return total


def conv_kernel(tab, fl, features, *refs):
    feat, sides, tables_in = refs[0:3], refs[3:7], refs[7]
    own_w, near_w, far_w = refs[8], refs[9], refs[10:14]
    outs = refs[14:18]
    fs, hs, w1, w2, bias, tables, slots, pad, pad_face, acc, shift, turned, sem = refs[18:]
    me = lax.axis_index("chan")
    odd = lax.axis_index("slab") % 2

    f_copies = [pltpu.make_async_copy(tables_in, tables, sem.at[0])]
    for m in range(4):
        source = feat[m - 1] if m else features.at[me]
        f_copies.append(pltpu.make_async_copy(source, fs.at[m], sem.at[4 + m]))
        f_copies.append(pltpu.make_async_copy(sides[m], hs.at[m], sem.at[8 + m]))
    for copy in f_copies:
        copy.start()

    def load_shard(m, layer, source, at):
        weights = (w1, w2)[layer]
        g = 32 * m if layer == 0 else pl.multiple_of((me ^ m) * 32, 32)
        found = [pltpu.make_async_copy(source.at[pl.ds(0, 27)], weights.at[:, pl.ds(g, 32), :], sem.at[at])]
        if layer == 0:
            found.append(
                pltpu.make_async_copy(source.at[27, pl.ds(0, 16)], bias.at[m], sem.at[at + 1])
            )
        return found

    w_copies = ([], [])
    for layer in range(2):
        w_copies[layer].extend(load_shard(0, layer, own_w.at[layer], 12 + 2 * layer))
        w_copies[layer].extend(load_shard(1, layer, near_w.at[layer], 16 + 2 * layer))
    for layer in range(2):
        for copy in w_copies[layer]:
            copy.start()
    for layer in range(2):
        for m in (2, 3):
            at = 20 + 4 * (m - 2) + 2 * layer
            mine, other = far_w[m - 2], far_w[m]

            @pl.when(odd == layer)
            def _():
                for copy in load_shard(m, layer, mine, at):
                    copy.start()

            @pl.when(odd != layer)
            def _():
                for copy in load_shard(m, layer, other, at):
                    copy.start()

            w_copies[layer].extend(load_shard(m, layer, mine, at))
    w1_copies, w2_copies = w_copies
    for copy in f_copies:
        copy.wait()

    slots[NONE] = jnp.zeros((8, 8, 8, 128), F32)
    for b in range(4):
        brick = jnp.concatenate([fs[m, b] for m in range(4)], axis=0)
        slots[b] = brick.T.astype(F32).reshape(8, 8, 8, 128)
    for side in range(2):
        for c in range(2):
            face = jnp.concatenate([hs[m, pl.ds(64 * side + 32 * c, 32)] for m in range(4)], axis=0)
            first = 6 if side == 0 else 0
            slots[4 + 2 * side + c, first : first + 2] = face.T.astype(F32).reshape(2, 8, 8, 128)

    def own(pair):
        def slot(w, k):
            t = tab[2 * pair + w, k]
            return jnp.where(t < 0, NONE, t)

        return slot

    def below(c, k):
        t = tables[0 + jnp.maximum(tables[9, c], 0), k]
        if k < 18:
            found = jnp.where(t == tables[9, 0], 4, jnp.where(t == tables[9, 1], 5, NONE))
            return jnp.where(t < 0, NONE, found)
        u = fl[0, 0, jnp.clip(t - 6, 0, 1)]
        return jnp.where((t < 6) | (u < 0), NONE, u)

    def above(c, k):
        t = tables[16 + jnp.maximum(tables[24, c], 0), k]
        if k >= 9:
            found = jnp.where(t == tables[24, 0], 6, jnp.where(t == tables[24, 1], 7, NONE))
            return jnp.where(t < 0, NONE, found)
        u = fl[0, 1, jnp.clip(t - 4, 0, 1)]
        return jnp.where((t < 4) | (t > 5) | (u < 0), NONE, u)

    gather_padded(slots, pad_face, 0, below, [(0, 6, 0), (0, 7, 1), (1, 0, 2)])
    gather_padded(slots, pad_face, 1, above, [(-1, 7, 0), (0, 0, 1), (0, 1, 2)])
    for pair in range(2):
        gather_padded(slots, pad, pair, own(pair), OWN_PLANES)

    for copy in w1_copies:
        copy.wait()
    values = sum(bias[m].astype(F32) for m in range(4))
    shift[...] = values[0:8] + values[8:16]
    shift_second = shift[1:2, :]
    shift_first = shift[0:1, :] + shift[pl.ds(2 + me, 1), :]

    def finish(pair, moved):
        for j in range(4):
            for zo in range(2):
                tile = silu(acc[128 * j : 128 * j + 128, 128 * zo : 128 * zo + 128] + moved)
                tile = tile.reshape(8, 2, 8, 128)
                for w in range(2):
                    b = 2 * pair + w
                    slots[b, 2 * j + zo] = jnp.where(tab[b, 13] >= 0, tile[:, w], 0.0)

    for pair in range(2):
        acc[...] = conv_pair(pad, pair, w1)
        finish(pair, shift_first)
    faces = silu(conv_face(pad_face, w1) + shift_first).reshape(2, 8, 2, 8, 128)
    for c in range(2):
        slots[4 + c, 7] = faces[0, :, c]
        slots[6 + c, 0] = faces[1, :, c]

    for pair in range(2):
        gather_padded(slots, pad, pair, own(pair), OWN_PLANES)
    for copy in w2_copies:
        copy.wait()
    for pair in range(2):
        acc[...] = conv_pair(pad, pair, w2)
        finish(pair, shift_second)
    for b in range(4):
        brick = slots[b].reshape(512, 128).astype(BF16).T
        for g in range(4):
            turned[g, b] = brick[32 * g : 32 * g + 32]
    out_copies = [
        pltpu.make_async_copy(turned.at[me ^ m], outs[m], sem.at[28 + m]) for m in range(4)
    ]
    for copy in out_copies:
        copy.start()
    for copy in out_copies:
        copy.wait()


def convolve(neighbours, face_lists, features, feat, sides, tables, own_w, near_w, far_w):
    piece = jax.ShapeDtypeStruct((4, 32, 512), BF16)
    return pl.pallas_call(
        conv_kernel,
        out_shape=[piece] * 4,
        in_specs=[SMEM] * 2 + [HBM] * 15,
        out_specs=[HBM] * 4,
        scratch_shapes=[
            pltpu.VMEM((4, 4, 32, 512), BF16),
            pltpu.VMEM((4, 128, 128), BF16),
            pltpu.VMEM((27, 128, 128), BF16),
            pltpu.VMEM((27, 128, 128), BF16),
            pltpu.VMEM((4, 16, 128), BF16),
            pltpu.SMEM((32, 128), jnp.int32),
            pltpu.VMEM((9, 8, 8, 8, 128), F32),
            pltpu.VMEM((2, 10, 10, 16, 384), BF16),
            pltpu.VMEM((2, 3, 10, 16, 384), BF16),
            pltpu.VMEM((512, 256), F32),
            pltpu.VMEM((8, 128), F32),
            pltpu.VMEM((4, 4, 32, 512), BF16),
            pltpu.SemaphoreType.DMA((32,)),
        ],
        compiler_params=pltpu.CompilerParams(vmem_limit_bytes=40 << 20),
        cost_estimate=pl.CostEstimate(flops=8 * 10**9, bytes_accessed=4 * 10**6, transcendentals=10**6),
        name="convolve",
    )(neighbours, face_lists, features, *feat, *sides, tables, own_w, near_w, *far_w)


def join_kernel(*refs):
    pieces, out = refs[:4], refs[4]
    me = lax.axis_index("chan")
    for m in range(4):
        out[me ^ m] = pieces[m][...]


def join(pieces):
    return pl.pallas_call(
        join_kernel,
        out_shape=jax.ShapeDtypeStruct((4, 4, 32, 512), BF16),
        in_specs=[VMEM] * 4,
        out_specs=VMEM,
        name="join_levels",
    )(*pieces)


def swap(value, m):
    return lax.ppermute(value, "chan", [(i, i ^ m) for i in range(4)])


def swap_slabs(value, m):
    count = lax.axis_size("slab")
    pairs = [(4 * s + g, 4 * (s ^ 1) + (g ^ m)) for s in range(count) for g in range(4)]
    return lax.ppermute(value, ("slab", "chan"), pairs)


def to_slab(value, steps):
    count = lax.axis_size("slab")
    return lax.ppermute(value, "slab", [(s, (s + steps) % count) for s in range(count)])


def shards(features, neighbours, face_lists, w_first, b_first, w_second, b_second, level_embed):
    *pieces, up, down = split(features, neighbours, face_lists)
    from_below, from_above = to_slab(up, 1), to_slab(down, -1)
    both, cross = turn_weights(w_first, w_second, b_first, b_second, level_embed)
    fetched = swap(cross, 2)
    feat = [swap(pieces[m - 1], m) for m in (1, 2, 3)]
    near = swap(both, 1)
    far = [fetched, swap(fetched, 1), swap_slabs(fetched, 0), swap_slabs(fetched, 1)]
    *sides, tables = sort_sides(from_below, from_above)
    sides = [sides[0]] + [swap(sides[m], m) for m in (1, 2, 3)]
    outs = convolve(neighbours, face_lists, features, feat, sides, tables, both, near, far)
    return join([outs[0]] + [swap(outs[m], m) for m in (1, 2, 3)])


def solution(mesh):
    placed = (
        P(None, "slab", "chan", None),
        P("slab", None),
        P("slab", None, None),
        P(None, None, "chan"),
        P("chan"),
        P(None, None, "chan"),
        P("chan"),
        P(None, "chan"),
    )
    return jax.shard_map(
        shards, mesh=mesh, in_specs=placed, out_specs=P(None, "slab", "chan", None), check_vma=False
    )
```

```python
import jax
import jax.numpy as jnp
from jax import lax
from jax.experimental import pallas as pl
from jax.experimental.pallas import tpu as pltpu
from jax.sharding import PartitionSpec as P

BF16, F32 = jnp.bfloat16, jnp.float32
NONE = 8
HBM = pl.BlockSpec(memory_space=pl.ANY)
VMEM = pl.BlockSpec(memory_space=pltpu.VMEM)
SMEM = pl.BlockSpec(memory_space=pltpu.SMEM)
SPAN = {-1: (7, 0, 1), 0: (0, 1, 8), 1: (0, 9, 1)}


def offset(dz, dy, dx):
    return 9 * (dz + 1) + 3 * (dy + 1) + (dx + 1)


PIECE = 17


def split_kernel(feat, w1, w2, b1, b2, lev, *refs):
    pieces, cross, held, sem = refs[:4], refs[4], refs[5], refs[6]
    me = lax.axis_index("chan")
    odd = lax.axis_index("slab") % 2

    @pl.when(odd == 0)
    def _():
        pltpu.make_async_copy(w1, cross, sem.at[0]).start()

    @pl.when(odd == 1)
    def _():
        pltpu.make_async_copy(w2, cross, sem.at[0]).start()

    small = [
        pltpu.make_async_copy(b1, held.at[pl.ds(0, 1)], sem.at[1]),
        pltpu.make_async_copy(b2, held.at[pl.ds(1, 1)], sem.at[2]),
        pltpu.make_async_copy(lev, held.at[pl.ds(2, 4)], sem.at[3]),
    ]
    large = [
        pltpu.make_async_copy(w, pieces[1].at[pl.ds(PIECE + 27 * layer, 27)], sem.at[4 + layer])
        for layer, w in enumerate((w1, w2))
    ]
    for m in range(4):
        for v in range(4):
            run = feat.at[me ^ m, :, :, pl.ds(128 * v, 128)]
            large.append(
                pltpu.make_async_copy(run, pieces[m].at[pl.ds(4 * v, 4)], sem.at[6 + 4 * m + v])
            )
    held[pl.ds(6, 2), :] = jnp.zeros((2, 32), F32)
    for copy in small + large:
        copy.start()
    for copy in small:
        copy.wait()

    values = jnp.concatenate([held[...]] * 4, axis=1)
    lane = lax.broadcasted_iota(jnp.int32, (8, 128), 1)
    values = jnp.where(lane // 32 == me, values, 0.0)
    high = values.astype(BF16).astype(F32)
    values = jnp.concatenate([high, values - high, jnp.zeros((16, 128), F32)], axis=0).astype(BF16)
    for m in range(4):
        pieces[m][16] = values
    pltpu.make_async_copy(w1, cross, sem.at[0]).wait()
    for copy in large:
        copy.wait()


def split(features, w1, w2, b1, b2, lev):
    piece = jax.ShapeDtypeStruct((PIECE, 32, 128), BF16)
    loaded = jax.ShapeDtypeStruct((PIECE + 54, 32, 128), BF16)
    return pl.pallas_call(
        split_kernel,
        out_shape=[piece, loaded, piece, piece, jax.ShapeDtypeStruct((27, 32, 128), BF16)],
        in_specs=[pl.BlockSpec(memory_space=pltpu.HBM)] * 6,
        out_specs=[VMEM] * 5,
        scratch_shapes=[pltpu.VMEM((8, 32), F32), pltpu.SemaphoreType.DMA((22,))],
        compiler_params=pltpu.CompilerParams(vmem_limit_bytes=60 << 20),
        name="split_features",
    )(features, w1, w2, b1.reshape(1, 32), b2.reshape(1, 32), lev)


def faces_kernel(near, lists_block, lists, *refs):
    pieces, sides, sem = refs[:4], refs[4:6], refs[6]
    copies = []
    for tier, run, out in ((1, 3, sides[0]), (0, 0, sides[1])):
        for c in range(2):
            b = jnp.maximum(lists[0, tier, c], 0)
            for m in range(4):
                i = 8 * tier + 4 * c + m
                copies.append(pltpu.make_async_copy(pieces[m].at[4 * run + b], out.at[4 * c + m], sem.at[i]))
    for copy in copies:
        copy.start()
    for out in sides:
        out[8] = jnp.zeros((32, 128), BF16)
        out[8, pl.ds(0, 4), pl.ds(0, 27)] = near[...].astype(F32).astype(BF16)
        out[8, pl.ds(8, 2), pl.ds(0, 2)] = lists_block[0].astype(F32).astype(BF16)
    for copy in copies:
        copy.wait()


def faces(neighbours, face_lists, pieces):
    side = jax.ShapeDtypeStruct((9, 32, 128), BF16)
    return pl.pallas_call(
        faces_kernel,
        out_shape=[side] * 2,
        in_specs=[VMEM, VMEM, SMEM] + [HBM] * 4,
        out_specs=[VMEM] * 2,
        scratch_shapes=[pltpu.SemaphoreType.DMA((16,))],
        compiler_params=pltpu.CompilerParams(vmem_limit_bytes=4 << 20),
        name="pick_faces",
    )(neighbours, face_lists, face_lists, *pieces)


def silu(v):
    return v / (1.0 + jnp.exp(-v))


def gather_padded(slots, pad, lead, slot, planes):
    x = lax.broadcasted_iota(jnp.int32, (1, 8, 128), 1)
    for dz, z_from, z_to in planes:
        for dy in (-1, 0, 1):
            y_from, y_to, n = SPAN[dy]
            parts = ([], [], [])
            for w in range(2):
                mid, left, right = (
                    slots[slot(w, offset(dz, dy, dx)), z_from, y_from : y_from + n] for dx in (0, -1, 1)
                )
                parts[0].append(pltpu.roll(jnp.where(x == 7, left, mid), 1, 1))
                parts[1].append(mid)
                parts[2].append(pltpu.roll(jnp.where(x == 0, right, mid), 7, 1))
            for d in range(3):
                tile = jnp.concatenate(parts[d], axis=1).astype(BF16)
                pad[lead, z_to, y_to : y_to + n, :, 128 * d : 128 * d + 128] = tile


OWN_PLANES = [(-1, 7, 0)] + [(0, z, z + 1) for z in range(8)] + [(1, 0, 9)]


def conv_pair(pad, lead, w):
    zero = jnp.zeros((128, 128), BF16)
    total = None
    blocks = [(zin, dy) for zin in range(4) for dy in range(3)]
    for first in range(0, 12, 2):
        left, right = [], []
        for zin, dy in blocks[first : first + 2]:
            planes = [pad[lead, zin + 2 * j, dy : dy + 8].reshape(128, 384) for j in range(4)]
            left.append(jnp.concatenate(planes, axis=0))
            for dx in range(3):
                even = w[9 * zin + 3 * dy + dx] if zin < 3 else zero
                odd = w[9 * (zin - 1) + 3 * dy + dx] if zin > 0 else zero
                right.append(jnp.concatenate([even, odd], axis=1))
        part = jnp.dot(
            jnp.concatenate(left, axis=1), jnp.concatenate(right, axis=0), preferred_element_type=F32
        )
        total = part if total is None else total + part
    return total


def conv_face(pad, w):
    total = None
    blocks = [(dz, dy) for dz in range(3) for dy in range(3)]
    for group in (blocks[0:2], blocks[2:4], blocks[4:6], blocks[6:9]):
        left, right = [], []
        for dz, dy in group:
            sides = [pad[side, dz, dy : dy + 8].reshape(128, 384) for side in range(2)]
            left.append(jnp.concatenate(sides, axis=0))
            right += [w[9 * dz + 3 * dy + dx] for dx in range(3)]
        part = jnp.dot(
            jnp.concatenate(left, axis=1), jnp.concatenate(right, axis=0), preferred_element_type=F32
        )
        total = part if total is None else total + part
    return total


def conv_kernel(tab, fl, *refs):
    feat, sides, own_w, far_w = refs[0:4], refs[4:6], refs[6:8], refs[8:12]
    outs = refs[12:16]
    fs, hs, w1, w2, bias, sent, sent_int, tables, slots, pad, pad_face, acc, shift, turned, sem = refs[16:]
    me = lax.axis_index("chan")
    odd = lax.axis_index("slab") % 2

    f_copies, t_copies = [], []
    for side in range(2):
        t_copies.append(
            pltpu.make_async_copy(sides[side].at[8, pl.ds(0, 16)], sent.at[side], sem.at[side])
        )
        f_copies.append(pltpu.make_async_copy(sides[side].at[pl.ds(0, 8)], hs.at[side], sem.at[2 + side]))
    for m in range(4):
        f_copies.append(pltpu.make_async_copy(feat[m].at[pl.ds(0, 16)], fs.at[m], sem.at[4 + m]))
        f_copies.append(pltpu.make_async_copy(feat[m].at[16, pl.ds(0, 16)], bias.at[m], sem.at[8 + m]))
    for copy in t_copies + f_copies:
        copy.start()

    def load_shard(m, layer, source):
        g = 32 * m if layer == 0 else pl.multiple_of((me ^ m) * 32, 32)
        return pltpu.make_async_copy(source, (w1, w2)[layer].at[:, pl.ds(g, 32), :], sem.at[12 + 2 * m + layer])

    w_copies = ([], [])
    for layer in range(2):
        near = [load_shard(0, layer, own_w[layer])]
        near.append(load_shard(1, layer, feat[1].at[pl.ds(PIECE + 27 * layer, 27)]))
        for copy in near:
            copy.start()
        w_copies[layer].extend(near)
        for m in (2, 3):
            mine, other = far_w[m - 2], far_w[m]

            @pl.when(odd == layer)
            def _():
                load_shard(m, layer, mine).start()

            @pl.when(odd != layer)
            def _():
                load_shard(m, layer, other).start()

            w_copies[layer].append(load_shard(m, layer, mine))
    w1_copies, w2_copies = w_copies
    for copy in t_copies:
        copy.wait()
    sent_int[...] = sent[...].astype(F32).astype(jnp.int32).reshape(32, 128)
    to_scalars = pltpu.make_async_copy(sent_int, tables, sem.at[24])
    to_scalars.start()
    for copy in f_copies:
        copy.wait()

    slots[NONE] = jnp.zeros((8, 8, 8, 128), F32)
    for b in range(4):
        for v in range(4):
            brick = jnp.concatenate([fs[m, 4 * v + b] for m in range(4)], axis=0)
            slots[b, 2 * v : 2 * v + 2] = brick.T.astype(F32).reshape(2, 8, 8, 128)
    for side in range(2):
        for c in range(2):
            face = jnp.concatenate([hs[side, 4 * c + m] for m in range(4)], axis=0)
            first = 6 if side == 0 else 0
            slots[4 + 2 * side + c, first : first + 2] = face.T.astype(F32).reshape(2, 8, 8, 128)

    to_scalars.wait()

    def own(pair):
        def slot(w, k):
            t = tab[2 * pair + w, k]
            return jnp.where(t < 0, NONE, t)

        return slot

    def below(c, k):
        t = tables[0 + jnp.maximum(tables[9, c], 0), k]
        if k < 18:
            found = jnp.where(t == tables[9, 0], 4, jnp.where(t == tables[9, 1], 5, NONE))
            return jnp.where(t < 0, NONE, found)
        u = fl[0, 0, jnp.clip(t - 6, 0, 1)]
        return jnp.where((t < 6) | (u < 0), NONE, u)

    def above(c, k):
        t = tables[16 + jnp.maximum(tables[24, c], 0), k]
        if k >= 9:
            found = jnp.where(t == tables[24, 0], 6, jnp.where(t == tables[24, 1], 7, NONE))
            return jnp.where(t < 0, NONE, found)
        u = fl[0, 1, jnp.clip(t - 4, 0, 1)]
        return jnp.where((t < 4) | (t > 5) | (u < 0), NONE, u)

    gather_padded(slots, pad_face, 0, below, [(0, 6, 0), (0, 7, 1), (1, 0, 2)])
    gather_padded(slots, pad_face, 1, above, [(-1, 7, 0), (0, 0, 1), (0, 1, 2)])
    for pair in range(2):
        gather_padded(slots, pad, pair, own(pair), OWN_PLANES)

    for copy in w1_copies:
        copy.wait()
    values = sum(bias[m].astype(F32) for m in range(4))
    shift[...] = values[0:8] + values[8:16]
    shift_second = shift[1:2, :]
    shift_first = shift[0:1, :] + shift[pl.ds(2 + me, 1), :]

    def finish(pair, moved):
        for j in range(4):
            for zo in range(2):
                tile = silu(acc[128 * j : 128 * j + 128, 128 * zo : 128 * zo + 128] + moved)
                tile = tile.reshape(8, 2, 8, 128)
                for w in range(2):
                    b = 2 * pair + w
                    slots[b, 2 * j + zo] = jnp.where(tab[b, 13] >= 0, tile[:, w], 0.0)

    for pair in range(2):
        acc[...] = conv_pair(pad, pair, w1)
        finish(pair, shift_first)
    faces = silu(conv_face(pad_face, w1) + shift_first).reshape(2, 8, 2, 8, 128)
    for c in range(2):
        slots[4 + c, 7] = faces[0, :, c]
        slots[6 + c, 0] = faces[1, :, c]

    for pair in range(2):
        gather_padded(slots, pad, pair, own(pair), OWN_PLANES)
    for copy in w2_copies:
        copy.wait()
    for pair in range(2):
        acc[...] = conv_pair(pad, pair, w2)
        finish(pair, shift_second)
    for b in range(4):
        brick = slots[b].reshape(512, 128).astype(BF16).T
        for g in range(4):
            turned[g, b] = brick[32 * g : 32 * g + 32]
    out_copies = [
        pltpu.make_async_copy(turned.at[me ^ m], outs[m], sem.at[20 + m]) for m in range(4)
    ]
    for copy in out_copies:
        copy.start()
    for copy in out_copies:
        copy.wait()


def convolve(neighbours, face_lists, feat, sides, own_w, far_w):
    piece = jax.ShapeDtypeStruct((4, 32, 512), BF16)
    return pl.pallas_call(
        conv_kernel,
        out_shape=[piece] * 4,
        in_specs=[SMEM] * 2 + [HBM] * 12,
        out_specs=[HBM] * 4,
        scratch_shapes=[
            pltpu.VMEM((4, 16, 32, 128), BF16),
            pltpu.VMEM((2, 8, 32, 128), BF16),
            pltpu.VMEM((27, 128, 128), BF16),
            pltpu.VMEM((27, 128, 128), BF16),
            pltpu.VMEM((4, 16, 128), BF16),
            pltpu.VMEM((2, 16, 128), BF16),
            pltpu.VMEM((32, 128), jnp.int32),
            pltpu.SMEM((32, 128), jnp.int32),
            pltpu.VMEM((9, 8, 8, 8, 128), F32),
            pltpu.VMEM((2, 10, 10, 16, 384), BF16),
            pltpu.VMEM((2, 3, 10, 16, 384), BF16),
            pltpu.VMEM((512, 256), F32),
            pltpu.VMEM((8, 128), F32),
            pltpu.VMEM((4, 4, 32, 512), BF16),
            pltpu.SemaphoreType.DMA((32,)),
        ],
        compiler_params=pltpu.CompilerParams(vmem_limit_bytes=40 << 20),
        cost_estimate=pl.CostEstimate(flops=8 * 10**9, bytes_accessed=4 * 10**6, transcendentals=10**6),
        name="convolve",
    )(neighbours, face_lists, *feat, *sides, *own_w, *far_w)


def join_kernel(*refs):
    pieces, out, sem = refs[:4], refs[4], refs[5]
    me = lax.axis_index("chan")
    copies = [pltpu.make_async_copy(pieces[m], out.at[me ^ m], sem.at[m]) for m in range(4)]
    for copy in copies:
        copy.start()
    for copy in copies:
        copy.wait()


def join(pieces):
    return pl.pallas_call(
        join_kernel,
        out_shape=jax.ShapeDtypeStruct((4, 4, 32, 512), BF16),
        in_specs=[HBM] * 4,
        out_specs=HBM,
        scratch_shapes=[pltpu.SemaphoreType.DMA((4,))],
        compiler_params=pltpu.CompilerParams(vmem_limit_bytes=8 << 20),
        name="join_levels",
    )(*pieces)


def swap(value, m):
    return lax.ppermute(value, "chan", [(i, i ^ m) for i in range(4)])


def swap_slabs(value, m):
    count = lax.axis_size("slab")
    pairs = [(4 * s + g, 4 * (s ^ 1) + (g ^ m)) for s in range(count) for g in range(4)]
    return lax.ppermute(value, ("slab", "chan"), pairs)


def to_slab(value, steps):
    count = lax.axis_size("slab")
    return lax.ppermute(value, "slab", [(s, (s + steps) % count) for s in range(count)])


def shards(features, neighbours, face_lists, w_first, b_first, w_second, b_second, level_embed):
    w1, w2 = w_first.transpose(0, 2, 1), w_second.transpose(0, 2, 1)
    own, one, two, three, cross = split(features, w1, w2, b_first, b_second, level_embed)
    fetched, two, three = lax.optimization_barrier((swap(cross, 2), swap(two, 2), swap(three, 3)))
    pieces = [own, swap(one, 1), two, three]
    up, down = faces(neighbours, face_lists, pieces)
    sides = [to_slab(up, 1), to_slab(down, -1)]
    far = [fetched, swap(fetched, 1), swap_slabs(fetched, 0), swap_slabs(fetched, 1)]
    outs = convolve(neighbours, face_lists, pieces, sides, (w1, w2), far)
    return join([outs[0]] + [swap(outs[m], m) for m in (1, 2, 3)])


def solution(mesh):
    placed = (
        P(None, "slab", "chan", None),
        P("slab", None),
        P("slab", None, None),
        P(None, None, "chan"),
        P("chan"),
        P(None, None, "chan"),
        P("chan"),
        P(None, "chan"),
    )
    return jax.shard_map(
        shards, mesh=mesh, in_specs=placed, out_specs=P(None, "slab", "chan", None), check_vma=False
    )
```

```python
import jax
import jax.numpy as jnp
from jax import lax
from jax.experimental import pallas as pl
from jax.experimental.pallas import tpu as pltpu
from jax.sharding import PartitionSpec as P

BF16, F32 = jnp.bfloat16, jnp.float32
NONE = 8
HBM = pl.BlockSpec(memory_space=pl.ANY)
VMEM = pl.BlockSpec(memory_space=pltpu.VMEM)
SMEM = pl.BlockSpec(memory_space=pltpu.SMEM)
SPAN = {-1: (7, 0, 1), 0: (0, 1, 8), 1: (0, 9, 1)}


def offset(dz, dy, dx):
    return 9 * (dz + 1) + 3 * (dy + 1) + (dx + 1)


PIECE = 17


def split_kernel(feat, w1, w2, b1, b2, lev, *refs):
    pieces, cross, held, sem = refs[:4], refs[4], refs[5], refs[6]
    me = lax.axis_index("chan")
    odd = layer_of_slab()

    @pl.when(odd == 0)
    def _():
        pltpu.make_async_copy(w1, cross, sem.at[0]).start()

    @pl.when(odd == 1)
    def _():
        pltpu.make_async_copy(w2, cross, sem.at[0]).start()

    small = [
        pltpu.make_async_copy(b1, held.at[pl.ds(0, 1)], sem.at[1]),
        pltpu.make_async_copy(b2, held.at[pl.ds(1, 1)], sem.at[2]),
        pltpu.make_async_copy(lev, held.at[pl.ds(2, 4)], sem.at[3]),
    ]
    large = [
        pltpu.make_async_copy(w, pieces[1].at[pl.ds(PIECE + 27 * layer, 27)], sem.at[4 + layer])
        for layer, w in enumerate((w1, w2))
    ]
    for m in range(4):
        for v in range(4):
            run = feat.at[me ^ m, :, :, pl.ds(128 * v, 128)]
            large.append(
                pltpu.make_async_copy(run, pieces[m].at[pl.ds(4 * v, 4)], sem.at[6 + 4 * m + v])
            )
    held[pl.ds(6, 2), :] = jnp.zeros((2, 32), F32)
    for copy in small + large:
        copy.start()
    for copy in small:
        copy.wait()

    values = jnp.concatenate([held[...]] * 4, axis=1)
    lane = lax.broadcasted_iota(jnp.int32, (8, 128), 1)
    values = jnp.where(lane // 32 == me, values, 0.0)
    high = values.astype(BF16).astype(F32)
    values = jnp.concatenate([high, values - high, jnp.zeros((16, 128), F32)], axis=0).astype(BF16)
    for m in range(4):
        pieces[m][16] = values
    pltpu.make_async_copy(w1, cross, sem.at[0]).wait()
    for copy in large:
        copy.wait()


def split(features, w1, w2, b1, b2, lev):
    piece = jax.ShapeDtypeStruct((PIECE, 32, 128), BF16)
    loaded = jax.ShapeDtypeStruct((PIECE + 54, 32, 128), BF16)
    return pl.pallas_call(
        split_kernel,
        out_shape=[piece, loaded, piece, piece, jax.ShapeDtypeStruct((27, 32, 128), BF16)],
        in_specs=[pl.BlockSpec(memory_space=pltpu.HBM)] * 6,
        out_specs=[VMEM] * 5,
        scratch_shapes=[pltpu.VMEM((8, 32), F32), pltpu.SemaphoreType.DMA((22,))],
        compiler_params=pltpu.CompilerParams(vmem_limit_bytes=60 << 20),
        name="split_features",
    )(features, w1, w2, b1.reshape(1, 32), b2.reshape(1, 32), lev)


def faces_kernel(near, lists_block, lists, *refs):
    pieces, sides, sem = refs[:4], refs[4:6], refs[6]
    copies = []
    for tier, run, out in ((1, 3, sides[0]), (0, 0, sides[1])):
        for c in range(2):
            b = jnp.maximum(lists[0, tier, c], 0)
            for m in range(4):
                i = 8 * tier + 4 * c + m
                copies.append(pltpu.make_async_copy(pieces[m].at[4 * run + b], out.at[4 * c + m], sem.at[i]))
    for copy in copies:
        copy.start()
    for out in sides:
        out[8] = jnp.zeros((32, 128), BF16)
        out[8, pl.ds(0, 4), pl.ds(0, 27)] = near[...].astype(F32).astype(BF16)
        out[8, pl.ds(8, 2), pl.ds(0, 2)] = lists_block[0].astype(F32).astype(BF16)
    for copy in copies:
        copy.wait()


def faces(neighbours, face_lists, pieces):
    side = jax.ShapeDtypeStruct((9, 32, 128), BF16)
    return pl.pallas_call(
        faces_kernel,
        out_shape=[side] * 2,
        in_specs=[VMEM, VMEM, SMEM] + [HBM] * 4,
        out_specs=[VMEM] * 2,
        scratch_shapes=[pltpu.SemaphoreType.DMA((16,))],
        compiler_params=pltpu.CompilerParams(vmem_limit_bytes=4 << 20),
        name="pick_faces",
    )(neighbours, face_lists, face_lists, *pieces)


def silu(v):
    return v / (1.0 + jnp.exp(-v))


def gather_padded(slots, pad, lead, slot, planes):
    x = lax.broadcasted_iota(jnp.int32, (1, 8, 128), 1)
    for dz, z_from, z_to in planes:
        for dy in (-1, 0, 1):
            y_from, y_to, n = SPAN[dy]
            parts = ([], [], [])
            for w in range(2):
                mid, left, right = (
                    slots[slot(w, offset(dz, dy, dx)), z_from, y_from : y_from + n] for dx in (0, -1, 1)
                )
                parts[0].append(pltpu.roll(jnp.where(x == 7, left, mid), 1, 1))
                parts[1].append(mid)
                parts[2].append(pltpu.roll(jnp.where(x == 0, right, mid), 7, 1))
            for d in range(3):
                tile = jnp.concatenate(parts[d], axis=1).astype(BF16)
                pad[lead, z_to, y_to : y_to + n, :, 128 * d : 128 * d + 128] = tile


OWN_PLANES = [(-1, 7, 0)] + [(0, z, z + 1) for z in range(8)] + [(1, 0, 9)]


def conv_pair(pad, lead, w):
    zero = jnp.zeros((128, 128), BF16)
    total = None
    blocks = [(zin, dy) for zin in range(4) for dy in range(3)]
    for first in range(0, 12, 2):
        left, right = [], []
        for zin, dy in blocks[first : first + 2]:
            planes = [pad[lead, zin + 2 * j, dy : dy + 8].reshape(128, 384) for j in range(4)]
            left.append(jnp.concatenate(planes, axis=0))
            for dx in range(3):
                even = w[9 * zin + 3 * dy + dx] if zin < 3 else zero
                odd = w[9 * (zin - 1) + 3 * dy + dx] if zin > 0 else zero
                right.append(jnp.concatenate([even, odd], axis=1))
        part = jnp.dot(
            jnp.concatenate(left, axis=1), jnp.concatenate(right, axis=0), preferred_element_type=F32
        )
        total = part if total is None else total + part
    return total


def conv_face(pad, w):
    total = None
    blocks = [(dz, dy) for dz in range(3) for dy in range(3)]
    for group in (blocks[0:2], blocks[2:4], blocks[4:6], blocks[6:9]):
        left, right = [], []
        for dz, dy in group:
            sides = [pad[side, dz, dy : dy + 8].reshape(128, 384) for side in range(2)]
            left.append(jnp.concatenate(sides, axis=0))
            right += [w[9 * dz + 3 * dy + dx] for dx in range(3)]
        part = jnp.dot(
            jnp.concatenate(left, axis=1), jnp.concatenate(right, axis=0), preferred_element_type=F32
        )
        total = part if total is None else total + part
    return total


def conv_kernel(tab, fl, *refs):
    feat, sides, own_w, far_w = refs[0:4], refs[4:6], refs[6:8], refs[8:12]
    outs = refs[12:16]
    fs, hs, w1, w2, bias, sent, sent_int, tables, slots, pad, pad_face, acc, shift, turned, sem = refs[16:]
    me = lax.axis_index("chan")
    odd = layer_of_slab()

    f_copies, t_copies = [], []
    for side in range(2):
        t_copies.append(
            pltpu.make_async_copy(sides[side].at[8, pl.ds(0, 16)], sent.at[side], sem.at[side])
        )
        f_copies.append(pltpu.make_async_copy(sides[side].at[pl.ds(0, 8)], hs.at[side], sem.at[2 + side]))
    for m in range(4):
        f_copies.append(pltpu.make_async_copy(feat[m].at[pl.ds(0, 16)], fs.at[m], sem.at[4 + m]))
        f_copies.append(pltpu.make_async_copy(feat[m].at[16, pl.ds(0, 16)], bias.at[m], sem.at[8 + m]))
    for copy in t_copies + f_copies:
        copy.start()

    def load_shard(m, layer, source):
        g = 32 * m if layer == 0 else pl.multiple_of((me ^ m) * 32, 32)
        return pltpu.make_async_copy(source, (w1, w2)[layer].at[:, pl.ds(g, 32), :], sem.at[12 + 2 * m + layer])

    w_copies = ([], [])
    for layer in range(2):
        near = [load_shard(0, layer, own_w[layer])]
        near.append(load_shard(1, layer, feat[1].at[pl.ds(PIECE + 27 * layer, 27)]))
        for copy in near:
            copy.start()
        w_copies[layer].extend(near)
        for m in (2, 3):
            mine, other = far_w[m - 2], far_w[m]

            @pl.when(odd == layer)
            def _():
                load_shard(m, layer, mine).start()

            @pl.when(odd != layer)
            def _():
                load_shard(m, layer, other).start()

            w_copies[layer].append(load_shard(m, layer, mine))
    w1_copies, w2_copies = w_copies
    for copy in t_copies:
        copy.wait()
    sent_int[...] = sent[...].astype(F32).astype(jnp.int32).reshape(32, 128)
    to_scalars = pltpu.make_async_copy(sent_int, tables, sem.at[24])
    to_scalars.start()
    for copy in f_copies:
        copy.wait()

    slots[NONE] = jnp.zeros((8, 8, 8, 128), F32)
    for b in range(4):
        for v in range(4):
            brick = jnp.concatenate([fs[m, 4 * v + b] for m in range(4)], axis=0)
            slots[b, 2 * v : 2 * v + 2] = brick.T.astype(F32).reshape(2, 8, 8, 128)
    for side in range(2):
        for c in range(2):
            face = jnp.concatenate([hs[side, 4 * c + m] for m in range(4)], axis=0)
            first = 6 if side == 0 else 0
            slots[4 + 2 * side + c, first : first + 2] = face.T.astype(F32).reshape(2, 8, 8, 128)

    to_scalars.wait()

    def own(pair):
        def slot(w, k):
            t = tab[2 * pair + w, k]
            return jnp.where(t < 0, NONE, t)

        return slot

    def below(c, k):
        t = tables[0 + jnp.maximum(tables[9, c], 0), k]
        if k < 18:
            found = jnp.where(t == tables[9, 0], 4, jnp.where(t == tables[9, 1], 5, NONE))
            return jnp.where(t < 0, NONE, found)
        u = fl[0, 0, jnp.clip(t - 6, 0, 1)]
        return jnp.where((t < 6) | (u < 0), NONE, u)

    def above(c, k):
        t = tables[16 + jnp.maximum(tables[24, c], 0), k]
        if k >= 9:
            found = jnp.where(t == tables[24, 0], 6, jnp.where(t == tables[24, 1], 7, NONE))
            return jnp.where(t < 0, NONE, found)
        u = fl[0, 1, jnp.clip(t - 4, 0, 1)]
        return jnp.where((t < 4) | (t > 5) | (u < 0), NONE, u)

    gather_padded(slots, pad_face, 0, below, [(0, 6, 0), (0, 7, 1), (1, 0, 2)])
    gather_padded(slots, pad_face, 1, above, [(-1, 7, 0), (0, 0, 1), (0, 1, 2)])
    for pair in range(2):
        gather_padded(slots, pad, pair, own(pair), OWN_PLANES)

    for copy in w1_copies:
        copy.wait()
    values = sum(bias[m].astype(F32) for m in range(4))
    shift[...] = values[0:8] + values[8:16]
    shift_second = shift[1:2, :]
    shift_first = shift[0:1, :] + shift[pl.ds(2 + me, 1), :]

    def finish(pair, moved):
        for j in range(4):
            for zo in range(2):
                tile = silu(acc[128 * j : 128 * j + 128, 128 * zo : 128 * zo + 128] + moved)
                tile = tile.reshape(8, 2, 8, 128)
                for w in range(2):
                    b = 2 * pair + w
                    slots[b, 2 * j + zo] = jnp.where(tab[b, 13] >= 0, tile[:, w], 0.0)

    for pair in range(2):
        acc[...] = conv_pair(pad, pair, w1)
        finish(pair, shift_first)
    faces = silu(conv_face(pad_face, w1) + shift_first).reshape(2, 8, 2, 8, 128)
    for c in range(2):
        slots[4 + c, 7] = faces[0, :, c]
        slots[6 + c, 0] = faces[1, :, c]

    for pair in range(2):
        gather_padded(slots, pad, pair, own(pair), OWN_PLANES)
    for copy in w2_copies:
        copy.wait()
    for pair in range(2):
        acc[...] = conv_pair(pad, pair, w2)
        finish(pair, shift_second)
    for b in range(4):
        brick = slots[b].reshape(512, 128).astype(BF16).T
        for g in range(4):
            turned[g, b] = brick[32 * g : 32 * g + 32]
    out_copies = [
        pltpu.make_async_copy(turned.at[me ^ m], outs[m], sem.at[20 + m]) for m in range(4)
    ]
    for copy in out_copies:
        copy.start()
    for copy in out_copies:
        copy.wait()


def convolve(neighbours, face_lists, feat, sides, own_w, far_w):
    piece = jax.ShapeDtypeStruct((4, 32, 512), BF16)
    return pl.pallas_call(
        conv_kernel,
        out_shape=[piece] * 4,
        in_specs=[SMEM] * 2 + [HBM] * 12,
        out_specs=[HBM] * 4,
        scratch_shapes=[
            pltpu.VMEM((4, 16, 32, 128), BF16),
            pltpu.VMEM((2, 8, 32, 128), BF16),
            pltpu.VMEM((27, 128, 128), BF16),
            pltpu.VMEM((27, 128, 128), BF16),
            pltpu.VMEM((4, 16, 128), BF16),
            pltpu.VMEM((2, 16, 128), BF16),
            pltpu.VMEM((32, 128), jnp.int32),
            pltpu.SMEM((32, 128), jnp.int32),
            pltpu.VMEM((9, 8, 8, 8, 128), F32),
            pltpu.VMEM((2, 10, 10, 16, 384), BF16),
            pltpu.VMEM((2, 3, 10, 16, 384), BF16),
            pltpu.VMEM((512, 256), F32),
            pltpu.VMEM((8, 128), F32),
            pltpu.VMEM((4, 4, 32, 512), BF16),
            pltpu.SemaphoreType.DMA((32,)),
        ],
        compiler_params=pltpu.CompilerParams(vmem_limit_bytes=40 << 20),
        cost_estimate=pl.CostEstimate(flops=8 * 10**9, bytes_accessed=4 * 10**6, transcendentals=10**6),
        name="convolve",
    )(neighbours, face_lists, *feat, *sides, *own_w, *far_w)


def join_kernel(*refs):
    pieces, out, sem = refs[:4], refs[4], refs[5]
    me = lax.axis_index("chan")
    copies = [pltpu.make_async_copy(pieces[m], out.at[me ^ m], sem.at[m]) for m in range(4)]
    for copy in copies:
        copy.start()
    for copy in copies:
        copy.wait()


def join(pieces):
    return pl.pallas_call(
        join_kernel,
        out_shape=jax.ShapeDtypeStruct((4, 4, 32, 512), BF16),
        in_specs=[HBM] * 4,
        out_specs=HBM,
        scratch_shapes=[pltpu.SemaphoreType.DMA((4,))],
        compiler_params=pltpu.CompilerParams(vmem_limit_bytes=8 << 20),
        name="join_levels",
    )(*pieces)


def swap(value, m):
    return lax.ppermute(value, "chan", [(i, i ^ m) for i in range(4)])


def layer_of_slab():
    slab = lax.axis_index("slab")
    return (slab + slab // 8) % 2


def swap_slabs(value, step, m):
    count = lax.axis_size("slab")
    pairs = [(4 * s + g, 4 * (s ^ step) + (g ^ m)) for s in range(count) for g in range(4)]
    return lax.ppermute(value, ("slab", "chan"), pairs)


def to_slab(value, steps):
    count = lax.axis_size("slab")
    return lax.ppermute(value, "slab", [(s, (s + steps) % count) for s in range(count)])


def shards(features, neighbours, face_lists, w_first, b_first, w_second, b_second, level_embed):
    w1, w2 = w_first.transpose(0, 2, 1), w_second.transpose(0, 2, 1)
    own, one, two, three, cross = split(features, w1, w2, b_first, b_second, level_embed)
    fetched, two, three = lax.optimization_barrier((swap(cross, 2), swap(two, 2), swap(three, 3)))
    pieces = [own, swap(one, 1), two, three]
    up, down = faces(neighbours, face_lists, pieces)
    sides = [to_slab(up, 1), to_slab(down, -1)]
    far = [fetched, swap(fetched, 1), swap_slabs(fetched, 1, 0), swap_slabs(fetched, 8, 1)]
    outs = convolve(neighbours, face_lists, pieces, sides, (w1, w2), far)
    return join([outs[0]] + [swap(outs[m], m) for m in (1, 2, 3)])


def solution(mesh):
    placed = (
        P(None, "slab", "chan", None),
        P("slab", None),
        P("slab", None, None),
        P(None, None, "chan"),
        P("chan"),
        P(None, None, "chan"),
        P("chan"),
        P(None, "chan"),
    )
    return jax.shard_map(
        shards, mesh=mesh, in_specs=placed, out_specs=P(None, "slab", "chan", None), check_vma=False
    )
```

```python
import jax
import jax.numpy as jnp
from jax import lax
from jax.experimental import pallas as pl
from jax.experimental.pallas import tpu as pltpu
from jax.sharding import PartitionSpec as P

BF16, F32 = jnp.bfloat16, jnp.float32
NONE = 8
HBM = pl.BlockSpec(memory_space=pl.ANY)
VMEM = pl.BlockSpec(memory_space=pltpu.VMEM)
SMEM = pl.BlockSpec(memory_space=pltpu.SMEM)
SPAN = {-1: (7, 0, 1), 0: (0, 1, 8), 1: (0, 9, 1)}


def offset(dz, dy, dx):
    return 9 * (dz + 1) + 3 * (dy + 1) + (dx + 1)


PIECE = 17


def split_kernel(feat, w1, w2, b1, b2, lev, *refs):
    pieces, cross, held, sem = refs[:4], refs[4], refs[5], refs[6]
    me = lax.axis_index("chan")
    odd = layer_of_slab()

    @pl.when(odd == 0)
    def _():
        pltpu.make_async_copy(w1, cross, sem.at[0]).start()

    @pl.when(odd == 1)
    def _():
        pltpu.make_async_copy(w2, cross, sem.at[0]).start()

    small = [
        pltpu.make_async_copy(b1, held.at[pl.ds(0, 1)], sem.at[1]),
        pltpu.make_async_copy(b2, held.at[pl.ds(1, 1)], sem.at[2]),
        pltpu.make_async_copy(lev, held.at[pl.ds(2, 4)], sem.at[3]),
    ]
    large = [
        pltpu.make_async_copy(w, pieces[1].at[pl.ds(PIECE + 27 * layer, 27)], sem.at[4 + layer])
        for layer, w in enumerate((w1, w2))
    ]
    for m in range(4):
        for v in range(4):
            run = feat.at[me ^ m, :, :, pl.ds(128 * v, 128)]
            large.append(
                pltpu.make_async_copy(run, pieces[m].at[pl.ds(4 * v, 4)], sem.at[6 + 4 * m + v])
            )
    held[pl.ds(6, 2), :] = jnp.zeros((2, 32), F32)
    for copy in small + large:
        copy.start()
    for copy in small:
        copy.wait()

    values = jnp.concatenate([held[...]] * 4, axis=1)
    lane = lax.broadcasted_iota(jnp.int32, (8, 128), 1)
    values = jnp.where(lane // 32 == me, values, 0.0)
    high = values.astype(BF16).astype(F32)
    values = jnp.concatenate([high, values - high, jnp.zeros((16, 128), F32)], axis=0).astype(BF16)
    for m in range(4):
        pieces[m][16] = values
    pltpu.make_async_copy(w1, cross, sem.at[0]).wait()
    for copy in large:
        copy.wait()


def split(features, w1, w2, b1, b2, lev):
    piece = jax.ShapeDtypeStruct((PIECE, 32, 128), BF16)
    loaded = jax.ShapeDtypeStruct((PIECE + 54, 32, 128), BF16)
    return pl.pallas_call(
        split_kernel,
        out_shape=[piece, loaded, piece, piece, jax.ShapeDtypeStruct((27, 32, 128), BF16)],
        in_specs=[pl.BlockSpec(memory_space=pltpu.HBM)] * 6,
        out_specs=[VMEM] * 5,
        scratch_shapes=[pltpu.VMEM((8, 32), F32), pltpu.SemaphoreType.DMA((22,))],
        compiler_params=pltpu.CompilerParams(vmem_limit_bytes=60 << 20),
        name="split_features",
    )(features, w1, w2, b1.reshape(1, 32), b2.reshape(1, 32), lev)


def faces_kernel(near, lists_block, lists, *refs):
    pieces, sides, sem = refs[:4], refs[4:6], refs[6]
    odd = lax.axis_index("slab") % 2
    copies = []
    for i, out in enumerate(sides):
        tier = (odd + 1 + i) % 2
        for c in range(2):
            b = jnp.maximum(lists[0, tier, c], 0)
            for m in range(4):
                source = pieces[m].at[12 * tier + b]
                copies.append(pltpu.make_async_copy(source, out.at[4 * c + m], sem.at[8 * i + 4 * c + m]))
    for copy in copies:
        copy.start()
    for out in sides:
        out[8] = jnp.zeros((32, 128), BF16)
        out[8, pl.ds(0, 4), pl.ds(0, 27)] = near[...].astype(F32).astype(BF16)
        out[8, pl.ds(8, 2), pl.ds(0, 2)] = lists_block[0].astype(F32).astype(BF16)
    for copy in copies:
        copy.wait()


def faces(neighbours, face_lists, pieces):
    side = jax.ShapeDtypeStruct((9, 32, 128), BF16)
    return pl.pallas_call(
        faces_kernel,
        out_shape=[side] * 2,
        in_specs=[VMEM, VMEM, SMEM] + [HBM] * 4,
        out_specs=[VMEM] * 2,
        scratch_shapes=[pltpu.SemaphoreType.DMA((16,))],
        compiler_params=pltpu.CompilerParams(vmem_limit_bytes=4 << 20),
        name="pick_faces",
    )(neighbours, face_lists, face_lists, *pieces)


def silu(v):
    return v / (1.0 + jnp.exp(-v))


def gather_padded(slots, pad, lead, slot, planes):
    x = lax.broadcasted_iota(jnp.int32, (1, 8, 128), 1)
    for dz, z_from, z_to in planes:
        for dy in (-1, 0, 1):
            y_from, y_to, n = SPAN[dy]
            parts = ([], [], [])
            for w in range(2):
                mid, left, right = (
                    slots[slot(w, offset(dz, dy, dx)), z_from, y_from : y_from + n] for dx in (0, -1, 1)
                )
                parts[0].append(pltpu.roll(jnp.where(x == 7, left, mid), 1, 1))
                parts[1].append(mid)
                parts[2].append(pltpu.roll(jnp.where(x == 0, right, mid), 7, 1))
            for d in range(3):
                tile = jnp.concatenate(parts[d], axis=1).astype(BF16)
                pad[lead, z_to, y_to : y_to + n, :, 128 * d : 128 * d + 128] = tile


OWN_PLANES = [(-1, 7, 0)] + [(0, z, z + 1) for z in range(8)] + [(1, 0, 9)]


def conv_pair(pad, lead, w):
    zero = jnp.zeros((128, 128), BF16)
    total = None
    blocks = [(zin, dy) for zin in range(4) for dy in range(3)]
    for first in range(0, 12, 2):
        left, right = [], []
        for zin, dy in blocks[first : first + 2]:
            planes = [pad[lead, zin + 2 * j, dy : dy + 8].reshape(128, 384) for j in range(4)]
            left.append(jnp.concatenate(planes, axis=0))
            for dx in range(3):
                even = w[9 * zin + 3 * dy + dx] if zin < 3 else zero
                odd = w[9 * (zin - 1) + 3 * dy + dx] if zin > 0 else zero
                right.append(jnp.concatenate([even, odd], axis=1))
        part = jnp.dot(
            jnp.concatenate(left, axis=1), jnp.concatenate(right, axis=0), preferred_element_type=F32
        )
        total = part if total is None else total + part
    return total


def conv_face(pad, w):
    total = None
    blocks = [(dz, dy) for dz in range(3) for dy in range(3)]
    for group in (blocks[0:2], blocks[2:4], blocks[4:6], blocks[6:9]):
        left, right = [], []
        for dz, dy in group:
            sides = [pad[side, dz, dy : dy + 8].reshape(128, 384) for side in range(2)]
            left.append(jnp.concatenate(sides, axis=0))
            right += [w[9 * dz + 3 * dy + dx] for dx in range(3)]
        part = jnp.dot(
            jnp.concatenate(left, axis=1), jnp.concatenate(right, axis=0), preferred_element_type=F32
        )
        total = part if total is None else total + part
    return total


def conv_kernel(tab, fl, *refs):
    feat, sides, own_w, far_w = refs[0:4], refs[4:6], refs[6:8], refs[8:12]
    outs = refs[12:16]
    fs, hs, w1, w2, bias, sent, sent_int, tables, slots, pad, pad_face, acc, shift, turned, sem = refs[16:]
    me = lax.axis_index("chan")
    odd = layer_of_slab()

    f_copies, t_copies = [], []
    for i in range(2):
        side = (lax.axis_index("slab") + 1 + i) % 2
        t_copies.append(pltpu.make_async_copy(sides[i].at[8, pl.ds(0, 16)], sent.at[side], sem.at[i]))
        f_copies.append(pltpu.make_async_copy(sides[i].at[pl.ds(0, 8)], hs.at[side], sem.at[2 + i]))
    for m in range(4):
        f_copies.append(pltpu.make_async_copy(feat[m].at[pl.ds(0, 16)], fs.at[m], sem.at[4 + m]))
        f_copies.append(pltpu.make_async_copy(feat[m].at[16, pl.ds(0, 16)], bias.at[m], sem.at[8 + m]))
    for copy in t_copies + f_copies:
        copy.start()

    def load_shard(m, layer, source):
        g = 32 * m if layer == 0 else pl.multiple_of((me ^ m) * 32, 32)
        return pltpu.make_async_copy(source, (w1, w2)[layer].at[:, pl.ds(g, 32), :], sem.at[12 + 2 * m + layer])

    w_copies = ([], [])
    for layer in range(2):
        near = [load_shard(0, layer, own_w[layer])]
        near.append(load_shard(1, layer, feat[1].at[pl.ds(PIECE + 27 * layer, 27)]))
        for copy in near:
            copy.start()
        w_copies[layer].extend(near)
        for m in (2, 3):
            mine, other = far_w[m - 2], far_w[m]

            @pl.when(odd == layer)
            def _():
                load_shard(m, layer, mine).start()

            @pl.when(odd != layer)
            def _():
                load_shard(m, layer, other).start()

            w_copies[layer].append(load_shard(m, layer, mine))
    w1_copies, w2_copies = w_copies
    for copy in t_copies:
        copy.wait()
    sent_int[...] = sent[...].astype(F32).astype(jnp.int32).reshape(32, 128)
    to_scalars = pltpu.make_async_copy(sent_int, tables, sem.at[24])
    to_scalars.start()
    for copy in f_copies:
        copy.wait()

    slots[NONE] = jnp.zeros((8, 8, 8, 128), F32)
    for b in range(4):
        for v in range(4):
            brick = jnp.concatenate([fs[m, 4 * v + b] for m in range(4)], axis=0)
            slots[b, 2 * v : 2 * v + 2] = brick.T.astype(F32).reshape(2, 8, 8, 128)
    for side in range(2):
        for c in range(2):
            face = jnp.concatenate([hs[side, 4 * c + m] for m in range(4)], axis=0)
            first = 6 if side == 0 else 0
            slots[4 + 2 * side + c, first : first + 2] = face.T.astype(F32).reshape(2, 8, 8, 128)

    to_scalars.wait()

    def own(pair):
        def slot(w, k):
            t = tab[2 * pair + w, k]
            return jnp.where(t < 0, NONE, t)

        return slot

    def below(c, k):
        t = tables[0 + jnp.maximum(tables[9, c], 0), k]
        if k < 18:
            found = jnp.where(t == tables[9, 0], 4, jnp.where(t == tables[9, 1], 5, NONE))
            return jnp.where(t < 0, NONE, found)
        u = fl[0, 0, jnp.clip(t - 6, 0, 1)]
        return jnp.where((t < 6) | (u < 0), NONE, u)

    def above(c, k):
        t = tables[16 + jnp.maximum(tables[24, c], 0), k]
        if k >= 9:
            found = jnp.where(t == tables[24, 0], 6, jnp.where(t == tables[24, 1], 7, NONE))
            return jnp.where(t < 0, NONE, found)
        u = fl[0, 1, jnp.clip(t - 4, 0, 1)]
        return jnp.where((t < 4) | (t > 5) | (u < 0), NONE, u)

    gather_padded(slots, pad_face, 0, below, [(0, 6, 0), (0, 7, 1), (1, 0, 2)])
    gather_padded(slots, pad_face, 1, above, [(-1, 7, 0), (0, 0, 1), (0, 1, 2)])
    for pair in range(2):
        gather_padded(slots, pad, pair, own(pair), OWN_PLANES)

    for copy in w1_copies:
        copy.wait()
    values = sum(bias[m].astype(F32) for m in range(4))
    shift[...] = values[0:8] + values[8:16]
    shift_second = shift[1:2, :]
    shift_first = shift[0:1, :] + shift[pl.ds(2 + me, 1), :]

    def finish(pair, moved):
        for j in range(4):
            for zo in range(2):
                tile = silu(acc[128 * j : 128 * j + 128, 128 * zo : 128 * zo + 128] + moved)
                tile = tile.reshape(8, 2, 8, 128)
                for w in range(2):
                    b = 2 * pair + w
                    slots[b, 2 * j + zo] = jnp.where(tab[b, 13] >= 0, tile[:, w], 0.0)

    for pair in range(2):
        acc[...] = conv_pair(pad, pair, w1)
        finish(pair, shift_first)
    faces = silu(conv_face(pad_face, w1) + shift_first).reshape(2, 8, 2, 8, 128)
    for c in range(2):
        slots[4 + c, 7] = faces[0, :, c]
        slots[6 + c, 0] = faces[1, :, c]

    for pair in range(2):
        gather_padded(slots, pad, pair, own(pair), OWN_PLANES)
    for copy in w2_copies:
        copy.wait()
    for pair in range(2):
        acc[...] = conv_pair(pad, pair, w2)
        finish(pair, shift_second)
    for b in range(4):
        brick = slots[b].reshape(512, 128).astype(BF16).T
        for g in range(4):
            turned[g, b] = brick[32 * g : 32 * g + 32]
    out_copies = [
        pltpu.make_async_copy(turned.at[me ^ m], outs[m], sem.at[20 + m]) for m in range(4)
    ]
    for copy in out_copies:
        copy.start()
    for copy in out_copies:
        copy.wait()


def convolve(neighbours, face_lists, feat, sides, own_w, far_w):
    piece = jax.ShapeDtypeStruct((4, 32, 512), BF16)
    return pl.pallas_call(
        conv_kernel,
        out_shape=[piece] * 4,
        in_specs=[SMEM] * 2 + [HBM] * 12,
        out_specs=[HBM] * 4,
        scratch_shapes=[
            pltpu.VMEM((4, 16, 32, 128), BF16),
            pltpu.VMEM((2, 8, 32, 128), BF16),
            pltpu.VMEM((27, 128, 128), BF16),
            pltpu.VMEM((27, 128, 128), BF16),
            pltpu.VMEM((4, 16, 128), BF16),
            pltpu.VMEM((2, 16, 128), BF16),
            pltpu.VMEM((32, 128), jnp.int32),
            pltpu.SMEM((32, 128), jnp.int32),
            pltpu.VMEM((9, 8, 8, 8, 128), F32),
            pltpu.VMEM((2, 10, 10, 16, 384), BF16),
            pltpu.VMEM((2, 3, 10, 16, 384), BF16),
            pltpu.VMEM((512, 256), F32),
            pltpu.VMEM((8, 128), F32),
            pltpu.VMEM((4, 4, 32, 512), BF16),
            pltpu.SemaphoreType.DMA((32,)),
        ],
        compiler_params=pltpu.CompilerParams(vmem_limit_bytes=40 << 20),
        cost_estimate=pl.CostEstimate(flops=8 * 10**9, bytes_accessed=4 * 10**6, transcendentals=10**6),
        name="convolve",
    )(neighbours, face_lists, *feat, *sides, *own_w, *far_w)


def join_kernel(*refs):
    pieces, out, sem = refs[:4], refs[4], refs[5]
    me = lax.axis_index("chan")
    copies = [pltpu.make_async_copy(pieces[m], out.at[me ^ m], sem.at[m]) for m in range(4)]
    for copy in copies:
        copy.start()
    for copy in copies:
        copy.wait()


def join(pieces):
    return pl.pallas_call(
        join_kernel,
        out_shape=jax.ShapeDtypeStruct((4, 4, 32, 512), BF16),
        in_specs=[HBM] * 4,
        out_specs=HBM,
        scratch_shapes=[pltpu.SemaphoreType.DMA((4,))],
        compiler_params=pltpu.CompilerParams(vmem_limit_bytes=8 << 20),
        name="join_levels",
    )(*pieces)


def swap(value, m):
    return lax.ppermute(value, "chan", [(i, i ^ m) for i in range(4)])


def layer_of_slab():
    slab = lax.axis_index("slab")
    return (slab + slab // 8) % 2


def swap_slabs(value, step, m):
    count = lax.axis_size("slab")
    pairs = [(4 * s + g, 4 * (s ^ step) + (g ^ m)) for s in range(count) for g in range(4)]
    return lax.ppermute(value, ("slab", "chan"), pairs)


def swap_faces(value, first):
    count = lax.axis_size("slab")
    return lax.ppermute(value, "slab", [(s, (((s + first) ^ 1) - first) % count) for s in range(count)])


def shards(features, neighbours, face_lists, w_first, b_first, w_second, b_second, level_embed):
    w1, w2 = w_first.transpose(0, 2, 1), w_second.transpose(0, 2, 1)
    own, one, two, three, cross = split(features, w1, w2, b_first, b_second, level_embed)
    fetched, two, three = lax.optimization_barrier((swap(cross, 2), swap(two, 2), swap(three, 3)))
    pieces = [own, swap(one, 1), two, three]
    sides = faces(neighbours, face_lists, pieces)
    sides = [swap_faces(sides[i], i) for i in range(2)]
    far = [fetched, swap(fetched, 1), swap_slabs(fetched, 1, 0), swap_slabs(fetched, 8, 1)]
    outs = convolve(neighbours, face_lists, pieces, sides, (w1, w2), far)
    return join([outs[0]] + [swap(outs[m], m) for m in (1, 2, 3)])


def solution(mesh):
    placed = (
        P(None, "slab", "chan", None),
        P("slab", None),
        P("slab", None, None),
        P(None, None, "chan"),
        P("chan"),
        P(None, None, "chan"),
        P("chan"),
        P(None, "chan"),
    )
    return jax.shard_map(
        shards, mesh=mesh, in_specs=placed, out_specs=P(None, "slab", "chan", None), check_vma=False
    )
```

```python
import jax
import jax.numpy as jnp
from jax import lax
from jax.experimental import pallas as pl
from jax.experimental.pallas import tpu as pltpu
from jax.sharding import PartitionSpec as P

BF16, F32 = jnp.bfloat16, jnp.float32
NONE = 8
HBM = pl.BlockSpec(memory_space=pl.ANY)
VMEM = pl.BlockSpec(memory_space=pltpu.VMEM)
SMEM = pl.BlockSpec(memory_space=pltpu.SMEM)
SPAN = {-1: (7, 0, 1), 0: (0, 1, 8), 1: (0, 9, 1)}


def offset(dz, dy, dx):
    return 9 * (dz + 1) + 3 * (dy + 1) + (dx + 1)


PIECE = 17


def split_kernel(feat, near, lists, b1, b2, lev, *refs):
    pieces, tables = refs[:4], refs[4]
    me = lax.axis_index("chan")
    values = jnp.concatenate([b1[...], b2[...], lev[...], jnp.zeros((2, 32), F32)], axis=0)
    values = jnp.concatenate([values] * 4, axis=1)
    lane = lax.broadcasted_iota(jnp.int32, (8, 128), 1)
    values = jnp.where(lane // 32 == me, values, 0.0)
    high = values.astype(BF16).astype(F32)
    values = jnp.concatenate([high, values - high, jnp.zeros((16, 128), F32)], axis=0).astype(BF16)
    for m in range(4):
        for b in range(4):
            for v in range(4):
                pieces[m][4 * v + b] = feat[me ^ m, b, :, 128 * v : 128 * v + 128]
        pieces[m][16] = values
    tables[...] = jnp.zeros((8, 128), jnp.int32)
    tables[pl.ds(0, 4), pl.ds(0, 27)] = near[...]
    tables[pl.ds(4, 2), pl.ds(0, 2)] = lists[0]
    sent = tables[...].astype(F32)
    pieces[0][17] = jnp.concatenate([sent, jnp.zeros((24, 128), F32)], axis=0).astype(BF16)


def split(features, neighbours, face_lists, b1, b2, lev):
    piece = jax.ShapeDtypeStruct((PIECE, 32, 128), BF16)
    kept = jax.ShapeDtypeStruct((PIECE + 1, 32, 128), BF16)
    return pl.pallas_call(
        split_kernel,
        out_shape=[kept, piece, piece, piece, jax.ShapeDtypeStruct((8, 128), jnp.int32)],
        in_specs=[VMEM] * 6,
        out_specs=[VMEM] * 5,
        compiler_params=pltpu.CompilerParams(vmem_limit_bytes=8 << 20),
        name="split_features",
    )(features, neighbours, face_lists, b1.reshape(1, 32), b2.reshape(1, 32), lev)


def faces_kernel(tables, *refs):
    pieces, sides, sem = refs[:4], refs[4:6], refs[6]
    odd = lax.axis_index("slab") % 2
    copies = []
    for i, out in enumerate(sides):
        tier = (odd + 1 + i) % 2
        for c in range(2):
            b = jnp.maximum(tables[4 + tier, c], 0)
            for m in range(4):
                source = pieces[m].at[12 * tier + b]
                copies.append(pltpu.make_async_copy(source, out.at[4 * c + m], sem.at[8 * i + 4 * c + m]))
        copies.append(pltpu.make_async_copy(pieces[0].at[17], out.at[8], sem.at[16 + i]))
    for copy in copies:
        copy.start()
    for copy in copies:
        copy.wait()


def faces(tables, pieces):
    side = jax.ShapeDtypeStruct((9, 32, 128), BF16)
    return pl.pallas_call(
        faces_kernel,
        out_shape=[side] * 2,
        in_specs=[SMEM] + [HBM] * 4,
        out_specs=[VMEM] * 2,
        scratch_shapes=[pltpu.SemaphoreType.DMA((18,))],
        compiler_params=pltpu.CompilerParams(vmem_limit_bytes=4 << 20),
        name="pick_faces",
    )(tables, *pieces)


def silu(v):
    return v / (1.0 + jnp.exp(-v))


def gather_padded(slots, pad, lead, slot, planes):
    x = lax.broadcasted_iota(jnp.int32, (1, 8, 128), 1)
    for dz, z_from, z_to in planes:
        for dy in (-1, 0, 1):
            y_from, y_to, n = SPAN[dy]
            parts = ([], [], [])
            for w in range(2):
                mid, left, right = (
                    slots[slot(w, offset(dz, dy, dx)), z_from, y_from : y_from + n] for dx in (0, -1, 1)
                )
                parts[0].append(pltpu.roll(jnp.where(x == 7, left, mid), 1, 1))
                parts[1].append(mid)
                parts[2].append(pltpu.roll(jnp.where(x == 0, right, mid), 7, 1))
            for d in range(3):
                tile = jnp.concatenate(parts[d], axis=1).astype(BF16)
                pad[lead, z_to, y_to : y_to + n, :, 128 * d : 128 * d + 128] = tile


OWN_PLANES = [(-1, 7, 0)] + [(0, z, z + 1) for z in range(8)] + [(1, 0, 9)]


def conv_pair(pad, lead, w):
    zero = jnp.zeros((128, 128), BF16)
    total = None
    blocks = [(zin, dy) for zin in range(4) for dy in range(3)]
    for first in range(0, 12, 2):
        left, right = [], []
        for zin, dy in blocks[first : first + 2]:
            planes = [pad[lead, zin + 2 * j, dy : dy + 8].reshape(128, 384) for j in range(4)]
            left.append(jnp.concatenate(planes, axis=0))
            for dx in range(3):
                even = w[9 * zin + 3 * dy + dx] if zin < 3 else zero
                odd = w[9 * (zin - 1) + 3 * dy + dx] if zin > 0 else zero
                right.append(jnp.concatenate([even, odd], axis=1))
        part = jnp.dot(
            jnp.concatenate(left, axis=1), jnp.concatenate(right, axis=0), preferred_element_type=F32
        )
        total = part if total is None else total + part
    return total


def conv_face(pad, w):
    total = None
    blocks = [(dz, dy) for dz in range(3) for dy in range(3)]
    for group in (blocks[0:2], blocks[2:4], blocks[4:6], blocks[6:9]):
        left, right = [], []
        for dz, dy in group:
            sides = [pad[side, dz, dy : dy + 8].reshape(128, 384) for side in range(2)]
            left.append(jnp.concatenate(sides, axis=0))
            right += [w[9 * dz + 3 * dy + dx] for dx in range(3)]
        part = jnp.dot(
            jnp.concatenate(left, axis=1), jnp.concatenate(right, axis=0), preferred_element_type=F32
        )
        total = part if total is None else total + part
    return total


def load_shards(sources, weights, order, sem):
    return [
        pltpu.make_async_copy(
            source, weights.at[:, pl.ds(pl.multiple_of(32 * order[m], 32), 32), :], sem.at[m]
        )
        for m, source in enumerate(sources)
    ]


def finish(acc, moved, tab, pair, slots):
    for j in range(4):
        for zo in range(2):
            tile = silu(acc[pair, 128 * j : 128 * j + 128, 128 * zo : 128 * zo + 128] + moved)
            tile = tile.reshape(8, 2, 8, 128)
            for w in range(2):
                b = 2 * pair + w
                slots[b, 2 * j + zo] = jnp.where(tab[b, 13] >= 0, tile[:, w], 0.0)


def first_kernel(tab, *refs):
    feat, sides, shards = refs[0:4], refs[4:6], refs[6:10]
    pad_out, shift = refs[10:12]
    fs, hs, w1, bias, sent, sent_int, tables, slots, pad, pad_face, acc, sem = refs[12:]
    me = lax.axis_index("chan")

    f_copies, t_copies = [], []
    for i in range(2):
        side = (lax.axis_index("slab") + 1 + i) % 2
        t_copies.append(pltpu.make_async_copy(sides[i].at[8, pl.ds(0, 16)], sent.at[side], sem.at[i]))
        f_copies.append(pltpu.make_async_copy(sides[i].at[pl.ds(0, 8)], hs.at[side], sem.at[2 + i]))
    for m in range(4):
        f_copies.append(pltpu.make_async_copy(feat[m].at[pl.ds(0, 16)], fs.at[m], sem.at[4 + m]))
        f_copies.append(pltpu.make_async_copy(feat[m].at[16, pl.ds(0, 16)], bias.at[m], sem.at[8 + m]))
    w_copies = [
        pltpu.make_async_copy(shards[m], w1.at[:, pl.ds(32 * m, 32), :], sem.at[12 + m]) for m in range(4)
    ]
    for copy in t_copies + f_copies + w_copies:
        copy.start()
    for copy in t_copies:
        copy.wait()
    sent_int[...] = sent[...].astype(F32).astype(jnp.int32).reshape(32, 128)
    to_scalars = pltpu.make_async_copy(sent_int, tables, sem.at[16])
    to_scalars.start()
    for copy in f_copies:
        copy.wait()

    slots[NONE] = jnp.zeros((8, 8, 8, 128), F32)
    for b in range(4):
        for v in range(4):
            brick = jnp.concatenate([fs[m, 4 * v + b] for m in range(4)], axis=0)
            slots[b, 2 * v : 2 * v + 2] = brick.T.astype(F32).reshape(2, 8, 8, 128)
    for side in range(2):
        for c in range(2):
            face = jnp.concatenate([hs[side, 4 * c + m] for m in range(4)], axis=0)
            first = 6 if side == 0 else 0
            slots[4 + 2 * side + c, first : first + 2] = face.T.astype(F32).reshape(2, 8, 8, 128)

    to_scalars.wait()

    def own(pair):
        def slot(w, k):
            t = tab[2 * pair + w, k]
            return jnp.where(t < 0, NONE, t)

        return slot

    def below(c, k):
        t = tables[0 + jnp.maximum(tables[5, c], 0), k]
        if k < 18:
            found = jnp.where(t == tables[5, 0], 4, jnp.where(t == tables[5, 1], 5, NONE))
            return jnp.where(t < 0, NONE, found)
        u = tab[4, jnp.clip(t - 6, 0, 1)]
        return jnp.where((t < 6) | (u < 0), NONE, u)

    def above(c, k):
        t = tables[16 + jnp.maximum(tables[20, c], 0), k]
        if k >= 9:
            found = jnp.where(t == tables[20, 0], 6, jnp.where(t == tables[20, 1], 7, NONE))
            return jnp.where(t < 0, NONE, found)
        u = tab[5, jnp.clip(t - 4, 0, 1)]
        return jnp.where((t < 4) | (t > 5) | (u < 0), NONE, u)

    gather_padded(slots, pad_face, 0, below, [(0, 6, 0), (0, 7, 1), (1, 0, 2)])
    gather_padded(slots, pad_face, 1, above, [(-1, 7, 0), (0, 0, 1), (0, 1, 2)])
    for pair in range(2):
        gather_padded(slots, pad, pair, own(pair), OWN_PLANES)

    values = sum(bias[m].astype(F32) for m in range(4))
    shift[...] = values[0:8] + values[8:16]
    moved = shift[0:1, :] + shift[pl.ds(2 + me, 1), :]
    for copy in w_copies:
        copy.wait()

    for pair in range(2):
        acc[pair] = conv_pair(pad, pair, w1)
        finish(acc, moved, tab, pair, slots)
    sides_out = silu(conv_face(pad_face, w1) + moved).reshape(2, 8, 2, 8, 128)
    for c in range(2):
        slots[4 + c, 7] = sides_out[0, :, c]
        slots[6 + c, 0] = sides_out[1, :, c]
    for pair in range(2):
        gather_padded(slots, pad_out, pair, own(pair), OWN_PLANES)


def convolve_first(tables, feat, sides, shards):
    return pl.pallas_call(
        first_kernel,
        out_shape=[jax.ShapeDtypeStruct((2, 10, 10, 16, 384), BF16), jax.ShapeDtypeStruct((8, 128), F32)],
        in_specs=[SMEM] + [HBM] * 10,
        out_specs=[VMEM] * 2,
        scratch_shapes=[
            pltpu.VMEM((4, 16, 32, 128), BF16),
            pltpu.VMEM((2, 8, 32, 128), BF16),
            pltpu.VMEM((27, 128, 128), BF16),
            pltpu.VMEM((4, 16, 128), BF16),
            pltpu.VMEM((2, 16, 128), BF16),
            pltpu.VMEM((32, 128), jnp.int32),
            pltpu.SMEM((32, 128), jnp.int32),
            pltpu.VMEM((9, 8, 8, 8, 128), F32),
            pltpu.VMEM((2, 10, 10, 16, 384), BF16),
            pltpu.VMEM((2, 3, 10, 16, 384), BF16),
            pltpu.VMEM((2, 512, 256), F32),
            pltpu.SemaphoreType.DMA((17,)),
        ],
        compiler_params=pltpu.CompilerParams(vmem_limit_bytes=24 << 20),
        cost_estimate=pl.CostEstimate(flops=5 * 10**9, bytes_accessed=4 * 10**6, transcendentals=10**6),
        name="convolve_first",
    )(tables, *feat, *sides, *shards)


def second_kernel(tab, pad, shift, *refs):
    shards, outs = refs[0:4], refs[4:8]
    w2, slots, acc, turned, sem = refs[8:]
    me = lax.axis_index("chan")
    w_copies = load_shards(shards, w2, [me ^ m for m in range(4)], sem)
    for copy in w_copies:
        copy.start()
    for copy in w_copies:
        copy.wait()
    for pair in range(2):
        acc[pair] = conv_pair(pad, pair, w2)
        finish(acc, shift[1:2, :], tab, pair, slots)
    for b in range(4):
        brick = slots[b].reshape(512, 128).astype(BF16).T
        for g in range(4):
            turned[g, b] = brick[32 * g : 32 * g + 32]
    for m in range(4):
        outs[m][...] = turned[me ^ m]


def convolve_second(tables, pad, shift, shards):
    piece = jax.ShapeDtypeStruct((4, 32, 512), BF16)
    return pl.pallas_call(
        second_kernel,
        out_shape=[piece] * 4,
        in_specs=[SMEM, VMEM, VMEM] + [HBM] * 4,
        out_specs=[VMEM] * 4,
        scratch_shapes=[
            pltpu.VMEM((27, 128, 128), BF16),
            pltpu.VMEM((4, 8, 8, 8, 128), F32),
            pltpu.VMEM((2, 512, 256), F32),
            pltpu.VMEM((4, 4, 32, 512), BF16),
            pltpu.SemaphoreType.DMA((4,)),
        ],
        compiler_params=pltpu.CompilerParams(vmem_limit_bytes=24 << 20),
        cost_estimate=pl.CostEstimate(flops=4 * 10**9, bytes_accessed=4 * 10**6, transcendentals=10**6),
        name="convolve_second",
    )(tables, pad, shift, *shards)


def join_kernel(*refs):
    pieces, out, sem = refs[:4], refs[4], refs[5]
    me = lax.axis_index("chan")
    copies = [pltpu.make_async_copy(pieces[m], out.at[me ^ m], sem.at[m]) for m in range(4)]
    for copy in copies:
        copy.start()
    for copy in copies:
        copy.wait()


def join(pieces):
    return pl.pallas_call(
        join_kernel,
        out_shape=jax.ShapeDtypeStruct((4, 4, 32, 512), BF16),
        in_specs=[HBM] * 4,
        out_specs=HBM,
        scratch_shapes=[pltpu.SemaphoreType.DMA((4,))],
        compiler_params=pltpu.CompilerParams(vmem_limit_bytes=8 << 20),
        name="join_levels",
    )(*pieces)


def swap(value, m):
    return lax.ppermute(value, "chan", [(i, i ^ m) for i in range(4)])


def swap_faces(value, first):
    count = lax.axis_size("slab")
    return lax.ppermute(value, "slab", [(s, (((s + first) ^ 1) - first) % count) for s in range(count)])


def shards(features, neighbours, face_lists, w_first, b_first, w_second, b_second, level_embed):
    w1, w2 = w_first.transpose(0, 2, 1), w_second.transpose(0, 2, 1)
    far = swap(w1, 2)
    own, one, two, three, tables = split(
        features, neighbours, face_lists, b_first, b_second, level_embed
    )
    far, two, three, later = lax.optimization_barrier((far, swap(two, 2), swap(three, 3), w2))
    pieces = [own, swap(one, 1), two, three]
    first = [w1, swap(w1, 1), far, swap(far, 1)]
    sides = faces(tables, pieces)
    sides = [swap_faces(sides[i], i) for i in range(2)]
    second = [w2] + [swap(later, m) for m in (1, 2, 3)]
    pad, shift = convolve_first(tables, pieces, sides, first)
    outs = convolve_second(tables, pad, shift, second)
    return join([outs[0]] + [swap(outs[m], m) for m in (1, 2, 3)])


def solution(mesh):
    placed = (
        P(None, "slab", "chan", None),
        P("slab", None),
        P("slab", None, None),
        P(None, None, "chan"),
        P("chan"),
        P(None, None, "chan"),
        P("chan"),
        P(None, "chan"),
    )
    return jax.shard_map(
        shards, mesh=mesh, in_specs=placed, out_specs=P(None, "slab", "chan", None), check_vma=False
    )
```

```python
import jax
import jax.numpy as jnp
from jax import lax
from jax.experimental import pallas as pl
from jax.experimental.pallas import tpu as pltpu
from jax.sharding import PartitionSpec as P

BF16, F32 = jnp.bfloat16, jnp.float32
NONE = 8
HBM = pl.BlockSpec(memory_space=pl.ANY)
VMEM = pl.BlockSpec(memory_space=pltpu.VMEM)
SMEM = pl.BlockSpec(memory_space=pltpu.SMEM)
SPAN = {-1: (7, 0, 1), 0: (0, 1, 8), 1: (0, 9, 1)}


def offset(dz, dy, dx):
    return 9 * (dz + 1) + 3 * (dy + 1) + (dx + 1)


PIECE = 17


def split_kernel(feat, near, lists, b1, b2, lev, *refs):
    pieces, tables = refs[:4], refs[4]
    me = lax.axis_index("chan")
    values = jnp.concatenate([b1[...], b2[...], lev[...], jnp.zeros((2, 32), F32)], axis=0)
    values = jnp.concatenate([values] * 4, axis=1)
    lane = lax.broadcasted_iota(jnp.int32, (8, 128), 1)
    values = jnp.where(lane // 32 == me, values, 0.0)
    high = values.astype(BF16).astype(F32)
    values = jnp.concatenate([high, values - high, jnp.zeros((16, 128), F32)], axis=0).astype(BF16)
    for m in range(4):
        for b in range(4):
            for v in range(4):
                pieces[m][4 * v + b] = feat[me ^ m, b, :, 128 * v : 128 * v + 128]
        pieces[m][16] = values
    tables[...] = jnp.zeros((8, 128), jnp.int32)
    tables[pl.ds(0, 4), pl.ds(0, 27)] = near[...]
    tables[pl.ds(4, 2), pl.ds(0, 2)] = lists[0]
    sent = tables[...].astype(F32)
    pieces[0][17] = jnp.concatenate([sent, jnp.zeros((24, 128), F32)], axis=0).astype(BF16)


def split(features, neighbours, face_lists, b1, b2, lev):
    piece = jax.ShapeDtypeStruct((PIECE, 32, 128), BF16)
    kept = jax.ShapeDtypeStruct((PIECE + 1, 32, 128), BF16)
    return pl.pallas_call(
        split_kernel,
        out_shape=[kept, piece, piece, piece, jax.ShapeDtypeStruct((8, 128), jnp.int32)],
        in_specs=[VMEM] * 6,
        out_specs=[VMEM] * 5,
        compiler_params=pltpu.CompilerParams(vmem_limit_bytes=8 << 20),
        name="split_features",
    )(features, neighbours, face_lists, b1.reshape(1, 32), b2.reshape(1, 32), lev)


def faces_kernel(tables, *refs):
    pieces, sides, sem = refs[:4], refs[4:6], refs[6]
    odd = lax.axis_index("slab") % 2
    copies = []
    for i, out in enumerate(sides):
        tier = (odd + 1 + i) % 2
        for c in range(2):
            b = jnp.maximum(tables[4 + tier, c], 0)
            for m in range(4):
                source = pieces[m].at[12 * tier + b]
                copies.append(pltpu.make_async_copy(source, out.at[4 * c + m], sem.at[8 * i + 4 * c + m]))
        copies.append(pltpu.make_async_copy(pieces[0].at[17], out.at[8], sem.at[16 + i]))
    for copy in copies:
        copy.start()
    for copy in copies:
        copy.wait()


def faces(tables, pieces):
    side = jax.ShapeDtypeStruct((9, 32, 128), BF16)
    return pl.pallas_call(
        faces_kernel,
        out_shape=[side] * 2,
        in_specs=[SMEM] + [HBM] * 4,
        out_specs=[VMEM] * 2,
        scratch_shapes=[pltpu.SemaphoreType.DMA((18,))],
        compiler_params=pltpu.CompilerParams(vmem_limit_bytes=4 << 20),
        name="pick_faces",
    )(tables, *pieces)


def silu(v):
    return v / (1.0 + jnp.exp(-v))


def gather_padded(slots, pad, lead, slot, planes):
    x = lax.broadcasted_iota(jnp.int32, (1, 8, 128), 1)
    for dz, z_from, z_to in planes:
        for dy in (-1, 0, 1):
            y_from, y_to, n = SPAN[dy]
            parts = ([], [], [])
            for w in range(2):
                mid, left, right = (
                    slots[slot(w, offset(dz, dy, dx)), z_from, y_from : y_from + n] for dx in (0, -1, 1)
                )
                parts[0].append(pltpu.roll(jnp.where(x == 7, left, mid), 1, 1))
                parts[1].append(mid)
                parts[2].append(pltpu.roll(jnp.where(x == 0, right, mid), 7, 1))
            for d in range(3):
                tile = jnp.concatenate(parts[d], axis=1).astype(BF16)
                pad[lead, z_to, y_to : y_to + n, :, 128 * d : 128 * d + 128] = tile


OWN_PLANES = [(-1, 7, 0)] + [(0, z, z + 1) for z in range(8)] + [(1, 0, 9)]


def conv_pair(pad, lead, w):
    zero = jnp.zeros((128, 128), BF16)
    total = None
    blocks = [(zin, dy) for zin in range(4) for dy in range(3)]
    for first in range(0, 12, 2):
        left, right = [], []
        for zin, dy in blocks[first : first + 2]:
            planes = [pad[lead, zin + 2 * j, dy : dy + 8].reshape(128, 384) for j in range(4)]
            left.append(jnp.concatenate(planes, axis=0))
            for dx in range(3):
                even = w[9 * zin + 3 * dy + dx] if zin < 3 else zero
                odd = w[9 * (zin - 1) + 3 * dy + dx] if zin > 0 else zero
                right.append(jnp.concatenate([even, odd], axis=1))
        part = jnp.dot(
            jnp.concatenate(left, axis=1), jnp.concatenate(right, axis=0), preferred_element_type=F32
        )
        total = part if total is None else total + part
    return total


def conv_face(pad, w):
    total = None
    blocks = [(dz, dy) for dz in range(3) for dy in range(3)]
    for group in (blocks[0:2], blocks[2:4], blocks[4:6], blocks[6:9]):
        left, right = [], []
        for dz, dy in group:
            sides = [pad[side, dz, dy : dy + 8].reshape(128, 384) for side in range(2)]
            left.append(jnp.concatenate(sides, axis=0))
            right += [w[9 * dz + 3 * dy + dx] for dx in range(3)]
        part = jnp.dot(
            jnp.concatenate(left, axis=1), jnp.concatenate(right, axis=0), preferred_element_type=F32
        )
        total = part if total is None else total + part
    return total


def load_shards(sources, weights, order, sem):
    return [
        pltpu.make_async_copy(
            source, weights.at[:, pl.ds(pl.multiple_of(32 * order[m], 32), 32), :], sem.at[m]
        )
        for m, source in enumerate(sources)
    ]


def finish(acc, moved, tab, pair, slots):
    for j in range(4):
        for zo in range(2):
            tile = silu(acc[pair, 128 * j : 128 * j + 128, 128 * zo : 128 * zo + 128] + moved)
            tile = tile.reshape(8, 2, 8, 128)
            for w in range(2):
                b = 2 * pair + w
                slots[b, 2 * j + zo] = jnp.where(tab[b, 13] >= 0, tile[:, w], 0.0)


def first_kernel(tab, *refs):
    feat, sides, shards = refs[0:4], refs[4:6], refs[6:10]
    pad_out, shift = refs[10:12]
    fs, hs, w1, bias, sent, sent_int, tables, slots, pad, pad_face, acc, sem = refs[12:]
    me = lax.axis_index("chan")

    f_copies, t_copies = [], []
    for i in range(2):
        side = (lax.axis_index("slab") + 1 + i) % 2
        t_copies.append(pltpu.make_async_copy(sides[i].at[8, pl.ds(0, 16)], sent.at[side], sem.at[i]))
        f_copies.append(pltpu.make_async_copy(sides[i].at[pl.ds(0, 8)], hs.at[side], sem.at[2 + i]))
    for m in range(4):
        f_copies.append(pltpu.make_async_copy(feat[m].at[pl.ds(0, 16)], fs.at[m], sem.at[4 + m]))
        f_copies.append(pltpu.make_async_copy(feat[m].at[16, pl.ds(0, 16)], bias.at[m], sem.at[8 + m]))
    w_copies = [
        pltpu.make_async_copy(shards[m], w1.at[:, pl.ds(32 * m, 32), :], sem.at[12 + m]) for m in range(4)
    ]
    for copy in t_copies + f_copies + w_copies:
        copy.start()
    for copy in t_copies:
        copy.wait()
    sent_int[...] = sent[...].astype(F32).astype(jnp.int32).reshape(32, 128)
    to_scalars = pltpu.make_async_copy(sent_int, tables, sem.at[16])
    to_scalars.start()
    for copy in f_copies:
        copy.wait()

    slots[NONE] = jnp.zeros((8, 8, 8, 128), F32)
    for b in range(4):
        for v in range(4):
            brick = jnp.concatenate([fs[m, 4 * v + b] for m in range(4)], axis=0)
            slots[b, 2 * v : 2 * v + 2] = brick.T.astype(F32).reshape(2, 8, 8, 128)
    for side in range(2):
        for c in range(2):
            face = jnp.concatenate([hs[side, 4 * c + m] for m in range(4)], axis=0)
            first = 6 if side == 0 else 0
            slots[4 + 2 * side + c, first : first + 2] = face.T.astype(F32).reshape(2, 8, 8, 128)

    to_scalars.wait()

    def own(pair):
        def slot(w, k):
            t = tab[2 * pair + w, k]
            return jnp.where(t < 0, NONE, t)

        return slot

    def below(c, k):
        t = tables[0 + jnp.maximum(tables[5, c], 0), k]
        if k < 18:
            found = jnp.where(t == tables[5, 0], 4, jnp.where(t == tables[5, 1], 5, NONE))
            return jnp.where(t < 0, NONE, found)
        u = tab[4, jnp.clip(t - 6, 0, 1)]
        return jnp.where((t < 6) | (u < 0), NONE, u)

    def above(c, k):
        t = tables[16 + jnp.maximum(tables[20, c], 0), k]
        if k >= 9:
            found = jnp.where(t == tables[20, 0], 6, jnp.where(t == tables[20, 1], 7, NONE))
            return jnp.where(t < 0, NONE, found)
        u = tab[5, jnp.clip(t - 4, 0, 1)]
        return jnp.where((t < 4) | (t > 5) | (u < 0), NONE, u)

    gather_padded(slots, pad_face, 0, below, [(0, 6, 0), (0, 7, 1), (1, 0, 2)])
    gather_padded(slots, pad_face, 1, above, [(-1, 7, 0), (0, 0, 1), (0, 1, 2)])
    for pair in range(2):
        gather_padded(slots, pad, pair, own(pair), OWN_PLANES)

    values = sum(bias[m].astype(F32) for m in range(4))
    shift[...] = values[0:8] + values[8:16]
    moved = shift[0:1, :] + shift[pl.ds(2 + me, 1), :]
    for copy in w_copies:
        copy.wait()

    for pair in range(2):
        acc[pair] = conv_pair(pad, pair, w1)
        finish(acc, moved, tab, pair, slots)
    sides_out = silu(conv_face(pad_face, w1) + moved).reshape(2, 8, 2, 8, 128)
    for c in range(2):
        slots[4 + c, 7] = sides_out[0, :, c]
        slots[6 + c, 0] = sides_out[1, :, c]
    for pair in range(2):
        gather_padded(slots, pad_out, pair, own(pair), OWN_PLANES)


def convolve_first(tables, feat, sides, shards):
    return pl.pallas_call(
        first_kernel,
        out_shape=[jax.ShapeDtypeStruct((2, 10, 10, 16, 384), BF16), jax.ShapeDtypeStruct((8, 128), F32)],
        in_specs=[SMEM] + [HBM] * 10,
        out_specs=[VMEM] * 2,
        scratch_shapes=[
            pltpu.VMEM((4, 16, 32, 128), BF16),
            pltpu.VMEM((2, 8, 32, 128), BF16),
            pltpu.VMEM((27, 128, 128), BF16),
            pltpu.VMEM((4, 16, 128), BF16),
            pltpu.VMEM((2, 16, 128), BF16),
            pltpu.VMEM((32, 128), jnp.int32),
            pltpu.SMEM((32, 128), jnp.int32),
            pltpu.VMEM((9, 8, 8, 8, 128), F32),
            pltpu.VMEM((2, 10, 10, 16, 384), BF16),
            pltpu.VMEM((2, 3, 10, 16, 384), BF16),
            pltpu.VMEM((2, 512, 256), F32),
            pltpu.SemaphoreType.DMA((17,)),
        ],
        compiler_params=pltpu.CompilerParams(vmem_limit_bytes=24 << 20),
        cost_estimate=pl.CostEstimate(flops=10**6, bytes_accessed=10**4, transcendentals=0),
        name="convolve_first",
    )(tables, *feat, *sides, *shards)


def second_kernel(tab, pad, shift, *refs):
    shards, outs = refs[0:4], refs[4:8]
    w2, slots, acc, turned, sem = refs[8:]
    me = lax.axis_index("chan")
    w_copies = load_shards(shards, w2, [me ^ m for m in range(4)], sem)
    for copy in w_copies:
        copy.start()
    for copy in w_copies:
        copy.wait()
    for pair in range(2):
        acc[pair] = conv_pair(pad, pair, w2)
        finish(acc, shift[1:2, :], tab, pair, slots)
    for b in range(4):
        brick = slots[b].reshape(512, 128).astype(BF16).T
        for g in range(4):
            turned[g, b] = brick[32 * g : 32 * g + 32]
    for m in range(4):
        outs[m][...] = turned[me ^ m]


def convolve_second(tables, pad, shift, shards):
    piece = jax.ShapeDtypeStruct((4, 32, 512), BF16)
    return pl.pallas_call(
        second_kernel,
        out_shape=[piece] * 4,
        in_specs=[SMEM, VMEM, VMEM] + [HBM] * 4,
        out_specs=[VMEM] * 4,
        scratch_shapes=[
            pltpu.VMEM((27, 128, 128), BF16),
            pltpu.VMEM((4, 8, 8, 8, 128), F32),
            pltpu.VMEM((2, 512, 256), F32),
            pltpu.VMEM((4, 4, 32, 512), BF16),
            pltpu.SemaphoreType.DMA((4,)),
        ],
        compiler_params=pltpu.CompilerParams(vmem_limit_bytes=24 << 20),
        cost_estimate=pl.CostEstimate(flops=4 * 10**9, bytes_accessed=4 * 10**6, transcendentals=10**6),
        name="convolve_second",
    )(tables, pad, shift, *shards)


def join_kernel(*refs):
    pieces, out, sem = refs[:4], refs[4], refs[5]
    me = lax.axis_index("chan")
    copies = [pltpu.make_async_copy(pieces[m], out.at[me ^ m], sem.at[m]) for m in range(4)]
    for copy in copies:
        copy.start()
    for copy in copies:
        copy.wait()


def join(pieces):
    return pl.pallas_call(
        join_kernel,
        out_shape=jax.ShapeDtypeStruct((4, 4, 32, 512), BF16),
        in_specs=[HBM] * 4,
        out_specs=HBM,
        scratch_shapes=[pltpu.SemaphoreType.DMA((4,))],
        compiler_params=pltpu.CompilerParams(vmem_limit_bytes=8 << 20),
        name="join_levels",
    )(*pieces)


def swap(value, m):
    return lax.ppermute(value, "chan", [(i, i ^ m) for i in range(4)])


def swap_faces(value, first):
    count = lax.axis_size("slab")
    return lax.ppermute(value, "slab", [(s, (((s + first) ^ 1) - first) % count) for s in range(count)])


def shards(features, neighbours, face_lists, w_first, b_first, w_second, b_second, level_embed):
    w1, w2 = w_first.transpose(0, 2, 1), w_second.transpose(0, 2, 1)
    far = swap(w1, 2)
    own, one, two, three, tables = split(
        features, neighbours, face_lists, b_first, b_second, level_embed
    )
    far, one, two, three, later, near = lax.optimization_barrier(
        (far, swap(one, 1), swap(two, 2), swap(three, 3), w2, swap(w2, 1))
    )
    pieces = [own, one, two, three]
    first = [w1, swap(w1, 1), far, swap(far, 1)]
    sides = faces(tables, pieces)
    sides = [swap_faces(sides[i], i) for i in range(2)]
    second = [w2, near, swap(later, 2), swap(later, 3)]
    pad, shift = convolve_first(tables, pieces, sides, first)
    outs = convolve_second(tables, pad, shift, second)
    return join([outs[0]] + [swap(outs[m], m) for m in (1, 2, 3)])


def solution(mesh):
    placed = (
        P(None, "slab", "chan", None),
        P("slab", None),
        P("slab", None, None),
        P(None, None, "chan"),
        P("chan"),
        P(None, None, "chan"),
        P("chan"),
        P(None, "chan"),
    )
    return jax.shard_map(
        shards, mesh=mesh, in_specs=placed, out_specs=P(None, "slab", "chan", None), check_vma=False
    )
```

```python
import jax
import jax.numpy as jnp
from jax import lax
from jax.experimental import pallas as pl
from jax.experimental.pallas import tpu as pltpu
from jax.sharding import PartitionSpec as P

BF16, F32 = jnp.bfloat16, jnp.float32
NONE = 8
HBM = pl.BlockSpec(memory_space=pl.ANY)
VMEM = pl.BlockSpec(memory_space=pltpu.VMEM)
SMEM = pl.BlockSpec(memory_space=pltpu.SMEM)
SPAN = {-1: (7, 0, 1), 0: (0, 1, 8), 1: (0, 9, 1)}


def offset(dz, dy, dx):
    return 9 * (dz + 1) + 3 * (dy + 1) + (dx + 1)


PIECE = 17


def split_kernel(feat, near, lists, b1, b2, lev, *refs):
    pieces, tables = refs[:4], refs[4]
    me = lax.axis_index("chan")
    values = jnp.concatenate([b1[...], b2[...], lev[...], jnp.zeros((2, 32), F32)], axis=0)
    values = jnp.concatenate([values] * 4, axis=1)
    lane = lax.broadcasted_iota(jnp.int32, (8, 128), 1)
    values = jnp.where(lane // 32 == me, values, 0.0)
    high = values.astype(BF16).astype(F32)
    values = jnp.concatenate([high, values - high, jnp.zeros((16, 128), F32)], axis=0).astype(BF16)
    for m in range(4):
        for b in range(4):
            for v in range(4):
                pieces[m][4 * v + b] = feat[me ^ m, b, :, 128 * v : 128 * v + 128]
        pieces[m][16] = values
    tables[...] = jnp.zeros((8, 128), jnp.int32)
    tables[pl.ds(0, 4), pl.ds(0, 27)] = near[...]
    tables[pl.ds(4, 2), pl.ds(0, 2)] = lists[0]
    sent = tables[...].astype(F32)
    pieces[0][17] = jnp.concatenate([sent, jnp.zeros((24, 128), F32)], axis=0).astype(BF16)


def split(features, neighbours, face_lists, b1, b2, lev):
    piece = jax.ShapeDtypeStruct((PIECE, 32, 128), BF16)
    kept = jax.ShapeDtypeStruct((PIECE + 1, 32, 128), BF16)
    return pl.pallas_call(
        split_kernel,
        out_shape=[kept, piece, piece, piece, jax.ShapeDtypeStruct((8, 128), jnp.int32)],
        in_specs=[VMEM] * 6,
        out_specs=[VMEM] * 5,
        compiler_params=pltpu.CompilerParams(vmem_limit_bytes=8 << 20),
        name="split_features",
    )(features, neighbours, face_lists, b1.reshape(1, 32), b2.reshape(1, 32), lev)


def faces_kernel(tables, *refs):
    pieces, sides, sem = refs[:4], refs[4:6], refs[6]
    odd = lax.axis_index("slab") % 2
    copies = []
    for i, out in enumerate(sides):
        tier = (odd + 1 + i) % 2
        for c in range(2):
            b = jnp.maximum(tables[4 + tier, c], 0)
            for m in range(4):
                source = pieces[m].at[12 * tier + b]
                copies.append(pltpu.make_async_copy(source, out.at[4 * c + m], sem.at[8 * i + 4 * c + m]))
        copies.append(pltpu.make_async_copy(pieces[0].at[17], out.at[8], sem.at[16 + i]))
    for copy in copies:
        copy.start()
    for copy in copies:
        copy.wait()


def faces(tables, pieces):
    side = jax.ShapeDtypeStruct((9, 32, 128), BF16)
    return pl.pallas_call(
        faces_kernel,
        out_shape=[side] * 2,
        in_specs=[SMEM] + [HBM] * 4,
        out_specs=[VMEM] * 2,
        scratch_shapes=[pltpu.SemaphoreType.DMA((18,))],
        compiler_params=pltpu.CompilerParams(vmem_limit_bytes=4 << 20),
        name="pick_faces",
    )(tables, *pieces)


def silu(v):
    return v / (1.0 + jnp.exp(-v))


def gather_padded(slots, pad, lead, slot, planes):
    x = lax.broadcasted_iota(jnp.int32, (1, 8, 128), 1)
    for dz, z_from, z_to in planes:
        for dy in (-1, 0, 1):
            y_from, y_to, n = SPAN[dy]
            parts = ([], [], [])
            for w in range(2):
                mid, left, right = (
                    slots[slot(w, offset(dz, dy, dx)), z_from, y_from : y_from + n] for dx in (0, -1, 1)
                )
                parts[0].append(pltpu.roll(jnp.where(x == 7, left, mid), 1, 1))
                parts[1].append(mid)
                parts[2].append(pltpu.roll(jnp.where(x == 0, right, mid), 7, 1))
            for d in range(3):
                tile = jnp.concatenate(parts[d], axis=1).astype(BF16)
                pad[lead, z_to, y_to : y_to + n, :, 128 * d : 128 * d + 128] = tile


OWN_PLANES = [(-1, 7, 0)] + [(0, z, z + 1) for z in range(8)] + [(1, 0, 9)]


def conv_pair(pad, lead, w):
    zero = jnp.zeros((128, 128), BF16)
    total = None
    blocks = [(zin, dy) for zin in range(4) for dy in range(3)]
    for first in range(0, 12, 2):
        left, right = [], []
        for zin, dy in blocks[first : first + 2]:
            planes = [pad[lead, zin + 2 * j, dy : dy + 8].reshape(128, 384) for j in range(4)]
            left.append(jnp.concatenate(planes, axis=0))
            for dx in range(3):
                even = w[9 * zin + 3 * dy + dx] if zin < 3 else zero
                odd = w[9 * (zin - 1) + 3 * dy + dx] if zin > 0 else zero
                right.append(jnp.concatenate([even, odd], axis=1))
        part = jnp.dot(
            jnp.concatenate(left, axis=1), jnp.concatenate(right, axis=0), preferred_element_type=F32
        )
        total = part if total is None else total + part
    return total


def conv_face(pad, w):
    total = None
    blocks = [(dz, dy) for dz in range(3) for dy in range(3)]
    for group in (blocks[0:2], blocks[2:4], blocks[4:6], blocks[6:9]):
        left, right = [], []
        for dz, dy in group:
            sides = [pad[side, dz, dy : dy + 8].reshape(128, 384) for side in range(2)]
            left.append(jnp.concatenate(sides, axis=0))
            right += [w[9 * dz + 3 * dy + dx] for dx in range(3)]
        part = jnp.dot(
            jnp.concatenate(left, axis=1), jnp.concatenate(right, axis=0), preferred_element_type=F32
        )
        total = part if total is None else total + part
    return total


def load_shards(sources, weights, order, sem):
    return [
        pltpu.make_async_copy(
            source, weights.at[:, pl.ds(pl.multiple_of(32 * order[m], 32), 32), :], sem.at[m]
        )
        for m, source in enumerate(sources)
    ]


def finish(acc, moved, tab, pair, slots):
    for j in range(4):
        for zo in range(2):
            tile = silu(acc[pair, 128 * j : 128 * j + 128, 128 * zo : 128 * zo + 128] + moved)
            tile = tile.reshape(8, 2, 8, 128)
            for w in range(2):
                b = 2 * pair + w
                slots[b, 2 * j + zo] = jnp.where(tab[b, 13] >= 0, tile[:, w], 0.0)


def first_kernel(tab, *refs):
    feat, sides, shards = refs[0:4], refs[4:6], refs[6:10]
    pad_out, shift = refs[10:12]
    fs, hs, w1, bias, sent, sent_int, tables, slots, pad, pad_face, acc, sem = refs[12:]
    me = lax.axis_index("chan")

    f_copies, t_copies = [], []
    for i in range(2):
        side = (lax.axis_index("slab") + 1 + i) % 2
        t_copies.append(pltpu.make_async_copy(sides[i].at[8, pl.ds(0, 16)], sent.at[side], sem.at[i]))
        f_copies.append(pltpu.make_async_copy(sides[i].at[pl.ds(0, 8)], hs.at[side], sem.at[2 + i]))
    for m in range(4):
        f_copies.append(pltpu.make_async_copy(feat[m].at[pl.ds(0, 16)], fs.at[m], sem.at[4 + m]))
        f_copies.append(pltpu.make_async_copy(feat[m].at[16, pl.ds(0, 16)], bias.at[m], sem.at[8 + m]))
    w_copies = [
        pltpu.make_async_copy(shards[m], w1.at[:, pl.ds(32 * m, 32), :], sem.at[12 + m]) for m in range(4)
    ]
    for copy in t_copies + f_copies + w_copies:
        copy.start()
    for copy in t_copies:
        copy.wait()
    sent_int[...] = sent[...].astype(F32).astype(jnp.int32).reshape(32, 128)
    to_scalars = pltpu.make_async_copy(sent_int, tables, sem.at[16])
    to_scalars.start()
    for copy in f_copies:
        copy.wait()

    slots[NONE] = jnp.zeros((8, 8, 8, 128), F32)
    for b in range(4):
        for v in range(4):
            brick = jnp.concatenate([fs[m, 4 * v + b] for m in range(4)], axis=0)
            slots[b, 2 * v : 2 * v + 2] = brick.T.astype(F32).reshape(2, 8, 8, 128)
    for side in range(2):
        for c in range(2):
            face = jnp.concatenate([hs[side, 4 * c + m] for m in range(4)], axis=0)
            first = 6 if side == 0 else 0
            slots[4 + 2 * side + c, first : first + 2] = face.T.astype(F32).reshape(2, 8, 8, 128)

    to_scalars.wait()

    def own(pair):
        def slot(w, k):
            t = tab[2 * pair + w, k]
            return jnp.where(t < 0, NONE, t)

        return slot

    def below(c, k):
        t = tables[0 + jnp.maximum(tables[5, c], 0), k]
        if k < 18:
            found = jnp.where(t == tables[5, 0], 4, jnp.where(t == tables[5, 1], 5, NONE))
            return jnp.where(t < 0, NONE, found)
        u = tab[4, jnp.clip(t - 6, 0, 1)]
        return jnp.where((t < 6) | (u < 0), NONE, u)

    def above(c, k):
        t = tables[16 + jnp.maximum(tables[20, c], 0), k]
        if k >= 9:
            found = jnp.where(t == tables[20, 0], 6, jnp.where(t == tables[20, 1], 7, NONE))
            return jnp.where(t < 0, NONE, found)
        u = tab[5, jnp.clip(t - 4, 0, 1)]
        return jnp.where((t < 4) | (t > 5) | (u < 0), NONE, u)

    gather_padded(slots, pad_face, 0, below, [(0, 6, 0), (0, 7, 1), (1, 0, 2)])
    gather_padded(slots, pad_face, 1, above, [(-1, 7, 0), (0, 0, 1), (0, 1, 2)])
    for pair in range(2):
        gather_padded(slots, pad, pair, own(pair), OWN_PLANES)

    values = sum(bias[m].astype(F32) for m in range(4))
    shift[...] = values[0:8] + values[8:16]
    moved = shift[0:1, :] + shift[pl.ds(2 + me, 1), :]
    for copy in w_copies:
        copy.wait()

    for pair in range(2):
        acc[pair] = conv_pair(pad, pair, w1)
        finish(acc, moved, tab, pair, slots)
    sides_out = silu(conv_face(pad_face, w1) + moved).reshape(2, 8, 2, 8, 128)
    for c in range(2):
        slots[4 + c, 7] = sides_out[0, :, c]
        slots[6 + c, 0] = sides_out[1, :, c]
    for pair in range(2):
        gather_padded(slots, pad_out, pair, own(pair), OWN_PLANES)


def convolve_first(tables, feat, sides, shards):
    return pl.pallas_call(
        first_kernel,
        out_shape=[jax.ShapeDtypeStruct((2, 10, 10, 16, 384), BF16), jax.ShapeDtypeStruct((8, 128), F32)],
        in_specs=[SMEM] + [HBM] * 10,
        out_specs=[VMEM] * 2,
        scratch_shapes=[
            pltpu.VMEM((4, 16, 32, 128), BF16),
            pltpu.VMEM((2, 8, 32, 128), BF16),
            pltpu.VMEM((27, 128, 128), BF16),
            pltpu.VMEM((4, 16, 128), BF16),
            pltpu.VMEM((2, 16, 128), BF16),
            pltpu.VMEM((32, 128), jnp.int32),
            pltpu.SMEM((32, 128), jnp.int32),
            pltpu.VMEM((9, 8, 8, 8, 128), F32),
            pltpu.VMEM((2, 10, 10, 16, 384), BF16),
            pltpu.VMEM((2, 3, 10, 16, 384), BF16),
            pltpu.VMEM((2, 512, 256), F32),
            pltpu.SemaphoreType.DMA((17,)),
        ],
        compiler_params=pltpu.CompilerParams(vmem_limit_bytes=24 << 20),
        cost_estimate=pl.CostEstimate(flops=5 * 10**9, bytes_accessed=4 * 10**6, transcendentals=10**6),
        name="convolve_first",
    )(tables, *feat, *sides, *shards)


def second_kernel(tab, pad, shift, *refs):
    shards, outs = refs[0:4], refs[4:8]
    w2, slots, acc, turned, sem = refs[8:]
    me = lax.axis_index("chan")
    w_copies = load_shards(shards, w2, [me ^ m for m in range(4)], sem)
    for copy in w_copies:
        copy.start()
    for copy in w_copies:
        copy.wait()
    for pair in range(2):
        acc[pair] = conv_pair(pad, pair, w2)
        finish(acc, shift[1:2, :], tab, pair, slots)
    for b in range(4):
        brick = slots[b].reshape(512, 128).astype(BF16).T
        for g in range(4):
            turned[g, b] = brick[32 * g : 32 * g + 32]
    for m in range(4):
        outs[m][...] = turned[me ^ m]


def convolve_second(tables, pad, shift, shards):
    piece = jax.ShapeDtypeStruct((4, 32, 512), BF16)
    return pl.pallas_call(
        second_kernel,
        out_shape=[piece] * 4,
        in_specs=[SMEM, VMEM, VMEM] + [HBM] * 4,
        out_specs=[VMEM] * 4,
        scratch_shapes=[
            pltpu.VMEM((27, 128, 128), BF16),
            pltpu.VMEM((4, 8, 8, 8, 128), F32),
            pltpu.VMEM((2, 512, 256), F32),
            pltpu.VMEM((4, 4, 32, 512), BF16),
            pltpu.SemaphoreType.DMA((4,)),
        ],
        compiler_params=pltpu.CompilerParams(vmem_limit_bytes=24 << 20),
        cost_estimate=pl.CostEstimate(flops=4 * 10**9, bytes_accessed=4 * 10**6, transcendentals=10**6),
        name="convolve_second",
    )(tables, pad, shift, *shards)


def join_kernel(*refs):
    pieces, out, sem = refs[:4], refs[4], refs[5]
    me = lax.axis_index("chan")
    copies = [pltpu.make_async_copy(pieces[m], out.at[me ^ m], sem.at[m]) for m in range(4)]
    for copy in copies:
        copy.start()
    for copy in copies:
        copy.wait()


def join(pieces):
    return pl.pallas_call(
        join_kernel,
        out_shape=jax.ShapeDtypeStruct((4, 4, 32, 512), BF16),
        in_specs=[HBM] * 4,
        out_specs=HBM,
        scratch_shapes=[pltpu.SemaphoreType.DMA((4,))],
        compiler_params=pltpu.CompilerParams(vmem_limit_bytes=8 << 20),
        name="join_levels",
    )(*pieces)


def swap(value, m):
    return lax.ppermute(value, "chan", [(i, i ^ m) for i in range(4)])


def swap_faces(value, first):
    count = lax.axis_size("slab")
    partner = [((s + first) ^ 1) - first for s in range(count)]
    return lax.ppermute(value, "slab", [(s, p if 0 <= p < count else s) for s, p in enumerate(partner)])


def shards(features, neighbours, face_lists, w_first, b_first, w_second, b_second, level_embed):
    w1, w2 = w_first.transpose(0, 2, 1), w_second.transpose(0, 2, 1)
    far = swap(w1, 2)
    own, one, two, three, tables = split(
        features, neighbours, face_lists, b_first, b_second, level_embed
    )
    far, one, two, three, later = lax.optimization_barrier(
        (far, swap(one, 1), swap(two, 2), swap(three, 3), w2)
    )
    pieces = [own, one, two, three]
    first = [w1, swap(w1, 1), far, swap(far, 1)]
    sides = faces(tables, pieces)
    sides = [swap_faces(sides[i], i) for i in range(2)]
    second = [w2] + [swap(later, m) for m in (1, 2, 3)]
    pad, shift = convolve_first(tables, pieces, sides, first)
    outs = convolve_second(tables, pad, shift, second)
    return join([outs[0]] + [swap(outs[m], m) for m in (1, 2, 3)])


def solution(mesh):
    placed = (
        P(None, "slab", "chan", None),
        P("slab", None),
        P("slab", None, None),
        P(None, None, "chan"),
        P("chan"),
        P(None, None, "chan"),
        P("chan"),
        P(None, "chan"),
    )
    return jax.shard_map(
        shards, mesh=mesh, in_specs=placed, out_specs=P(None, "slab", "chan", None), check_vma=False
    )
```

```python
import jax
import jax.numpy as jnp
from jax import lax
from jax.experimental import pallas as pl
from jax.experimental.pallas import tpu as pltpu
from jax.sharding import PartitionSpec as P

BF16, F32 = jnp.bfloat16, jnp.float32
NONE = 8
HBM = pl.BlockSpec(memory_space=pl.ANY)
VMEM = pl.BlockSpec(memory_space=pltpu.VMEM)
SMEM = pl.BlockSpec(memory_space=pltpu.SMEM)
SPAN = {-1: (7, 0, 1), 0: (0, 1, 8), 1: (0, 9, 1)}


def offset(dz, dy, dx):
    return 9 * (dz + 1) + 3 * (dy + 1) + (dx + 1)


PIECE = 17


def split_kernel(feat, near, lists, b1, b2, lev, *refs):
    pieces, tables = refs[:4], refs[4]
    me = lax.axis_index("chan")
    values = jnp.concatenate([b1[...], b2[...], lev[...], jnp.zeros((2, 32), F32)], axis=0)
    values = jnp.concatenate([values] * 4, axis=1)
    lane = lax.broadcasted_iota(jnp.int32, (8, 128), 1)
    values = jnp.where(lane // 32 == me, values, 0.0)
    high = values.astype(BF16).astype(F32)
    values = jnp.concatenate([high, values - high, jnp.zeros((16, 128), F32)], axis=0).astype(BF16)
    for m in range(4):
        for b in range(4):
            for v in range(4):
                pieces[m][4 * v + b] = feat[me ^ m, b, :, 128 * v : 128 * v + 128]
        pieces[m][16] = values
    tables[...] = jnp.zeros((8, 128), jnp.int32)
    tables[pl.ds(0, 4), pl.ds(0, 27)] = near[...]
    tables[pl.ds(4, 2), pl.ds(0, 2)] = lists[0]
    sent = tables[...].astype(F32)
    pieces[0][17] = jnp.concatenate([sent, jnp.zeros((24, 128), F32)], axis=0).astype(BF16)


def split(features, neighbours, face_lists, b1, b2, lev):
    piece = jax.ShapeDtypeStruct((PIECE, 32, 128), BF16)
    kept = jax.ShapeDtypeStruct((PIECE + 1, 32, 128), BF16)
    return pl.pallas_call(
        split_kernel,
        out_shape=[kept, piece, piece, piece, jax.ShapeDtypeStruct((8, 128), jnp.int32)],
        in_specs=[VMEM] * 6,
        out_specs=[VMEM] * 5,
        compiler_params=pltpu.CompilerParams(vmem_limit_bytes=8 << 20),
        name="split_features",
    )(features, neighbours, face_lists, b1.reshape(1, 32), b2.reshape(1, 32), lev)


def faces_kernel(tables, *refs):
    pieces, sides, sem = refs[:4], refs[4:6], refs[6]
    odd = lax.axis_index("slab") % 2
    copies = []
    for i, out in enumerate(sides):
        tier = (odd + 1 + i) % 2
        for c in range(2):
            b = jnp.maximum(tables[4 + tier, c], 0)
            for m in range(4):
                source = pieces[m].at[12 * tier + b]
                copies.append(pltpu.make_async_copy(source, out.at[4 * c + m], sem.at[8 * i + 4 * c + m]))
        copies.append(pltpu.make_async_copy(pieces[0].at[17], out.at[8], sem.at[16 + i]))
    for copy in copies:
        copy.start()
    for copy in copies:
        copy.wait()


def faces(tables, pieces):
    side = jax.ShapeDtypeStruct((9, 32, 128), BF16)
    return pl.pallas_call(
        faces_kernel,
        out_shape=[side] * 2,
        in_specs=[SMEM] + [HBM] * 4,
        out_specs=[VMEM] * 2,
        scratch_shapes=[pltpu.SemaphoreType.DMA((18,))],
        compiler_params=pltpu.CompilerParams(vmem_limit_bytes=4 << 20),
        name="pick_faces",
    )(tables, *pieces)


def silu(v):
    return v / (1.0 + jnp.exp(-v))


def gather_padded(slots, pad, slot, planes):
    x = lax.broadcasted_iota(jnp.int32, (1, 8, 128), 1)
    for dz, z_from, z_to in planes:
        for dy in (-1, 0, 1):
            y_from, y_to, n = SPAN[dy]
            parts = ([], [], [])
            for w in range(2):
                mid, left, right = (
                    slots[slot(w, offset(dz, dy, dx)), z_from, y_from : y_from + n] for dx in (0, -1, 1)
                )
                parts[0].append(pltpu.roll(jnp.where(x == 7, left, mid), 1, 1))
                parts[1].append(mid)
                parts[2].append(pltpu.roll(jnp.where(x == 0, right, mid), 7, 1))
            for d in range(3):
                tile = jnp.concatenate(parts[d], axis=1).astype(BF16)
                pad[z_to, y_to : y_to + n, :, 128 * d : 128 * d + 128] = tile


OWN_PLANES = [(-1, 7, 0)] + [(0, z, z + 1) for z in range(8)] + [(1, 0, 9)]


def conv_pair(pad, w):
    zero = jnp.zeros((128, 128), BF16)
    total = None
    blocks = [(zin, dy) for zin in range(4) for dy in range(3)]
    for first in range(0, 12, 2):
        left, right = [], []
        for zin, dy in blocks[first : first + 2]:
            planes = [pad[zin + 2 * j, dy : dy + 8].reshape(128, 384) for j in range(4)]
            left.append(jnp.concatenate(planes, axis=0))
            for dx in range(3):
                even = w[9 * zin + 3 * dy + dx] if zin < 3 else zero
                odd = w[9 * (zin - 1) + 3 * dy + dx] if zin > 0 else zero
                right.append(jnp.concatenate([even, odd], axis=1))
        part = jnp.dot(
            jnp.concatenate(left, axis=1), jnp.concatenate(right, axis=0), preferred_element_type=F32
        )
        total = part if total is None else total + part
    return total


def conv_face(pad, w):
    total = None
    blocks = [(dz, dy) for dz in range(3) for dy in range(3)]
    for group in (blocks[0:2], blocks[2:4], blocks[4:6], blocks[6:9]):
        left, right = [], []
        for dz, dy in group:
            sides = [pad[side, dz, dy : dy + 8].reshape(128, 384) for side in range(2)]
            left.append(jnp.concatenate(sides, axis=0))
            right += [w[9 * dz + 3 * dy + dx] for dx in range(3)]
        part = jnp.dot(
            jnp.concatenate(left, axis=1), jnp.concatenate(right, axis=0), preferred_element_type=F32
        )
        total = part if total is None else total + part
    return total


def finish(acc, moved, active, slots, first):
    for j in range(4):
        for zo in range(2):
            tile = silu(acc[128 * j : 128 * j + 128, 128 * zo : 128 * zo + 128] + moved)
            tile = tile.reshape(8, 2, 8, 128)
            for w in range(2):
                slots[first + w, 2 * j + zo] = jnp.where(active[w], tile[:, w], 0.0)


def give_out(slots, turned, outs):
    me = lax.axis_index("chan")
    for b in range(2):
        brick = slots[b].reshape(512, 128).astype(BF16).T
        for g in range(4):
            turned[g, b] = brick[32 * g : 32 * g + 32]
    for m in range(4):
        outs[m][...] = turned[me ^ m]


def conv_kernel(tab, *refs):
    feat, sides, own_w, near_w, far_w = refs[0:4], refs[4:6], refs[6:8], refs[8:10], refs[10:14]
    outs, pad_rest, w2, shift = refs[14:18], refs[18], refs[19], refs[20]
    fs, hs, w1, bias, sent, sent_int, tables, slots, pad, pad_face, acc, turned, sem = refs[21:]
    pads = (pad, pad_rest)
    me = lax.axis_index("chan")
    odd = layer_of_slab()

    f_copies, t_copies = [], []
    for i in range(2):
        side = (lax.axis_index("slab") + 1 + i) % 2
        t_copies.append(pltpu.make_async_copy(sides[i].at[8, pl.ds(0, 16)], sent.at[side], sem.at[i]))
        f_copies.append(pltpu.make_async_copy(sides[i].at[pl.ds(0, 8)], hs.at[side], sem.at[2 + i]))
    for m in range(4):
        f_copies.append(pltpu.make_async_copy(feat[m].at[pl.ds(0, 16)], fs.at[m], sem.at[4 + m]))
        f_copies.append(pltpu.make_async_copy(feat[m].at[16, pl.ds(0, 16)], bias.at[m], sem.at[8 + m]))
    for copy in t_copies + f_copies:
        copy.start()

    def load_shard(m, layer, source):
        g = 32 * m if layer == 0 else pl.multiple_of((me ^ m) * 32, 32)
        return pltpu.make_async_copy(source, (w1, w2)[layer].at[:, pl.ds(g, 32), :], sem.at[12 + 2 * m + layer])

    w_copies = ([], [])
    for layer in range(2):
        near = [load_shard(0, layer, own_w[layer])]
        near.append(load_shard(1, layer, near_w[layer]))
        for copy in near:
            copy.start()
        w_copies[layer].extend(near)
        for m in (2, 3):
            mine, other = far_w[m - 2], far_w[m]

            @pl.when(odd == layer)
            def _():
                load_shard(m, layer, mine).start()

            @pl.when(odd != layer)
            def _():
                load_shard(m, layer, other).start()

            w_copies[layer].append(load_shard(m, layer, mine))
    w1_copies, w2_copies = w_copies
    for copy in t_copies:
        copy.wait()
    sent_int[...] = sent[...].astype(F32).astype(jnp.int32).reshape(32, 128)
    to_scalars = pltpu.make_async_copy(sent_int, tables, sem.at[24])
    to_scalars.start()
    for copy in f_copies:
        copy.wait()

    slots[NONE] = jnp.zeros((8, 8, 8, 128), F32)
    for b in range(4):
        for v in range(4):
            brick = jnp.concatenate([fs[m, 4 * v + b] for m in range(4)], axis=0)
            slots[b, 2 * v : 2 * v + 2] = brick.T.astype(F32).reshape(2, 8, 8, 128)
    for side in range(2):
        for c in range(2):
            face = jnp.concatenate([hs[side, 4 * c + m] for m in range(4)], axis=0)
            first = 6 if side == 0 else 0
            slots[4 + 2 * side + c, first : first + 2] = face.T.astype(F32).reshape(2, 8, 8, 128)

    to_scalars.wait()

    def own(pair):
        def slot(w, k):
            t = tab[2 * pair + w, k]
            return jnp.where(t < 0, NONE, t)

        return slot

    def below(c, k):
        t = tables[0 + jnp.maximum(tables[5, c], 0), k]
        if k < 18:
            found = jnp.where(t == tables[5, 0], 4, jnp.where(t == tables[5, 1], 5, NONE))
            return jnp.where(t < 0, NONE, found)
        u = tab[4, jnp.clip(t - 6, 0, 1)]
        return jnp.where((t < 6) | (u < 0), NONE, u)

    def above(c, k):
        t = tables[16 + jnp.maximum(tables[20, c], 0), k]
        if k >= 9:
            found = jnp.where(t == tables[20, 0], 6, jnp.where(t == tables[20, 1], 7, NONE))
            return jnp.where(t < 0, NONE, found)
        u = tab[5, jnp.clip(t - 4, 0, 1)]
        return jnp.where((t < 4) | (t > 5) | (u < 0), NONE, u)

    gather_padded(slots, pad_face.at[0], below, [(0, 6, 0), (0, 7, 1), (1, 0, 2)])
    gather_padded(slots, pad_face.at[1], above, [(-1, 7, 0), (0, 0, 1), (0, 1, 2)])
    for pair in range(2):
        gather_padded(slots, pads[pair], own(pair), OWN_PLANES)

    for copy in w1_copies:
        copy.wait()
    values = sum(bias[m].astype(F32) for m in range(4))
    shift[0:8, :] = values[0:8] + values[8:16]
    for w in range(2):
        shift[8 + w : 9 + w, :] = jnp.full((1, 128), jnp.where(tab[2 + w, 13] >= 0, 1.0, 0.0), F32)
    shift[10:16, :] = jnp.zeros((6, 128), F32)
    shift_second = shift[1:2, :]
    shift_first = shift[0:1, :] + shift[pl.ds(2 + me, 1), :]

    for pair in range(2):
        acc[...] = conv_pair(pads[pair], w1)
        finish(acc, shift_first, [tab[2 * pair + w, 13] >= 0 for w in range(2)], slots, 2 * pair)
    faces = silu(conv_face(pad_face, w1) + shift_first).reshape(2, 8, 2, 8, 128)
    for c in range(2):
        slots[4 + c, 7] = faces[0, :, c]
        slots[6 + c, 0] = faces[1, :, c]

    for pair in range(2):
        gather_padded(slots, pads[pair], own(pair), OWN_PLANES)
    for copy in w2_copies:
        copy.wait()
    acc[...] = conv_pair(pads[0], w2)
    finish(acc, shift_second, [tab[w, 13] >= 0 for w in range(2)], slots, 0)
    give_out(slots, turned, outs)


def rest_kernel(pad, w2, shift, *refs):
    outs, slots, acc, turned = refs[:4], refs[4], refs[5], refs[6]
    acc[...] = conv_pair(pad, w2)
    finish(acc, shift[1:2, :], [shift[8 + w : 9 + w, :] > 0 for w in range(2)], slots, 0)
    give_out(slots, turned, outs)


HALF = jax.ShapeDtypeStruct((2, 32, 512), BF16)


def convolve(tables, feat, sides, own_w, near_w, far_w):
    *outs, pad, w2, shift = pl.pallas_call(
        conv_kernel,
        out_shape=[HALF] * 4
        + [
            jax.ShapeDtypeStruct((10, 10, 16, 384), BF16),
            jax.ShapeDtypeStruct((27, 128, 128), BF16),
            jax.ShapeDtypeStruct((16, 128), F32),
        ],
        in_specs=[SMEM] + [HBM] * 14,
        out_specs=[VMEM] * 7,
        scratch_shapes=[
            pltpu.VMEM((4, 16, 32, 128), BF16),
            pltpu.VMEM((2, 8, 32, 128), BF16),
            pltpu.VMEM((27, 128, 128), BF16),
            pltpu.VMEM((4, 16, 128), BF16),
            pltpu.VMEM((2, 16, 128), BF16),
            pltpu.VMEM((32, 128), jnp.int32),
            pltpu.SMEM((32, 128), jnp.int32),
            pltpu.VMEM((9, 8, 8, 8, 128), F32),
            pltpu.VMEM((10, 10, 16, 384), BF16),
            pltpu.VMEM((2, 3, 10, 16, 384), BF16),
            pltpu.VMEM((512, 256), F32),
            pltpu.VMEM((4, 2, 32, 512), BF16),
            pltpu.SemaphoreType.DMA((32,)),
        ],
        compiler_params=pltpu.CompilerParams(vmem_limit_bytes=40 << 20),
        cost_estimate=pl.CostEstimate(flops=6 * 10**9, bytes_accessed=4 * 10**6, transcendentals=10**6),
        name="convolve",
    )(tables, *feat, *sides, *own_w, *near_w, *far_w)
    return outs, pad, w2, shift


def convolve_rest(pad, w2, shift):
    return pl.pallas_call(
        rest_kernel,
        out_shape=[HALF] * 4,
        in_specs=[VMEM] * 3,
        out_specs=[VMEM] * 4,
        scratch_shapes=[
            pltpu.VMEM((2, 8, 8, 8, 128), F32),
            pltpu.VMEM((512, 256), F32),
            pltpu.VMEM((4, 2, 32, 512), BF16),
        ],
        compiler_params=pltpu.CompilerParams(vmem_limit_bytes=24 << 20),
        cost_estimate=pl.CostEstimate(flops=2 * 10**9, bytes_accessed=4 * 10**6, transcendentals=10**6),
        name="convolve_rest",
    )(pad, w2, shift)


def join_kernel(*refs):
    pieces, out, sem = refs[:8], refs[8], refs[9]
    me = lax.axis_index("chan")
    copies = [
        pltpu.make_async_copy(pieces[i], out.at[me ^ (i % 4), pl.ds(2 * (i // 4), 2)], sem.at[i])
        for i in range(8)
    ]
    for copy in copies:
        copy.start()
    for copy in copies:
        copy.wait()


def join(pieces):
    return pl.pallas_call(
        join_kernel,
        out_shape=jax.ShapeDtypeStruct((4, 4, 32, 512), BF16),
        in_specs=[HBM] * 8,
        out_specs=HBM,
        scratch_shapes=[pltpu.SemaphoreType.DMA((8,))],
        compiler_params=pltpu.CompilerParams(vmem_limit_bytes=8 << 20),
        name="join_levels",
    )(*pieces)


def swap(value, m):
    return lax.ppermute(value, "chan", [(i, i ^ m) for i in range(4)])


def layer_of_slab():
    slab = lax.axis_index("slab")
    return (slab + slab // 8) % 2


def swap_slabs(value, step, m):
    count = lax.axis_size("slab")
    pairs = [(4 * s + g, 4 * (s ^ step) + (g ^ m)) for s in range(count) for g in range(4)]
    return lax.ppermute(value, ("slab", "chan"), pairs)


def swap_faces(value, first):
    count = lax.axis_size("slab")
    partner = [((s + first) ^ 1) - first for s in range(count)]
    return lax.ppermute(value, "slab", [(s, p if 0 <= p < count else s) for s, p in enumerate(partner)])


def shards(features, neighbours, face_lists, w_first, b_first, w_second, b_second, level_embed):
    w1, w2 = w_first.transpose(0, 2, 1), w_second.transpose(0, 2, 1)
    fetched = swap(jnp.where(layer_of_slab() == 0, w1, w2), 2)
    own, one, two, three, tables = split(
        features, neighbours, face_lists, b_first, b_second, level_embed
    )
    fetched, one, two, three = lax.optimization_barrier(
        (fetched, swap(one, 1), swap(two, 2), swap(three, 3))
    )
    pieces = [own, one, two, three]
    near = [swap(w1, 1), swap(w2, 1)]
    far = [fetched, swap(fetched, 1), swap_slabs(fetched, 1, 0), swap_slabs(fetched, 8, 1)]
    sides = faces(tables, pieces)
    sides = [swap_faces(sides[i], i) for i in range(2)]
    early, *state = convolve(tables, pieces, sides, (w1, w2), near, far)
    early = [early[0]] + [swap(early[m], m) for m in (1, 2, 3)]
    late = convolve_rest(*state)
    return join(early + [late[0]] + [swap(late[m], m) for m in (1, 2, 3)])


def solution(mesh):
    placed = (
        P(None, "slab", "chan", None),
        P("slab", None),
        P("slab", None, None),
        P(None, None, "chan"),
        P("chan"),
        P(None, None, "chan"),
        P("chan"),
        P(None, "chan"),
    )
    return jax.shard_map(
        shards, mesh=mesh, in_specs=placed, out_specs=P(None, "slab", "chan", None), check_vma=False
    )
```

```python
import jax
import jax.numpy as jnp
from jax import lax
from jax.experimental import pallas as pl
from jax.experimental.pallas import tpu as pltpu
from jax.sharding import PartitionSpec as P

BF16, F32 = jnp.bfloat16, jnp.float32
NONE = 8
HBM = pl.BlockSpec(memory_space=pl.ANY)
VMEM = pl.BlockSpec(memory_space=pltpu.VMEM)
SMEM = pl.BlockSpec(memory_space=pltpu.SMEM)
SPAN = {-1: (7, 0, 1), 0: (0, 1, 8), 1: (0, 9, 1)}


def offset(dz, dy, dx):
    return 9 * (dz + 1) + 3 * (dy + 1) + (dx + 1)


PIECE = 17


def split_kernel(feat, near, lists, b1, b2, lev, *refs):
    pieces, tables = refs[:4], refs[4]
    me = lax.axis_index("chan")
    values = jnp.concatenate([b1[...], b2[...], lev[...], jnp.zeros((2, 32), F32)], axis=0)
    values = jnp.concatenate([values] * 4, axis=1)
    lane = lax.broadcasted_iota(jnp.int32, (8, 128), 1)
    values = jnp.where(lane // 32 == me, values, 0.0)
    high = values.astype(BF16).astype(F32)
    values = jnp.concatenate([high, values - high, jnp.zeros((16, 128), F32)], axis=0).astype(BF16)
    for m in range(4):
        for b in range(4):
            for v in range(4):
                pieces[m][4 * v + b] = feat[me ^ m, b, :, 128 * v : 128 * v + 128]
        pieces[m][16] = values
    tables[...] = jnp.zeros((8, 128), jnp.int32)
    tables[pl.ds(0, 4), pl.ds(0, 27)] = near[...]
    tables[pl.ds(4, 2), pl.ds(0, 2)] = lists[0]
    sent = tables[...].astype(F32)
    pieces[0][17] = jnp.concatenate([sent, jnp.zeros((24, 128), F32)], axis=0).astype(BF16)


def split(features, neighbours, face_lists, b1, b2, lev):
    piece = jax.ShapeDtypeStruct((PIECE, 32, 128), BF16)
    kept = jax.ShapeDtypeStruct((PIECE + 1, 32, 128), BF16)
    return pl.pallas_call(
        split_kernel,
        out_shape=[kept, piece, piece, piece, jax.ShapeDtypeStruct((8, 128), jnp.int32)],
        in_specs=[VMEM] * 6,
        out_specs=[VMEM] * 5,
        compiler_params=pltpu.CompilerParams(vmem_limit_bytes=8 << 20),
        name="split_features",
    )(features, neighbours, face_lists, b1.reshape(1, 32), b2.reshape(1, 32), lev)


def faces_kernel(tables, *refs):
    pieces, sides, sem = refs[:4], refs[4:6], refs[6]
    odd = lax.axis_index("slab") % 2
    copies = []
    for i, out in enumerate(sides):
        tier = (odd + 1 + i) % 2
        for c in range(2):
            b = jnp.maximum(tables[4 + tier, c], 0)
            for m in range(4):
                source = pieces[m].at[12 * tier + b]
                copies.append(pltpu.make_async_copy(source, out.at[4 * c + m], sem.at[8 * i + 4 * c + m]))
        copies.append(pltpu.make_async_copy(pieces[0].at[17], out.at[8], sem.at[16 + i]))
    for copy in copies:
        copy.start()
    for copy in copies:
        copy.wait()


def faces(tables, pieces):
    side = jax.ShapeDtypeStruct((9, 32, 128), BF16)
    return pl.pallas_call(
        faces_kernel,
        out_shape=[side] * 2,
        in_specs=[SMEM] + [HBM] * 4,
        out_specs=[VMEM] * 2,
        scratch_shapes=[pltpu.SemaphoreType.DMA((18,))],
        compiler_params=pltpu.CompilerParams(vmem_limit_bytes=4 << 20),
        name="pick_faces",
    )(tables, *pieces)


def silu(v):
    return v / (1.0 + jnp.exp(-v))


def gather_padded(slots, pad, lead, slot, planes):
    x = lax.broadcasted_iota(jnp.int32, (1, 8, 128), 1)
    for dz, z_from, z_to in planes:
        for dy in (-1, 0, 1):
            y_from, y_to, n = SPAN[dy]
            parts = ([], [], [])
            for w in range(2):
                mid, left, right = (
                    slots[slot(w, offset(dz, dy, dx)), z_from, y_from : y_from + n] for dx in (0, -1, 1)
                )
                parts[0].append(pltpu.roll(jnp.where(x == 7, left, mid), 1, 1))
                parts[1].append(mid)
                parts[2].append(pltpu.roll(jnp.where(x == 0, right, mid), 7, 1))
            for d in range(3):
                tile = jnp.concatenate(parts[d], axis=1).astype(BF16)
                pad[lead, z_to, y_to : y_to + n, :, 128 * d : 128 * d + 128] = tile


OWN_PLANES = [(-1, 7, 0)] + [(0, z, z + 1) for z in range(8)] + [(1, 0, 9)]


def conv_pair(pad, lead, w):
    zero = jnp.zeros((128, 128), BF16)
    total = None
    blocks = [(zin, dy) for zin in range(4) for dy in range(3)]
    for first in range(0, 12, 2):
        left, right = [], []
        for zin, dy in blocks[first : first + 2]:
            planes = [pad[lead, zin + 2 * j, dy : dy + 8].reshape(128, 384) for j in range(4)]
            left.append(jnp.concatenate(planes, axis=0))
            for dx in range(3):
                even = w[9 * zin + 3 * dy + dx] if zin < 3 else zero
                odd = w[9 * (zin - 1) + 3 * dy + dx] if zin > 0 else zero
                right.append(jnp.concatenate([even, odd], axis=1))
        part = jnp.dot(
            jnp.concatenate(left, axis=1), jnp.concatenate(right, axis=0), preferred_element_type=F32
        )
        total = part if total is None else total + part
    return total


def conv_face(pad, w):
    total = None
    blocks = [(dz, dy) for dz in range(3) for dy in range(3)]
    for group in (blocks[0:2], blocks[2:4], blocks[4:6], blocks[6:9]):
        left, right = [], []
        for dz, dy in group:
            sides = [pad[side, dz, dy : dy + 8].reshape(128, 384) for side in range(2)]
            left.append(jnp.concatenate(sides, axis=0))
            right += [w[9 * dz + 3 * dy + dx] for dx in range(3)]
        part = jnp.dot(
            jnp.concatenate(left, axis=1), jnp.concatenate(right, axis=0), preferred_element_type=F32
        )
        total = part if total is None else total + part
    return total


def layer_of_slab():
    slab = lax.axis_index("slab")
    return (slab + slab // 8) % 2


def load_shards(layer, near, far, weights, order, sem):
    copies = []
    for m in range(4):
        rows = weights.at[:, pl.ds(pl.multiple_of(32 * order[m], 32), 32), :]
        if m < 2:
            copies.append(pltpu.make_async_copy(near[m], rows, sem.at[m]))
            copies[m].start()
            continue

        @pl.when(layer_of_slab() == layer)
        def _():
            pltpu.make_async_copy(far[m - 2], rows, sem.at[m]).start()

        @pl.when(layer_of_slab() != layer)
        def _():
            pltpu.make_async_copy(far[m], rows, sem.at[m]).start()

        copies.append(pltpu.make_async_copy(far[m], rows, sem.at[m]))
    return copies


def finish(acc, moved, tab, pair, slots):
    for j in range(4):
        for zo in range(2):
            tile = silu(acc[pair, 128 * j : 128 * j + 128, 128 * zo : 128 * zo + 128] + moved)
            tile = tile.reshape(8, 2, 8, 128)
            for w in range(2):
                b = 2 * pair + w
                slots[b, 2 * j + zo] = jnp.where(tab[b, 13] >= 0, tile[:, w], 0.0)


def first_kernel(tab, *refs):
    feat, sides, near, far = refs[0:4], refs[4:6], refs[6:8], refs[8:12]
    pad_out, shift = refs[12:14]
    fs, hs, w1, bias, sent, sent_int, tables, slots, pad, pad_face, acc, sem, w_sem = refs[14:]
    me = lax.axis_index("chan")

    f_copies, t_copies = [], []
    for i in range(2):
        side = (lax.axis_index("slab") + 1 + i) % 2
        t_copies.append(pltpu.make_async_copy(sides[i].at[8, pl.ds(0, 16)], sent.at[side], sem.at[i]))
        f_copies.append(pltpu.make_async_copy(sides[i].at[pl.ds(0, 8)], hs.at[side], sem.at[2 + i]))
    for m in range(4):
        f_copies.append(pltpu.make_async_copy(feat[m].at[pl.ds(0, 16)], fs.at[m], sem.at[4 + m]))
        f_copies.append(pltpu.make_async_copy(feat[m].at[16, pl.ds(0, 16)], bias.at[m], sem.at[8 + m]))
    for copy in t_copies + f_copies:
        copy.start()
    w_copies = load_shards(0, near, far, w1, range(4), w_sem)
    for copy in t_copies:
        copy.wait()
    sent_int[...] = sent[...].astype(F32).astype(jnp.int32).reshape(32, 128)
    to_scalars = pltpu.make_async_copy(sent_int, tables, sem.at[16])
    to_scalars.start()
    for copy in f_copies:
        copy.wait()

    slots[NONE] = jnp.zeros((8, 8, 8, 128), F32)
    for b in range(4):
        for v in range(4):
            brick = jnp.concatenate([fs[m, 4 * v + b] for m in range(4)], axis=0)
            slots[b, 2 * v : 2 * v + 2] = brick.T.astype(F32).reshape(2, 8, 8, 128)
    for side in range(2):
        for c in range(2):
            face = jnp.concatenate([hs[side, 4 * c + m] for m in range(4)], axis=0)
            first = 6 if side == 0 else 0
            slots[4 + 2 * side + c, first : first + 2] = face.T.astype(F32).reshape(2, 8, 8, 128)

    to_scalars.wait()

    def own(pair):
        def slot(w, k):
            t = tab[2 * pair + w, k]
            return jnp.where(t < 0, NONE, t)

        return slot

    def below(c, k):
        t = tables[0 + jnp.maximum(tables[5, c], 0), k]
        if k < 18:
            found = jnp.where(t == tables[5, 0], 4, jnp.where(t == tables[5, 1], 5, NONE))
            return jnp.where(t < 0, NONE, found)
        u = tab[4, jnp.clip(t - 6, 0, 1)]
        return jnp.where((t < 6) | (u < 0), NONE, u)

    def above(c, k):
        t = tables[16 + jnp.maximum(tables[20, c], 0), k]
        if k >= 9:
            found = jnp.where(t == tables[20, 0], 6, jnp.where(t == tables[20, 1], 7, NONE))
            return jnp.where(t < 0, NONE, found)
        u = tab[5, jnp.clip(t - 4, 0, 1)]
        return jnp.where((t < 4) | (t > 5) | (u < 0), NONE, u)

    gather_padded(slots, pad_face, 0, below, [(0, 6, 0), (0, 7, 1), (1, 0, 2)])
    gather_padded(slots, pad_face, 1, above, [(-1, 7, 0), (0, 0, 1), (0, 1, 2)])
    for pair in range(2):
        gather_padded(slots, pad, pair, own(pair), OWN_PLANES)

    values = sum(bias[m].astype(F32) for m in range(4))
    shift[...] = values[0:8] + values[8:16]
    moved = shift[0:1, :] + shift[pl.ds(2 + me, 1), :]
    for copy in w_copies:
        copy.wait()

    for pair in range(2):
        acc[pair] = conv_pair(pad, pair, w1)
        finish(acc, moved, tab, pair, slots)
    sides_out = silu(conv_face(pad_face, w1) + moved).reshape(2, 8, 2, 8, 128)
    for c in range(2):
        slots[4 + c, 7] = sides_out[0, :, c]
        slots[6 + c, 0] = sides_out[1, :, c]
    for pair in range(2):
        gather_padded(slots, pad_out, pair, own(pair), OWN_PLANES)


def convolve_first(tables, feat, sides, near, far):
    return pl.pallas_call(
        first_kernel,
        out_shape=[jax.ShapeDtypeStruct((2, 10, 10, 16, 384), BF16), jax.ShapeDtypeStruct((8, 128), F32)],
        in_specs=[SMEM] + [HBM] * 12,
        out_specs=[VMEM] * 2,
        scratch_shapes=[
            pltpu.VMEM((4, 16, 32, 128), BF16),
            pltpu.VMEM((2, 8, 32, 128), BF16),
            pltpu.VMEM((27, 128, 128), BF16),
            pltpu.VMEM((4, 16, 128), BF16),
            pltpu.VMEM((2, 16, 128), BF16),
            pltpu.VMEM((32, 128), jnp.int32),
            pltpu.SMEM((32, 128), jnp.int32),
            pltpu.VMEM((9, 8, 8, 8, 128), F32),
            pltpu.VMEM((2, 10, 10, 16, 384), BF16),
            pltpu.VMEM((2, 3, 10, 16, 384), BF16),
            pltpu.VMEM((2, 512, 256), F32),
            pltpu.SemaphoreType.DMA((17,)),
            pltpu.SemaphoreType.DMA((4,)),
        ],
        compiler_params=pltpu.CompilerParams(vmem_limit_bytes=24 << 20),
        cost_estimate=pl.CostEstimate(flops=5 * 10**9, bytes_accessed=4 * 10**6, transcendentals=10**6),
        name="convolve_first",
    )(tables, *feat, *sides, *near, *far)


def second_kernel(tab, pad, shift, *refs):
    near, far, outs = refs[0:2], refs[2:6], refs[6:10]
    w2, slots, acc, turned, sem = refs[10:]
    me = lax.axis_index("chan")
    for copy in load_shards(1, near, far, w2, [me ^ m for m in range(4)], sem):
        copy.wait()
    for pair in range(2):
        acc[pair] = conv_pair(pad, pair, w2)
        finish(acc, shift[1:2, :], tab, pair, slots)
    for b in range(4):
        brick = slots[b].reshape(512, 128).astype(BF16).T
        for g in range(4):
            turned[g, b] = brick[32 * g : 32 * g + 32]
    for m in range(4):
        outs[m][...] = turned[me ^ m]


def convolve_second(tables, pad, shift, near, far):
    piece = jax.ShapeDtypeStruct((4, 32, 512), BF16)
    return pl.pallas_call(
        second_kernel,
        out_shape=[piece] * 4,
        in_specs=[SMEM, VMEM, VMEM] + [HBM] * 6,
        out_specs=[VMEM] * 4,
        scratch_shapes=[
            pltpu.VMEM((27, 128, 128), BF16),
            pltpu.VMEM((4, 8, 8, 8, 128), F32),
            pltpu.VMEM((2, 512, 256), F32),
            pltpu.VMEM((4, 4, 32, 512), BF16),
            pltpu.SemaphoreType.DMA((4,)),
        ],
        compiler_params=pltpu.CompilerParams(vmem_limit_bytes=24 << 20),
        cost_estimate=pl.CostEstimate(flops=4 * 10**9, bytes_accessed=4 * 10**6, transcendentals=10**6),
        name="convolve_second",
    )(tables, pad, shift, *near, *far)


def join_kernel(*refs):
    pieces, out, sem = refs[:4], refs[4], refs[5]
    me = lax.axis_index("chan")
    copies = [pltpu.make_async_copy(pieces[m], out.at[me ^ m], sem.at[m]) for m in range(4)]
    for copy in copies:
        copy.start()
    for copy in copies:
        copy.wait()


def join(pieces):
    return pl.pallas_call(
        join_kernel,
        out_shape=jax.ShapeDtypeStruct((4, 4, 32, 512), BF16),
        in_specs=[HBM] * 4,
        out_specs=HBM,
        scratch_shapes=[pltpu.SemaphoreType.DMA((4,))],
        compiler_params=pltpu.CompilerParams(vmem_limit_bytes=8 << 20),
        name="join_levels",
    )(*pieces)


def swap(value, m):
    return lax.ppermute(value, "chan", [(i, i ^ m) for i in range(4)])


def swap_slabs(value, step, m):
    count = lax.axis_size("slab")
    pairs = [(4 * s + g, 4 * (s ^ step) + (g ^ m)) for s in range(count) for g in range(4)]
    return lax.ppermute(value, ("slab", "chan"), pairs)


def swap_faces(value, first):
    count = lax.axis_size("slab")
    partner = [((s + first) ^ 1) - first for s in range(count)]
    return lax.ppermute(value, "slab", [(s, p if 0 <= p < count else s) for s, p in enumerate(partner)])


def shards(features, neighbours, face_lists, w_first, b_first, w_second, b_second, level_embed):
    w1, w2 = w_first.transpose(0, 2, 1), w_second.transpose(0, 2, 1)
    fetched = swap(jnp.where(layer_of_slab() == 0, w1, w2), 2)
    own, one, two, three, tables = split(
        features, neighbours, face_lists, b_first, b_second, level_embed
    )
    fetched, one, two, three = lax.optimization_barrier(
        (fetched, swap(one, 1), swap(two, 2), swap(three, 3))
    )
    pieces = [own, one, two, three]
    far = [fetched, swap(fetched, 1), swap_slabs(fetched, 1, 0), swap_slabs(fetched, 8, 1)]
    sides = faces(tables, pieces)
    sides = [swap_faces(sides[i], i) for i in range(2)]
    pad, shift = convolve_first(tables, pieces, sides, (w1, swap(w1, 1)), far)
    outs = convolve_second(tables, pad, shift, (w2, swap(w2, 1)), far)
    return join([outs[0]] + [swap(outs[m], m) for m in (1, 2, 3)])


def solution(mesh):
    placed = (
        P(None, "slab", "chan", None),
        P("slab", None),
        P("slab", None, None),
        P(None, None, "chan"),
        P("chan"),
        P(None, None, "chan"),
        P("chan"),
        P(None, "chan"),
    )
    return jax.shard_map(
        shards, mesh=mesh, in_specs=placed, out_specs=P(None, "slab", "chan", None), check_vma=False
    )
```

```python
import jax
import jax.numpy as jnp
from jax import lax
from jax.experimental import pallas as pl
from jax.experimental.pallas import tpu as pltpu
from jax.sharding import PartitionSpec as P

BF16, F32 = jnp.bfloat16, jnp.float32
NONE = 8
HBM = pl.BlockSpec(memory_space=pl.ANY)
VMEM = pl.BlockSpec(memory_space=pltpu.VMEM)
SMEM = pl.BlockSpec(memory_space=pltpu.SMEM)
SPAN = {-1: (7, 0, 1), 0: (0, 1, 8), 1: (0, 9, 1)}


def offset(dz, dy, dx):
    return 9 * (dz + 1) + 3 * (dy + 1) + (dx + 1)


PIECE = 17


def split_kernel(feat, small, *refs):
    pieces, tables = refs[:4], refs[4]
    me = lax.axis_index("chan")
    values = small[pl.ds(0, 8), pl.ds(0, 32)]
    values = jnp.concatenate([values] * 4, axis=1)
    lane = lax.broadcasted_iota(jnp.int32, (8, 128), 1)
    values = jnp.where(lane // 32 == me, values, 0.0)
    high = values.astype(BF16).astype(F32)
    values = jnp.concatenate([high, values - high, jnp.zeros((16, 128), F32)], axis=0).astype(BF16)
    for m in range(4):
        for b in range(4):
            for v in range(4):
                pieces[m][4 * v + b] = feat[me ^ m, b, :, 128 * v : 128 * v + 128]
        pieces[m][16] = values
    sent = small[pl.ds(8, 8), :]
    tables[...] = sent.astype(jnp.int32)
    pieces[0][17] = jnp.concatenate([sent, jnp.zeros((24, 128), F32)], axis=0).astype(BF16)


def in_rows(array, first, count):
    array = array.reshape(-1, array.shape[-1]).astype(F32)
    rows, lanes = array.shape
    return jnp.pad(array, ((first, count - first - rows), (0, 128 - lanes)))


def split(features, neighbours, face_lists, b1, b2, lev):
    small = [(b1, 0), (b2, 1), (lev, 2), (neighbours, 8), (face_lists, 12)]
    small = sum(in_rows(array, first, 16) for array, first in small)
    piece = jax.ShapeDtypeStruct((PIECE, 32, 128), BF16)
    kept = jax.ShapeDtypeStruct((PIECE + 1, 32, 128), BF16)
    return pl.pallas_call(
        split_kernel,
        out_shape=[kept, piece, piece, piece, jax.ShapeDtypeStruct((8, 128), jnp.int32)],
        in_specs=[VMEM] * 2,
        out_specs=[VMEM] * 5,
        compiler_params=pltpu.CompilerParams(vmem_limit_bytes=8 << 20),
        name="split_features",
    )(features, small)


def faces_kernel(tables, *refs):
    pieces, sides, sem = refs[:4], refs[4:6], refs[6]
    odd = lax.axis_index("slab") % 2
    copies = []
    for i, out in enumerate(sides):
        tier = (odd + 1 + i) % 2
        for c in range(2):
            b = jnp.maximum(tables[4 + tier, c], 0)
            for m in range(4):
                source = pieces[m].at[12 * tier + b]
                copies.append(pltpu.make_async_copy(source, out.at[4 * c + m], sem.at[8 * i + 4 * c + m]))
        copies.append(pltpu.make_async_copy(pieces[0].at[17], out.at[8], sem.at[16 + i]))
    for copy in copies:
        copy.start()
    for copy in copies:
        copy.wait()


def faces(tables, pieces):
    side = jax.ShapeDtypeStruct((9, 32, 128), BF16)
    return pl.pallas_call(
        faces_kernel,
        out_shape=[side] * 2,
        in_specs=[SMEM] + [HBM] * 4,
        out_specs=[VMEM] * 2,
        scratch_shapes=[pltpu.SemaphoreType.DMA((18,))],
        compiler_params=pltpu.CompilerParams(vmem_limit_bytes=4 << 20),
        name="pick_faces",
    )(tables, *pieces)


def silu(v):
    return v / (1.0 + jnp.exp(-v))


def gather_padded(slots, pad, lead, slot, planes):
    x = lax.broadcasted_iota(jnp.int32, (1, 8, 128), 1)
    for dz, z_from, z_to in planes:
        for dy in (-1, 0, 1):
            y_from, y_to, n = SPAN[dy]
            parts = ([], [], [])
            for w in range(2):
                mid, left, right = (
                    slots[slot(w, offset(dz, dy, dx)), z_from, y_from : y_from + n] for dx in (0, -1, 1)
                )
                parts[0].append(pltpu.roll(jnp.where(x == 7, left, mid), 1, 1))
                parts[1].append(mid)
                parts[2].append(pltpu.roll(jnp.where(x == 0, right, mid), 7, 1))
            for d in range(3):
                tile = jnp.concatenate(parts[d], axis=1).astype(BF16)
                pad[lead, z_to, y_to : y_to + n, :, 128 * d : 128 * d + 128] = tile


OWN_PLANES = [(-1, 7, 0)] + [(0, z, z + 1) for z in range(8)] + [(1, 0, 9)]


def conv_pair(pad, lead, w):
    zero = jnp.zeros((128, 128), BF16)
    total = None
    blocks = [(zin, dy) for zin in range(4) for dy in range(3)]
    for first in range(0, 12, 2):
        left, right = [], []
        for zin, dy in blocks[first : first + 2]:
            planes = [pad[lead, zin + 2 * j, dy : dy + 8].reshape(128, 384) for j in range(4)]
            left.append(jnp.concatenate(planes, axis=0))
            for dx in range(3):
                even = w[9 * zin + 3 * dy + dx] if zin < 3 else zero
                odd = w[9 * (zin - 1) + 3 * dy + dx] if zin > 0 else zero
                right.append(jnp.concatenate([even, odd], axis=1))
        part = jnp.dot(
            jnp.concatenate(left, axis=1), jnp.concatenate(right, axis=0), preferred_element_type=F32
        )
        total = part if total is None else total + part
    return total


def conv_face(pad, w):
    total = None
    blocks = [(dz, dy) for dz in range(3) for dy in range(3)]
    for group in (blocks[0:2], blocks[2:4], blocks[4:6], blocks[6:9]):
        left, right = [], []
        for dz, dy in group:
            sides = [pad[side, dz, dy : dy + 8].reshape(128, 384) for side in range(2)]
            left.append(jnp.concatenate(sides, axis=0))
            right += [w[9 * dz + 3 * dy + dx] for dx in range(3)]
        part = jnp.dot(
            jnp.concatenate(left, axis=1), jnp.concatenate(right, axis=0), preferred_element_type=F32
        )
        total = part if total is None else total + part
    return total


def load_shards(sources, weights, order, sem):
    return [
        pltpu.make_async_copy(
            source, weights.at[:, pl.ds(pl.multiple_of(32 * order[m], 32), 32), :], sem.at[m]
        )
        for m, source in enumerate(sources)
    ]


def finish(acc, moved, tab, pair, slots):
    for j in range(4):
        for zo in range(2):
            tile = silu(acc[pair, 128 * j : 128 * j + 128, 128 * zo : 128 * zo + 128] + moved)
            tile = tile.reshape(8, 2, 8, 128)
            for w in range(2):
                b = 2 * pair + w
                slots[b, 2 * j + zo] = jnp.where(tab[b, 13] >= 0, tile[:, w], 0.0)


def first_kernel(tab, *refs):
    feat, sides, shards = refs[0:4], refs[4:6], refs[6:10]
    pad_out, shift = refs[10:12]
    fs, hs, w1, bias, sent, sent_int, tables, slots, pad, pad_face, acc, sem = refs[12:]
    me = lax.axis_index("chan")

    f_copies, t_copies = [], []
    for i in range(2):
        side = (lax.axis_index("slab") + 1 + i) % 2
        t_copies.append(pltpu.make_async_copy(sides[i].at[8, pl.ds(0, 16)], sent.at[side], sem.at[i]))
        f_copies.append(pltpu.make_async_copy(sides[i].at[pl.ds(0, 8)], hs.at[side], sem.at[2 + i]))
    for m in range(4):
        f_copies.append(pltpu.make_async_copy(feat[m].at[pl.ds(0, 16)], fs.at[m], sem.at[4 + m]))
        f_copies.append(pltpu.make_async_copy(feat[m].at[16, pl.ds(0, 16)], bias.at[m], sem.at[8 + m]))
    w_copies = [
        pltpu.make_async_copy(shards[m], w1.at[:, pl.ds(32 * m, 32), :], sem.at[12 + m]) for m in range(4)
    ]
    for copy in t_copies + f_copies + w_copies:
        copy.start()
    for copy in t_copies:
        copy.wait()
    sent_int[...] = sent[...].astype(F32).astype(jnp.int32).reshape(32, 128)
    to_scalars = pltpu.make_async_copy(sent_int, tables, sem.at[16])
    to_scalars.start()
    for copy in f_copies:
        copy.wait()

    slots[NONE] = jnp.zeros((8, 8, 8, 128), F32)
    for b in range(4):
        for v in range(4):
            brick = jnp.concatenate([fs[m, 4 * v + b] for m in range(4)], axis=0)
            slots[b, 2 * v : 2 * v + 2] = brick.T.astype(F32).reshape(2, 8, 8, 128)
    for side in range(2):
        for c in range(2):
            face = jnp.concatenate([hs[side, 4 * c + m] for m in range(4)], axis=0)
            first = 6 if side == 0 else 0
            slots[4 + 2 * side + c, first : first + 2] = face.T.astype(F32).reshape(2, 8, 8, 128)

    to_scalars.wait()

    def own(pair):
        def slot(w, k):
            t = tab[2 * pair + w, k]
            return jnp.where(t < 0, NONE, t)

        return slot

    def below(c, k):
        t = tables[0 + jnp.maximum(tables[5, c], 0), k]
        if k < 18:
            found = jnp.where(t == tables[5, 0], 4, jnp.where(t == tables[5, 1], 5, NONE))
            return jnp.where(t < 0, NONE, found)
        u = tab[4, jnp.clip(t - 6, 0, 1)]
        return jnp.where((t < 6) | (u < 0), NONE, u)

    def above(c, k):
        t = tables[16 + jnp.maximum(tables[20, c], 0), k]
        if k >= 9:
            found = jnp.where(t == tables[20, 0], 6, jnp.where(t == tables[20, 1], 7, NONE))
            return jnp.where(t < 0, NONE, found)
        u = tab[5, jnp.clip(t - 4, 0, 1)]
        return jnp.where((t < 4) | (t > 5) | (u < 0), NONE, u)

    gather_padded(slots, pad_face, 0, below, [(0, 6, 0), (0, 7, 1), (1, 0, 2)])
    gather_padded(slots, pad_face, 1, above, [(-1, 7, 0), (0, 0, 1), (0, 1, 2)])
    for pair in range(2):
        gather_padded(slots, pad, pair, own(pair), OWN_PLANES)

    values = sum(bias[m].astype(F32) for m in range(4))
    shift[...] = values[0:8] + values[8:16]
    moved = shift[0:1, :] + shift[pl.ds(2 + me, 1), :]
    for copy in w_copies:
        copy.wait()

    for pair in range(2):
        acc[pair] = conv_pair(pad, pair, w1)
        finish(acc, moved, tab, pair, slots)
    sides_out = silu(conv_face(pad_face, w1) + moved).reshape(2, 8, 2, 8, 128)
    for c in range(2):
        slots[4 + c, 7] = sides_out[0, :, c]
        slots[6 + c, 0] = sides_out[1, :, c]
    for pair in range(2):
        gather_padded(slots, pad_out, pair, own(pair), OWN_PLANES)


def convolve_first(tables, feat, sides, shards):
    return pl.pallas_call(
        first_kernel,
        out_shape=[jax.ShapeDtypeStruct((2, 10, 10, 16, 384), BF16), jax.ShapeDtypeStruct((8, 128), F32)],
        in_specs=[SMEM] + [HBM] * 10,
        out_specs=[VMEM] * 2,
        scratch_shapes=[
            pltpu.VMEM((4, 16, 32, 128), BF16),
            pltpu.VMEM((2, 8, 32, 128), BF16),
            pltpu.VMEM((27, 128, 128), BF16),
            pltpu.VMEM((4, 16, 128), BF16),
            pltpu.VMEM((2, 16, 128), BF16),
            pltpu.VMEM((32, 128), jnp.int32),
            pltpu.SMEM((32, 128), jnp.int32),
            pltpu.VMEM((9, 8, 8, 8, 128), F32),
            pltpu.VMEM((2, 10, 10, 16, 384), BF16),
            pltpu.VMEM((2, 3, 10, 16, 384), BF16),
            pltpu.VMEM((2, 512, 256), F32),
            pltpu.SemaphoreType.DMA((17,)),
        ],
        compiler_params=pltpu.CompilerParams(vmem_limit_bytes=24 << 20),
        cost_estimate=pl.CostEstimate(flops=5 * 10**9, bytes_accessed=4 * 10**6, transcendentals=10**6),
        name="convolve_first",
    )(tables, *feat, *sides, *shards)


def second_kernel(tab, pad, shift, *refs):
    shards, outs = refs[0:4], refs[4:8]
    w2, slots, acc, turned, sem = refs[8:]
    me = lax.axis_index("chan")
    w_copies = load_shards(shards, w2, [me ^ m for m in range(4)], sem)
    for copy in w_copies:
        copy.start()
    for copy in w_copies:
        copy.wait()
    for pair in range(2):
        acc[pair] = conv_pair(pad, pair, w2)
        finish(acc, shift[1:2, :], tab, pair, slots)
    for b in range(4):
        brick = slots[b].reshape(512, 128).astype(BF16).T
        for g in range(4):
            turned[g, b] = brick[32 * g : 32 * g + 32]
    for m in range(4):
        outs[m][...] = turned[me ^ m]


def convolve_second(tables, pad, shift, shards):
    piece = jax.ShapeDtypeStruct((4, 32, 512), BF16)
    return pl.pallas_call(
        second_kernel,
        out_shape=[piece] * 4,
        in_specs=[SMEM, VMEM, VMEM] + [HBM] * 4,
        out_specs=[VMEM] * 4,
        scratch_shapes=[
            pltpu.VMEM((27, 128, 128), BF16),
            pltpu.VMEM((4, 8, 8, 8, 128), F32),
            pltpu.VMEM((2, 512, 256), F32),
            pltpu.VMEM((4, 4, 32, 512), BF16),
            pltpu.SemaphoreType.DMA((4,)),
        ],
        compiler_params=pltpu.CompilerParams(vmem_limit_bytes=24 << 20),
        cost_estimate=pl.CostEstimate(flops=4 * 10**9, bytes_accessed=4 * 10**6, transcendentals=10**6),
        name="convolve_second",
    )(tables, pad, shift, *shards)


def join_kernel(*refs):
    pieces, out, sem = refs[:4], refs[4], refs[5]
    me = lax.axis_index("chan")
    copies = [pltpu.make_async_copy(pieces[m], out.at[me ^ m], sem.at[m]) for m in range(4)]
    for copy in copies:
        copy.start()
    for copy in copies:
        copy.wait()


def join(pieces):
    return pl.pallas_call(
        join_kernel,
        out_shape=jax.ShapeDtypeStruct((4, 4, 32, 512), BF16),
        in_specs=[HBM] * 4,
        out_specs=HBM,
        scratch_shapes=[pltpu.SemaphoreType.DMA((4,))],
        compiler_params=pltpu.CompilerParams(vmem_limit_bytes=8 << 20),
        name="join_levels",
    )(*pieces)


def swap(value, m):
    return lax.ppermute(value, "chan", [(i, i ^ m) for i in range(4)])


def swap_faces(value, first):
    count = lax.axis_size("slab")
    partner = [((s + first) ^ 1) - first for s in range(count)]
    return lax.ppermute(value, "slab", [(s, p if 0 <= p < count else s) for s, p in enumerate(partner)])


def shards(features, neighbours, face_lists, w_first, b_first, w_second, b_second, level_embed):
    w1, w2 = w_first.transpose(0, 2, 1), w_second.transpose(0, 2, 1)
    far = swap(w1, 2)
    own, one, two, three, tables = split(
        features, neighbours, face_lists, b_first, b_second, level_embed
    )
    far, one, two, three, later = lax.optimization_barrier(
        (far, swap(one, 1), swap(two, 2), swap(three, 3), w2)
    )
    pieces = [own, one, two, three]
    first = [w1, swap(w1, 1), far, swap(far, 1)]
    sides = faces(tables, pieces)
    sides = [swap_faces(sides[i], i) for i in range(2)]
    second = [w2] + [swap(later, m) for m in (1, 2, 3)]
    pad, shift = convolve_first(tables, pieces, sides, first)
    outs = convolve_second(tables, pad, shift, second)
    return join([outs[0]] + [swap(outs[m], m) for m in (1, 2, 3)])


def solution(mesh):
    placed = (
        P(None, "slab", "chan", None),
        P("slab", None),
        P("slab", None, None),
        P(None, None, "chan"),
        P("chan"),
        P(None, None, "chan"),
        P("chan"),
        P(None, "chan"),
    )
    return jax.shard_map(
        shards, mesh=mesh, in_specs=placed, out_specs=P(None, "slab", "chan", None), check_vma=False
    )
```

```python
import jax
import jax.numpy as jnp
from jax import lax
from jax.experimental import pallas as pl
from jax.experimental.pallas import tpu as pltpu
from jax.sharding import PartitionSpec as P

BF16, F32 = jnp.bfloat16, jnp.float32
NONE = 8
HBM = pl.BlockSpec(memory_space=pl.ANY)
VMEM = pl.BlockSpec(memory_space=pltpu.VMEM)
SMEM = pl.BlockSpec(memory_space=pltpu.SMEM)
SPAN = {-1: (7, 0, 1), 0: (0, 1, 8), 1: (0, 9, 1)}


def offset(dz, dy, dx):
    return 9 * (dz + 1) + 3 * (dy + 1) + (dx + 1)


PIECE = 17


def split_kernel(feat, small, *refs):
    pieces, tables = refs[:4], refs[4]
    me = lax.axis_index("chan")
    values = small[pl.ds(0, 8), pl.ds(0, 32)]
    values = jnp.concatenate([values] * 4, axis=1)
    lane = lax.broadcasted_iota(jnp.int32, (8, 128), 1)
    values = jnp.where(lane // 32 == me, values, 0.0)
    high = values.astype(BF16).astype(F32)
    values = jnp.concatenate([high, values - high, jnp.zeros((16, 128), F32)], axis=0).astype(BF16)
    for m in range(4):
        for b in range(4):
            for v in range(4):
                pieces[m][4 * v + b] = feat[me ^ m, b, :, 128 * v : 128 * v + 128]
        pieces[m][16] = values
    sent = small[pl.ds(8, 8), :]
    tables[...] = sent.astype(jnp.int32)
    pieces[0][17] = jnp.concatenate([sent, jnp.zeros((24, 128), F32)], axis=0).astype(BF16)


def in_rows(array, first, count):
    array = array.reshape(-1, array.shape[-1]).astype(F32)
    rows, lanes = array.shape
    return jnp.pad(array, ((first, count - first - rows), (0, 128 - lanes)))


def split(features, neighbours, face_lists, b1, b2, lev):
    small = [(b1, 0), (b2, 1), (lev, 2), (neighbours, 8), (face_lists, 12)]
    small = sum(in_rows(array, first, 16) for array, first in small)
    piece = jax.ShapeDtypeStruct((PIECE, 32, 128), BF16)
    kept = jax.ShapeDtypeStruct((PIECE + 1, 32, 128), BF16)
    return pl.pallas_call(
        split_kernel,
        out_shape=[kept, piece, piece, piece, jax.ShapeDtypeStruct((8, 128), jnp.int32)],
        in_specs=[VMEM] * 2,
        out_specs=[VMEM] * 5,
        compiler_params=pltpu.CompilerParams(vmem_limit_bytes=8 << 20),
        name="split_features",
    )(features, small)


def faces_kernel(tables, *refs):
    pieces, sides = refs[:4], refs[4:6]
    odd = lax.axis_index("slab") % 2
    for i, out in enumerate(sides):
        tier = (odd + 1 + i) % 2
        for c in range(2):
            b = jnp.maximum(tables[4 + tier, c], 0)
            for m in range(4):
                out[4 * c + m] = pieces[m][12 * tier + b]
        out[8] = pieces[0][17]


def faces(tables, pieces):
    side = jax.ShapeDtypeStruct((9, 32, 128), BF16)
    return pl.pallas_call(
        faces_kernel,
        out_shape=[side] * 2,
        in_specs=[SMEM] + [VMEM] * 4,
        out_specs=[VMEM] * 2,
        compiler_params=pltpu.CompilerParams(vmem_limit_bytes=4 << 20),
        name="pick_faces",
    )(tables, *pieces)


def silu(v):
    return v / (1.0 + jnp.exp(-v))


def gather_padded(slots, pad, lead, slot, planes):
    x = lax.broadcasted_iota(jnp.int32, (1, 8, 128), 1)
    for dz, z_from, z_to in planes:
        for dy in (-1, 0, 1):
            y_from, y_to, n = SPAN[dy]
            parts = ([], [], [])
            for w in range(2):
                mid, left, right = (
                    slots[slot(w, offset(dz, dy, dx)), z_from, y_from : y_from + n] for dx in (0, -1, 1)
                )
                parts[0].append(pltpu.roll(jnp.where(x == 7, left, mid), 1, 1))
                parts[1].append(mid)
                parts[2].append(pltpu.roll(jnp.where(x == 0, right, mid), 7, 1))
            for d in range(3):
                tile = jnp.concatenate(parts[d], axis=1).astype(BF16)
                pad[lead, z_to, y_to : y_to + n, :, 128 * d : 128 * d + 128] = tile


OWN_PLANES = [(-1, 7, 0)] + [(0, z, z + 1) for z in range(8)] + [(1, 0, 9)]


def conv_pair(pad, lead, w):
    zero = jnp.zeros((128, 128), BF16)
    total = None
    blocks = [(zin, dy) for zin in range(4) for dy in range(3)]
    for first in range(0, 12, 2):
        left, right = [], []
        for zin, dy in blocks[first : first + 2]:
            planes = [pad[lead, zin + 2 * j, dy : dy + 8].reshape(128, 384) for j in range(4)]
            left.append(jnp.concatenate(planes, axis=0))
            for dx in range(3):
                even = w[9 * zin + 3 * dy + dx] if zin < 3 else zero
                odd = w[9 * (zin - 1) + 3 * dy + dx] if zin > 0 else zero
                right.append(jnp.concatenate([even, odd], axis=1))
        part = jnp.dot(
            jnp.concatenate(left, axis=1), jnp.concatenate(right, axis=0), preferred_element_type=F32
        )
        total = part if total is None else total + part
    return total


def conv_face(pad, w):
    total = None
    blocks = [(dz, dy) for dz in range(3) for dy in range(3)]
    for group in (blocks[0:2], blocks[2:4], blocks[4:6], blocks[6:9]):
        left, right = [], []
        for dz, dy in group:
            sides = [pad[side, dz, dy : dy + 8].reshape(128, 384) for side in range(2)]
            left.append(jnp.concatenate(sides, axis=0))
            right += [w[9 * dz + 3 * dy + dx] for dx in range(3)]
        part = jnp.dot(
            jnp.concatenate(left, axis=1), jnp.concatenate(right, axis=0), preferred_element_type=F32
        )
        total = part if total is None else total + part
    return total


def load_shards(sources, weights, order, sem):
    return [
        pltpu.make_async_copy(
            source, weights.at[:, pl.ds(pl.multiple_of(32 * order[m], 32), 32), :], sem.at[m]
        )
        for m, source in enumerate(sources)
    ]


def finish(acc, moved, tab, pair, slots):
    for j in range(4):
        for zo in range(2):
            tile = silu(acc[pair, 128 * j : 128 * j + 128, 128 * zo : 128 * zo + 128] + moved)
            tile = tile.reshape(8, 2, 8, 128)
            for w in range(2):
                b = 2 * pair + w
                slots[b, 2 * j + zo] = jnp.where(tab[b, 13] >= 0, tile[:, w], 0.0)


def first_kernel(tab, *refs):
    feat, sides, shards = refs[0:4], refs[4:6], refs[6:10]
    pad_out, shift = refs[10:12]
    hs, w1, sent, sent_int, tables, slots, pad, pad_face, acc, sem = refs[12:]
    me = lax.axis_index("chan")

    f_copies, t_copies = [], []
    for i in range(2):
        side = (lax.axis_index("slab") + 1 + i) % 2
        t_copies.append(pltpu.make_async_copy(sides[i].at[8, pl.ds(0, 16)], sent.at[side], sem.at[i]))
        f_copies.append(pltpu.make_async_copy(sides[i].at[pl.ds(0, 8)], hs.at[side], sem.at[2 + i]))
    w_copies = [
        pltpu.make_async_copy(shards[m], w1.at[:, pl.ds(32 * m, 32), :], sem.at[12 + m]) for m in range(4)
    ]
    for copy in t_copies + f_copies + w_copies:
        copy.start()
    for copy in t_copies:
        copy.wait()
    sent_int[...] = sent[...].astype(F32).astype(jnp.int32).reshape(32, 128)
    to_scalars = pltpu.make_async_copy(sent_int, tables, sem.at[16])
    to_scalars.start()
    for copy in f_copies:
        copy.wait()

    slots[NONE] = jnp.zeros((8, 8, 8, 128), F32)
    for b in range(4):
        for v in range(4):
            brick = jnp.concatenate([feat[m][4 * v + b] for m in range(4)], axis=0)
            slots[b, 2 * v : 2 * v + 2] = brick.T.astype(F32).reshape(2, 8, 8, 128)
    for side in range(2):
        for c in range(2):
            face = jnp.concatenate([hs[side, 4 * c + m] for m in range(4)], axis=0)
            first = 6 if side == 0 else 0
            slots[4 + 2 * side + c, first : first + 2] = face.T.astype(F32).reshape(2, 8, 8, 128)

    to_scalars.wait()

    def own(pair):
        def slot(w, k):
            t = tab[2 * pair + w, k]
            return jnp.where(t < 0, NONE, t)

        return slot

    def below(c, k):
        t = tables[0 + jnp.maximum(tables[5, c], 0), k]
        if k < 18:
            found = jnp.where(t == tables[5, 0], 4, jnp.where(t == tables[5, 1], 5, NONE))
            return jnp.where(t < 0, NONE, found)
        u = tab[4, jnp.clip(t - 6, 0, 1)]
        return jnp.where((t < 6) | (u < 0), NONE, u)

    def above(c, k):
        t = tables[16 + jnp.maximum(tables[20, c], 0), k]
        if k >= 9:
            found = jnp.where(t == tables[20, 0], 6, jnp.where(t == tables[20, 1], 7, NONE))
            return jnp.where(t < 0, NONE, found)
        u = tab[5, jnp.clip(t - 4, 0, 1)]
        return jnp.where((t < 4) | (t > 5) | (u < 0), NONE, u)

    gather_padded(slots, pad_face, 0, below, [(0, 6, 0), (0, 7, 1), (1, 0, 2)])
    gather_padded(slots, pad_face, 1, above, [(-1, 7, 0), (0, 0, 1), (0, 1, 2)])
    for pair in range(2):
        gather_padded(slots, pad, pair, own(pair), OWN_PLANES)

    values = sum(feat[m][16, pl.ds(0, 16), :].astype(F32) for m in range(4))
    shift[...] = values[0:8] + values[8:16]
    moved = shift[0:1, :] + shift[pl.ds(2 + me, 1), :]
    for copy in w_copies:
        copy.wait()

    for pair in range(2):
        acc[pair] = conv_pair(pad, pair, w1)
        finish(acc, moved, tab, pair, slots)
    sides_out = silu(conv_face(pad_face, w1) + moved).reshape(2, 8, 2, 8, 128)
    for c in range(2):
        slots[4 + c, 7] = sides_out[0, :, c]
        slots[6 + c, 0] = sides_out[1, :, c]
    for pair in range(2):
        gather_padded(slots, pad_out, pair, own(pair), OWN_PLANES)


def convolve_first(tables, feat, sides, shards):
    return pl.pallas_call(
        first_kernel,
        out_shape=[jax.ShapeDtypeStruct((2, 10, 10, 16, 384), BF16), jax.ShapeDtypeStruct((8, 128), F32)],
        in_specs=[SMEM] + [VMEM] * 4 + [HBM] * 6,
        out_specs=[VMEM] * 2,
        scratch_shapes=[
            pltpu.VMEM((2, 8, 32, 128), BF16),
            pltpu.VMEM((27, 128, 128), BF16),
            pltpu.VMEM((2, 16, 128), BF16),
            pltpu.VMEM((32, 128), jnp.int32),
            pltpu.SMEM((32, 128), jnp.int32),
            pltpu.VMEM((9, 8, 8, 8, 128), F32),
            pltpu.VMEM((2, 10, 10, 16, 384), BF16),
            pltpu.VMEM((2, 3, 10, 16, 384), BF16),
            pltpu.VMEM((2, 512, 256), F32),
            pltpu.SemaphoreType.DMA((17,)),
        ],
        compiler_params=pltpu.CompilerParams(vmem_limit_bytes=24 << 20),
        cost_estimate=pl.CostEstimate(flops=5 * 10**9, bytes_accessed=4 * 10**6, transcendentals=10**6),
        name="convolve_first",
    )(tables, *feat, *sides, *shards)


def second_kernel(tab, pad, shift, *refs):
    shards, outs = refs[0:4], refs[4:8]
    w2, slots, acc, turned, sem = refs[8:]
    me = lax.axis_index("chan")
    w_copies = load_shards(shards, w2, [me ^ m for m in range(4)], sem)
    for copy in w_copies:
        copy.start()
    for copy in w_copies:
        copy.wait()
    for pair in range(2):
        acc[pair] = conv_pair(pad, pair, w2)
        finish(acc, shift[1:2, :], tab, pair, slots)
    for b in range(4):
        brick = slots[b].reshape(512, 128).astype(BF16).T
        for g in range(4):
            turned[g, b] = brick[32 * g : 32 * g + 32]
    for m in range(4):
        outs[m][...] = turned[me ^ m]


def convolve_second(tables, pad, shift, shards):
    piece = jax.ShapeDtypeStruct((4, 32, 512), BF16)
    return pl.pallas_call(
        second_kernel,
        out_shape=[piece] * 4,
        in_specs=[SMEM, VMEM, VMEM] + [HBM] * 4,
        out_specs=[VMEM] * 4,
        scratch_shapes=[
            pltpu.VMEM((27, 128, 128), BF16),
            pltpu.VMEM((4, 8, 8, 8, 128), F32),
            pltpu.VMEM((2, 512, 256), F32),
            pltpu.VMEM((4, 4, 32, 512), BF16),
            pltpu.SemaphoreType.DMA((4,)),
        ],
        compiler_params=pltpu.CompilerParams(vmem_limit_bytes=24 << 20),
        cost_estimate=pl.CostEstimate(flops=4 * 10**9, bytes_accessed=4 * 10**6, transcendentals=10**6),
        name="convolve_second",
    )(tables, pad, shift, *shards)


def join_kernel(*refs):
    pieces, out, sem = refs[:4], refs[4], refs[5]
    me = lax.axis_index("chan")
    copies = [pltpu.make_async_copy(pieces[m], out.at[me ^ m], sem.at[m]) for m in range(4)]
    for copy in copies:
        copy.start()
    for copy in copies:
        copy.wait()


def join(pieces):
    return pl.pallas_call(
        join_kernel,
        out_shape=jax.ShapeDtypeStruct((4, 4, 32, 512), BF16),
        in_specs=[HBM] * 4,
        out_specs=HBM,
        scratch_shapes=[pltpu.SemaphoreType.DMA((4,))],
        compiler_params=pltpu.CompilerParams(vmem_limit_bytes=8 << 20),
        name="join_levels",
    )(*pieces)


def swap(value, m):
    return lax.ppermute(value, "chan", [(i, i ^ m) for i in range(4)])


def swap_faces(value, first):
    count = lax.axis_size("slab")
    partner = [((s + first) ^ 1) - first for s in range(count)]
    return lax.ppermute(value, "slab", [(s, p if 0 <= p < count else s) for s, p in enumerate(partner)])


def shards(features, neighbours, face_lists, w_first, b_first, w_second, b_second, level_embed):
    w1, w2 = w_first.transpose(0, 2, 1), w_second.transpose(0, 2, 1)
    far = swap(w1, 2)
    own, one, two, three, tables = split(
        features, neighbours, face_lists, b_first, b_second, level_embed
    )
    far, one, two, three, later = lax.optimization_barrier(
        (far, swap(one, 1), swap(two, 2), swap(three, 3), w2)
    )
    pieces = [own, one, two, three]
    first = [w1, swap(w1, 1), far, swap(far, 1)]
    sides = faces(tables, pieces)
    sides = [swap_faces(sides[i], i) for i in range(2)]
    second = [w2] + [swap(later, m) for m in (1, 2, 3)]
    pad, shift = convolve_first(tables, pieces, sides, first)
    outs = convolve_second(tables, pad, shift, second)
    return join([outs[0]] + [swap(outs[m], m) for m in (1, 2, 3)])


def solution(mesh):
    placed = (
        P(None, "slab", "chan", None),
        P("slab", None),
        P("slab", None, None),
        P(None, None, "chan"),
        P("chan"),
        P(None, None, "chan"),
        P("chan"),
        P(None, "chan"),
    )
    return jax.shard_map(
        shards, mesh=mesh, in_specs=placed, out_specs=P(None, "slab", "chan", None), check_vma=False
    )
```

```python
import jax
import jax.numpy as jnp
from jax import lax
from jax.experimental import pallas as pl
from jax.experimental.pallas import tpu as pltpu
from jax.sharding import PartitionSpec as P

BF16, F32 = jnp.bfloat16, jnp.float32
NONE = 8
HBM = pl.BlockSpec(memory_space=pl.ANY)
VMEM = pl.BlockSpec(memory_space=pltpu.VMEM)
SMEM = pl.BlockSpec(memory_space=pltpu.SMEM)
SPAN = {-1: (7, 0, 1), 0: (0, 1, 8), 1: (0, 9, 1)}


def offset(dz, dy, dx):
    return 9 * (dz + 1) + 3 * (dy + 1) + (dx + 1)


PIECE = 17


def split_kernel(feat, small, *refs):
    pieces, tables = refs[:4], refs[4]
    me = lax.axis_index("chan")
    values = small[pl.ds(0, 8), pl.ds(0, 32)]
    values = jnp.concatenate([values] * 4, axis=1)
    lane = lax.broadcasted_iota(jnp.int32, (8, 128), 1)
    values = jnp.where(lane // 32 == me, values, 0.0)
    high = values.astype(BF16).astype(F32)
    values = jnp.concatenate([high, values - high, jnp.zeros((16, 128), F32)], axis=0).astype(BF16)
    for m in range(4):
        for b in range(4):
            for v in range(4):
                pieces[m][4 * v + b] = feat[me ^ m, b, :, 128 * v : 128 * v + 128]
        pieces[m][16] = values
    sent = small[pl.ds(8, 8), :]
    tables[...] = sent.astype(jnp.int32)
    pieces[0][17] = jnp.concatenate([sent, jnp.zeros((24, 128), F32)], axis=0).astype(BF16)


def in_rows(array, first, count):
    array = array.reshape(-1, array.shape[-1]).astype(F32)
    rows, lanes = array.shape
    return jnp.pad(array, ((first, count - first - rows), (0, 128 - lanes)))


def split(features, neighbours, face_lists, b1, b2, lev):
    small = [(b1, 0), (b2, 1), (lev, 2), (neighbours, 8), (face_lists, 12)]
    small = sum(in_rows(array, first, 16) for array, first in small)
    piece = jax.ShapeDtypeStruct((PIECE, 32, 128), BF16)
    kept = jax.ShapeDtypeStruct((PIECE + 1, 32, 128), BF16)
    return pl.pallas_call(
        split_kernel,
        out_shape=[kept, piece, piece, piece, jax.ShapeDtypeStruct((8, 128), jnp.int32)],
        in_specs=[VMEM] * 2,
        out_specs=[VMEM] * 5,
        compiler_params=pltpu.CompilerParams(vmem_limit_bytes=8 << 20),
        name="split_features",
    )(features, small)


def faces_kernel(tables, *refs):
    pieces, sides = refs[:4], refs[4:6]
    odd = lax.axis_index("slab") % 2
    for i, out in enumerate(sides):
        tier = (odd + 1 + i) % 2
        for c in range(2):
            b = jnp.maximum(tables[4 + tier, c], 0)
            for m in range(4):
                out[4 * c + m] = pieces[m][12 * tier + b]
        out[8] = pieces[0][17]


def faces(tables, pieces):
    side = jax.ShapeDtypeStruct((9, 32, 128), BF16)
    return pl.pallas_call(
        faces_kernel,
        out_shape=[side] * 2,
        in_specs=[SMEM] + [VMEM] * 4,
        out_specs=[VMEM] * 2,
        compiler_params=pltpu.CompilerParams(vmem_limit_bytes=4 << 20),
        name="pick_faces",
    )(tables, *pieces)


def silu(v):
    return v / (1.0 + jnp.exp(-v))


def gather_padded(slots, pad, lead, slot, planes):
    x = lax.broadcasted_iota(jnp.int32, (1, 8, 128), 1)
    for dz, z_from, z_to in planes:
        for dy in (-1, 0, 1):
            y_from, y_to, n = SPAN[dy]
            parts = ([], [], [])
            for w in range(2):
                mid, left, right = (
                    slots[slot(w, offset(dz, dy, dx)), z_from, y_from : y_from + n] for dx in (0, -1, 1)
                )
                parts[0].append(pltpu.roll(jnp.where(x == 7, left, mid), 1, 1))
                parts[1].append(mid)
                parts[2].append(pltpu.roll(jnp.where(x == 0, right, mid), 7, 1))
            for d in range(3):
                tile = jnp.concatenate(parts[d], axis=1).astype(BF16)
                pad[lead, z_to, y_to : y_to + n, :, 128 * d : 128 * d + 128] = tile


OWN_PLANES = [(-1, 7, 0)] + [(0, z, z + 1) for z in range(8)] + [(1, 0, 9)]


def conv_pair(pad, lead, w):
    zero = jnp.zeros((128, 128), BF16)
    total = None
    blocks = [(zin, dy) for zin in range(4) for dy in range(3)]
    for first in range(0, 12, 2):
        left, right = [], []
        for zin, dy in blocks[first : first + 2]:
            planes = [pad[lead, zin + 2 * j, dy : dy + 8].reshape(128, 384) for j in range(4)]
            left.append(jnp.concatenate(planes, axis=0))
            for dx in range(3):
                even = w[9 * zin + 3 * dy + dx] if zin < 3 else zero
                odd = w[9 * (zin - 1) + 3 * dy + dx] if zin > 0 else zero
                right.append(jnp.concatenate([even, odd], axis=1))
        part = jnp.dot(
            jnp.concatenate(left, axis=1), jnp.concatenate(right, axis=0), preferred_element_type=F32
        )
        total = part if total is None else total + part
    return total


def conv_face(pad, w):
    total = None
    blocks = [(dz, dy) for dz in range(3) for dy in range(3)]
    for group in (blocks[0:2], blocks[2:4], blocks[4:6], blocks[6:9]):
        left, right = [], []
        for dz, dy in group:
            sides = [pad[side, dz, dy : dy + 8].reshape(128, 384) for side in range(2)]
            left.append(jnp.concatenate(sides, axis=0))
            right += [w[9 * dz + 3 * dy + dx] for dx in range(3)]
        part = jnp.dot(
            jnp.concatenate(left, axis=1), jnp.concatenate(right, axis=0), preferred_element_type=F32
        )
        total = part if total is None else total + part
    return total


def load_shards(sources, weights, order, sem):
    return [
        pltpu.make_async_copy(
            source, weights.at[:, pl.ds(pl.multiple_of(32 * order[m], 32), 32), :], sem.at[m]
        )
        for m, source in enumerate(sources)
    ]


def finish(acc, moved, tab, pair, slots):
    for j in range(4):
        for zo in range(2):
            tile = silu(acc[pair, 128 * j : 128 * j + 128, 128 * zo : 128 * zo + 128] + moved)
            tile = tile.reshape(8, 2, 8, 128)
            for w in range(2):
                b = 2 * pair + w
                slots[b, 2 * j + zo] = jnp.where(tab[b, 13] >= 0, tile[:, w], 0.0)


def first_kernel(tab, *refs):
    feat, sides, shards = refs[0:4], refs[4:6], refs[6:10]
    pad_out, shift = refs[10:12]
    hs, w1, sent, sent_int, tables, slots, pad, pad_face, acc, sem = refs[12:]
    me = lax.axis_index("chan")

    f_copies, t_copies = [], []
    for i in range(2):
        side = (lax.axis_index("slab") + 1 + i) % 2
        t_copies.append(pltpu.make_async_copy(sides[i].at[8, pl.ds(0, 16)], sent.at[side], sem.at[i]))
        f_copies.append(pltpu.make_async_copy(sides[i].at[pl.ds(0, 8)], hs.at[side], sem.at[2 + i]))
    w_copies = [
        pltpu.make_async_copy(shards[m], w1.at[:, pl.ds(32 * m, 32), :], sem.at[12 + m]) for m in range(4)
    ]
    for copy in t_copies + f_copies + w_copies:
        copy.start()
    for copy in t_copies:
        copy.wait()
    sent_int[...] = sent[...].astype(F32).astype(jnp.int32).reshape(32, 128)
    to_scalars = pltpu.make_async_copy(sent_int, tables, sem.at[16])
    to_scalars.start()
    for copy in f_copies:
        copy.wait()

    slots[NONE] = jnp.zeros((8, 8, 8, 128), F32)
    for b in range(4):
        for v in range(4):
            brick = jnp.concatenate([feat[m][4 * v + b] for m in range(4)], axis=0)
            slots[b, 2 * v : 2 * v + 2] = brick.T.astype(F32).reshape(2, 8, 8, 128)
    for side in range(2):
        for c in range(2):
            face = jnp.concatenate([hs[side, 4 * c + m] for m in range(4)], axis=0)
            first = 6 if side == 0 else 0
            slots[4 + 2 * side + c, first : first + 2] = face.T.astype(F32).reshape(2, 8, 8, 128)

    to_scalars.wait()

    def own(pair):
        def slot(w, k):
            t = tab[2 * pair + w, k]
            return jnp.where(t < 0, NONE, t)

        return slot

    def below(c, k):
        t = tables[0 + jnp.maximum(tables[5, c], 0), k]
        if k < 18:
            found = jnp.where(t == tables[5, 0], 4, jnp.where(t == tables[5, 1], 5, NONE))
            return jnp.where(t < 0, NONE, found)
        u = tab[4, jnp.clip(t - 6, 0, 1)]
        return jnp.where((t < 6) | (u < 0), NONE, u)

    def above(c, k):
        t = tables[16 + jnp.maximum(tables[20, c], 0), k]
        if k >= 9:
            found = jnp.where(t == tables[20, 0], 6, jnp.where(t == tables[20, 1], 7, NONE))
            return jnp.where(t < 0, NONE, found)
        u = tab[5, jnp.clip(t - 4, 0, 1)]
        return jnp.where((t < 4) | (t > 5) | (u < 0), NONE, u)

    gather_padded(slots, pad_face, 0, below, [(0, 6, 0), (0, 7, 1), (1, 0, 2)])
    gather_padded(slots, pad_face, 1, above, [(-1, 7, 0), (0, 0, 1), (0, 1, 2)])
    for pair in range(2):
        gather_padded(slots, pad, pair, own(pair), OWN_PLANES)

    values = sum(feat[m][16, pl.ds(0, 16), :].astype(F32) for m in range(4))
    shift[...] = values[0:8] + values[8:16]
    moved = shift[0:1, :] + shift[pl.ds(2 + me, 1), :]
    for copy in w_copies:
        copy.wait()

    for pair in range(2):
        acc[pair] = conv_pair(pad, pair, w1)
        finish(acc, moved, tab, pair, slots)
    sides_out = silu(conv_face(pad_face, w1) + moved).reshape(2, 8, 2, 8, 128)
    for c in range(2):
        slots[4 + c, 7] = sides_out[0, :, c]
        slots[6 + c, 0] = sides_out[1, :, c]
    for pair in range(2):
        gather_padded(slots, pad_out, pair, own(pair), OWN_PLANES)


def convolve_first(tables, feat, sides, shards):
    return pl.pallas_call(
        first_kernel,
        out_shape=[jax.ShapeDtypeStruct((2, 10, 10, 16, 384), BF16), jax.ShapeDtypeStruct((8, 128), F32)],
        in_specs=[SMEM] + [VMEM] * 4 + [HBM] * 6,
        out_specs=[VMEM] * 2,
        scratch_shapes=[
            pltpu.VMEM((2, 8, 32, 128), BF16),
            pltpu.VMEM((27, 128, 128), BF16),
            pltpu.VMEM((2, 16, 128), BF16),
            pltpu.VMEM((32, 128), jnp.int32),
            pltpu.SMEM((32, 128), jnp.int32),
            pltpu.VMEM((9, 8, 8, 8, 128), F32),
            pltpu.VMEM((2, 10, 10, 16, 384), BF16),
            pltpu.VMEM((2, 3, 10, 16, 384), BF16),
            pltpu.VMEM((2, 512, 256), F32),
            pltpu.SemaphoreType.DMA((17,)),
        ],
        compiler_params=pltpu.CompilerParams(vmem_limit_bytes=24 << 20),
        cost_estimate=pl.CostEstimate(flops=5 * 10**9, bytes_accessed=4 * 10**6, transcendentals=10**6),
        name="convolve_first",
    )(tables, *feat, *sides, *shards)


def second_kernel(tab, pad, shift, *refs):
    shards, outs = refs[0:4], refs[4:8]
    w2, slots, acc, turned, sem = refs[8:]
    me = lax.axis_index("chan")
    w_copies = load_shards(shards, w2, [me ^ m for m in range(4)], sem)
    for copy in w_copies:
        copy.start()
    for copy in w_copies:
        copy.wait()
    for pair in range(2):
        acc[pair] = conv_pair(pad, pair, w2)
        finish(acc, shift[1:2, :], tab, pair, slots)
    for b in range(4):
        brick = slots[b].reshape(512, 128).astype(BF16).T
        for g in range(4):
            turned[g, b] = brick[32 * g : 32 * g + 32]
    for m in range(4):
        outs[m][...] = turned[me ^ m]


def convolve_second(tables, pad, shift, shards):
    piece = jax.ShapeDtypeStruct((4, 32, 512), BF16)
    return pl.pallas_call(
        second_kernel,
        out_shape=[piece] * 4,
        in_specs=[SMEM, VMEM, VMEM] + [HBM] * 4,
        out_specs=[VMEM] * 4,
        scratch_shapes=[
            pltpu.VMEM((27, 128, 128), BF16),
            pltpu.VMEM((4, 8, 8, 8, 128), F32),
            pltpu.VMEM((2, 512, 256), F32),
            pltpu.VMEM((4, 4, 32, 512), BF16),
            pltpu.SemaphoreType.DMA((4,)),
        ],
        compiler_params=pltpu.CompilerParams(vmem_limit_bytes=24 << 20),
        cost_estimate=pl.CostEstimate(flops=4 * 10**9, bytes_accessed=4 * 10**6, transcendentals=10**6),
        name="convolve_second",
    )(tables, pad, shift, *shards)


def join_kernel(*refs):
    pieces, out, sem = refs[:4], refs[4], refs[5]
    me = lax.axis_index("chan")
    copies = [pltpu.make_async_copy(pieces[m], out.at[me ^ m], sem.at[m]) for m in range(4)]
    for copy in copies:
        copy.start()
    for copy in copies:
        copy.wait()


def join(pieces):
    return pl.pallas_call(
        join_kernel,
        out_shape=jax.ShapeDtypeStruct((4, 4, 32, 512), BF16),
        in_specs=[HBM] * 4,
        out_specs=HBM,
        scratch_shapes=[pltpu.SemaphoreType.DMA((4,))],
        compiler_params=pltpu.CompilerParams(vmem_limit_bytes=8 << 20),
        name="join_levels",
    )(*pieces)


def swap(value, m):
    return lax.ppermute(value, "chan", [(i, i ^ m) for i in range(4)])


def swap_faces(value, first):
    count = lax.axis_size("slab")
    partner = [((s + first) ^ 1) - first for s in range(count)]
    return lax.ppermute(value, "slab", [(s, p if 0 <= p < count else s) for s, p in enumerate(partner)])


def shards(features, neighbours, face_lists, w_first, b_first, w_second, b_second, level_embed):
    w1, w2 = w_first.transpose(0, 2, 1), w_second.transpose(0, 2, 1)
    far = swap(w1, 2)
    own, one, two, three, tables = split(
        features, neighbours, face_lists, b_first, b_second, level_embed
    )
    far, one, two, three, later = lax.optimization_barrier(
        (far, swap(one, 1), swap(two, 2), swap(three, 3), w2)
    )
    pieces = [own, one, two, three]
    first = [w1, swap(w1, 1), far, swap(far, 1)]
    sides = faces(tables, pieces)
    sides = [swap_faces(sides[i], i) for i in range(2)]
    second = [w2, swap(later, 1), swap(later, 2)]
    pad, shift = convolve_first(tables, pieces, sides, first)
    passed, shift = lax.optimization_barrier((second[2], shift))
    second = [w2, second[1], passed, swap(passed, 1)]
    outs = convolve_second(tables, pad, shift, second)
    return join([outs[0]] + [swap(outs[m], m) for m in (1, 2, 3)])


def solution(mesh):
    placed = (
        P(None, "slab", "chan", None),
        P("slab", None),
        P("slab", None, None),
        P(None, None, "chan"),
        P("chan"),
        P(None, None, "chan"),
        P("chan"),
        P(None, "chan"),
    )
    return jax.shard_map(
        shards, mesh=mesh, in_specs=placed, out_specs=P(None, "slab", "chan", None), check_vma=False
    )
```
